32 devices in a mesh: seq: 8 (over y, x, core), dp: 4 (over z).
Axes of the slice: x: 2, y: 2, z: 4, core: 2. Of those that a mesh axis runs over, the one named last changes fastest.
Arguments:
- layer_input: bfloat16 [4, 1536, 2048], P('dp', 'seq'), may hold values from -6 to 6
- doc_lengths: int32 [4, 4], P('dp'), may hold values from 1 to 1440, 1536 in all within a row
- attention_gain: bfloat16 [2048], P(('seq', 'dp')), may hold values from 0.5 to 1.5
- query_down: bfloat16 [2048, 1024], P(('seq', 'dp')), may hold values from -0.125 to 0.125
- query_gain: bfloat16 [1024], P(('seq', 'dp')), may hold values from 0.5 to 1.5
- query_up: bfloat16 [1024, 4096], P(('seq', 'dp')), may hold values from -0.1875 to 0.1875
- keyvalue_weight: bfloat16 [2048, 512], P(('seq', 'dp')), may hold values from -0.125 to 0.125
- output_weight: bfloat16 [4096, 2048], P(('seq', 'dp')), may hold values from -0.75 to 0.75
- feedforward_gain: bfloat16 [2048], P(('seq', 'dp')), may hold values from 0.5 to 1.5
- gate_weight: bfloat16 [2048, 5632], P(('seq', 'dp')), may hold values from -0.125 to 0.125
- up_weight: bfloat16 [2048, 5632], P(('seq', 'dp')), may hold values from -0.125 to 0.125
- down_weight: bfloat16 [5632, 2048], P(('seq', 'dp')), may hold values from -0.078125 to 0.078125
- cotangent: bfloat16 [4, 1536, 2048], P('dp', 'seq'), may hold values from -6 to 6
Outputs:
- layer_output: bfloat16 [4, 1536, 2048], P('dp', 'seq')
- input_grad: float32 [4, 1536, 2048], P('dp', 'seq')
- grad_attention_gain: float32 [2048], P(('seq', 'dp'))
- grad_query_down: float32 [2048, 1024], P(('seq', 'dp'))
- grad_query_gain: float32 [1024], P(('seq', 'dp'))
- grad_query_up: float32 [1024, 4096], P(('seq', 'dp'))
- grad_keyvalue: float32 [2048, 512], P(('seq', 'dp'))
- grad_output_weight: float32 [4096, 2048], P(('seq', 'dp'))
- grad_feedforward_gain: float32 [2048], P(('seq', 'dp'))
- grad_gate: float32 [2048, 5632], P(('seq', 'dp'))
- grad_up: float32 [2048, 5632], P(('seq', 'dp'))
- grad_down: float32 [5632, 2048], P(('seq', 'dp'))
The draws below stay inside these ranges and needn't reach their ends.
Inputs may be any that keep to these rules, and one draw needn't show every extreme that they name: `doc_lengths`: each row's 4 lengths sum to 1536; one of them, at a place drawn from the seed, is exactly 1440.
All inputs are finite; a program needn't handle non-finite values.
Results may differ from the reference program's by a relative error of at most 0.029.
Values may be sent and summed in bfloat16 or wider, within the bound.
No kernel may reach another device: no remote copies, remote signals or barrier semaphores. Data moves between devices by JAX's collectives and lax.ppermute only.
A program may use at most 384 MiB of HBM per device.

```python
import math
import jax
import jax.numpy as jnp
import numpy as np
from jax import lax

D = 2048
QL = 1024
HEADS = 16
HEAD_DIM = 256
FF = 5632
TOK_DEV = 192
DOCS = 4
GROUP = 1536
N_DP = 4


def shard_levels(stream_key, extent, split, low, high):
    gain = 1.0
    for axis_at, blocks in split:
        steps = jax.random.uniform(jax.random.fold_in(jax.random.fold_in(stream_key, 6), axis_at), (blocks,), jnp.float32, low / len(split), high / len(split))
        gain = gain * jnp.repeat(jnp.exp(steps), extent[axis_at] // blocks).reshape((-1,) + (1,) * (len(extent) - 1 - axis_at))
    return gain


def profile(amount, total, bound, lean):
    loads = [(1 << 20) // math.isqrt(rank ** lean) + 1 for rank in range(2, amount + 1)]
    spare, counts = total - bound - (amount - 1), [1] * (amount - 1)
    while spare > 0:
        free = [i for i in range(amount - 1) if counts[i] < bound]
        whole, remaining = sum([loads[i] for i in free]), spare
        for i in free:
            addition = min(bound - counts[i], max(1, remaining * loads[i] // whole), spare)
            counts[i] = counts[i] + addition
            spare = spare - addition
    return np.array([bound] + counts)


def uneven(own_key, count, total, reach, skew):
    if count == 2:
        one = jax.random.randint(own_key, (), max(1, total - reach), min(reach, total - 1) + 1)
        return jnp.stack([one, total - one])
    tallies = jnp.asarray(profile(count, total, reach, skew), jnp.int32)
    pairs = (count - 1) // 2
    giver, taker = tallies[1:1 + 2 * pairs:2], tallies[2:2 + 2 * pairs:2]
    margin = jnp.minimum(giver - 1, reach - taker)
    shifted = jax.random.randint(jax.random.fold_in(own_key, 1), (pairs,), 0, 1 << 20) % (margin + 1)
    tallies = tallies.at[1:1 + 2 * pairs:2].set(giver - shifted).at[2:2 + 2 * pairs:2].set(taker + shifted)
    return tallies[jax.random.permutation(jax.random.fold_in(own_key, 2), count)]


def scatter_about(own_key, dims, scale, limit, pieces=(), kind=jnp.bfloat16):
    values = jax.random.normal(own_key, dims, jnp.float32) * scale
    if len(pieces) > 0:
        values = shard_levels(own_key, dims, pieces, -0.22, 0.18) * values
    return jnp.clip(values, min=-limit, max=limit).astype(kind)


def setup_inputs(seed: int = 0) -> dict:
    splits = jax.random.split(jax.random.key(seed), 14)
    layer_input = scatter_about(splits[0], (N_DP, GROUP, D), 1.0, 6.0, ((0, 4), (1, 8)))
    doc_lengths = jax.vmap(lambda own: uneven(own, DOCS, GROUP, GROUP - TOK_DEV // 2, 0))(jax.random.split(splits[1], N_DP)).reshape((N_DP, DOCS)).astype(jnp.int32)
    attention_gain = jnp.clip(1.0 + 0.1 * jax.random.normal(splits[2], (D,), jnp.float32), 0.5, 1.5).astype(jnp.bfloat16)
    query_down = scatter_about(splits[3], (D, QL), D ** -0.5, 0.125, ((0, 32),))
    query_gain = jnp.clip(1.0 + 0.1 * jax.random.normal(splits[4], (QL,), jnp.float32), 0.5, 1.5).astype(jnp.bfloat16)
    query_up = scatter_about(splits[5], (QL, HEADS * HEAD_DIM), QL ** -0.5, 0.1875, ((0, 32),))
    keyvalue_weight = scatter_about(splits[6], (D, 2 * HEAD_DIM), D ** -0.5, 0.125, ((0, 32),))
    output_weight = scatter_about(splits[7], (HEADS * HEAD_DIM, D), (HEADS * HEAD_DIM // 64) ** -0.5, 0.75, ((0, 32),))
    feedforward_gain = jnp.clip(1.0 + 0.1 * jax.random.normal(splits[8], (D,), jnp.float32), 0.5, 1.5).astype(jnp.bfloat16)
    gate_weight = scatter_about(splits[9], (D, FF), D ** -0.5, 0.125, ((0, 32),))
    up_weight = scatter_about(splits[10], (D, FF), D ** -0.5, 0.125, ((0, 32),))
    down_weight = scatter_about(splits[11], (FF, D), FF ** -0.5, 0.078125, ((0, 32),))
    cotangent = scatter_about(splits[12], (N_DP, GROUP, D), 1.0, 6.0, ((0, 4), (1, 8)))
    return {"layer_input": layer_input, "doc_lengths": doc_lengths, "attention_gain": attention_gain, "query_down": query_down, "query_gain": query_gain, "query_up": query_up, "keyvalue_weight": keyvalue_weight, "output_weight": output_weight, "feedforward_gain": feedforward_gain, "gate_weight": gate_weight, "up_weight": up_weight, "down_weight": down_weight, "cotangent": cotangent}


EPS = 1e-05
ROPE_BASE = 10000.0
NEGATIVE = -1e+30
HIGHEST = lax.Precision.HIGHEST

@jax.custom_vjp
def low(v):
    return lax.optimization_barrier(v.astype(jnp.bfloat16)).astype(jnp.float32)

@jax.custom_vjp
def low_back(v):
    return v

def low_keep(v):
    return (low(v), None)

def low_pass(kept, grad):
    return (grad,)

def back_keep(v):
    return (v, None)

def back_low(kept, grad):
    return (low(grad),)
low.defvjp(low_keep, low_pass)
low_back.defvjp(back_keep, back_low)

def matmul(left_side, right_side):
    return jnp.dot(left_side, right_side, precision=HIGHEST, preferred_element_type=jnp.float32)

def rms_norm(values, norm_gain):
    return values * lax.rsqrt(lax.optimization_barrier(jnp.mean(values * values, axis=-1, keepdims=True)) + EPS) * norm_gain

def rope_tables(position, feature_width):
    half_width = feature_width // 2
    freqs = ROPE_BASE ** (-jnp.arange(half_width, dtype=jnp.float32) * 2.0 / feature_width)
    angles = position.astype(jnp.float32)[:, None] * freqs[None, :]
    return (jnp.cos(angles), jnp.sin(angles))

def rotate(values, cosine, sine_part):
    half_width = values.shape[-1] // 2
    first_half = values[..., :half_width]
    second_half = values[..., half_width:]
    return jnp.concatenate([first_half * cosine - second_half * sine_part, second_half * cosine + first_half * sine_part], axis=-1)

def document_info(lengths_row, group_len):
    doc_ends = jnp.cumsum(lengths_row).astype(jnp.int32)
    places = jnp.arange(group_len, dtype=jnp.int32)
    past_ends = (places[:, None] >= doc_ends[None, :]).astype(jnp.int32)
    segment = lax.optimization_barrier(jnp.sum(past_ends, axis=1)).astype(jnp.int32)
    starts = lax.optimization_barrier(jnp.sum(past_ends * lengths_row[None, :], axis=1)).astype(jnp.int32)
    return (segment, places - starts)

def group_layer(tokens, segment, position, weights):
    attention_gain, query_down, query_gain, query_up, keyvalue_weight, output_weight, feedforward_gain, gate_weight, up_weight, down_weight = weights
    group_len = tokens.shape[0]
    normed = low(rms_norm(tokens, attention_gain))
    latent = low_back(matmul(normed, query_down))
    latent_low = low(rms_norm(latent, query_gain))
    query_raw = low_back(matmul(latent_low, query_up)).reshape(group_len, HEADS, HEAD_DIM)
    keyvalue = low_back(matmul(normed, keyvalue_weight))
    cosine, sine_part = rope_tables(position, HEAD_DIM)
    queries = low(rotate(query_raw, cosine[:, None, :], sine_part[:, None, :]) * HEAD_DIM ** (-0.5))
    keys = low(rotate(keyvalue[:, :HEAD_DIM], cosine, sine_part))
    values = low(keyvalue[:, HEAD_DIM:])
    span = min(256, group_len)
    places = jnp.arange(group_len, dtype=jnp.int32)

    def attend(start):
        query_block = lax.dynamic_slice_in_dim(queries, start, span, 0).reshape(span * HEADS, HEAD_DIM)
        row_index = start + jnp.arange(span * HEADS, dtype=jnp.int32) // HEADS
        row_segment = jnp.repeat(lax.dynamic_slice_in_dim(segment, start, span, 0), HEADS)
        visible = (places[None, :] <= row_index[:, None]) & (segment[None, :] == row_segment[:, None])
        scores = low_back(matmul(query_block, keys.T))
        scores = jnp.where(visible, scores, NEGATIVE)
        row_max = lax.optimization_barrier(jnp.max(scores, axis=1, keepdims=True))
        exp_terms = jnp.where(visible, jnp.exp(scores - row_max), 0.0)
        prob_rows = low(exp_terms / lax.optimization_barrier(jnp.sum(exp_terms, axis=1, keepdims=True)))
        return matmul(prob_rows, values).reshape(span, HEADS * HEAD_DIM)
    starts = jnp.arange(group_len // span, dtype=jnp.int32) * span
    mixed = lax.map(jax.checkpoint(attend), starts).reshape(group_len, HEADS * HEAD_DIM)
    mixed = low_back(low(mixed))
    hidden = tokens + low_back(matmul(mixed, output_weight))
    feed_low = low(rms_norm(hidden, feedforward_gain))
    gate_proj = low_back(matmul(feed_low, gate_weight))
    upward = low_back(matmul(feed_low, up_weight))
    active = low(jax.nn.silu(gate_proj) * upward)
    return hidden + low_back(matmul(active, down_weight))

def reference(layer_input, doc_lengths, attention_gain, query_down, query_gain, query_up, keyvalue_weight, output_weight, feedforward_gain, gate_weight, up_weight, down_weight, cotangent):
    group_len = layer_input.shape[1]
    segment, position = jax.vmap(lambda lengths_row: document_info(lengths_row, group_len))(doc_lengths)
    weights = tuple((weight.astype(jnp.float32) for weight in (attention_gain, query_down, query_gain, query_up, keyvalue_weight, output_weight, feedforward_gain, gate_weight, up_weight, down_weight)))
    tokens = layer_input.astype(jnp.float32)

    def forward(all_tokens, all_weights):

        def one_group(packed):
            return group_layer(packed[0], packed[1], packed[2], all_weights)
        return lax.map(one_group, (all_tokens, segment, position))
    result, pullback = jax.vjp(forward, tokens, weights)
    input_grad, weight_grads = pullback(cotangent.astype(jnp.float32))
    grad_attention_gain, grad_query_down, grad_query_gain, grad_query_up, grad_keyvalue, grad_output_weight, grad_feedforward_gain, grad_gate, grad_up, grad_down = weight_grads
    return (result.astype(jnp.bfloat16), input_grad, grad_attention_gain, grad_query_down, grad_query_gain, grad_query_up, grad_keyvalue, grad_output_weight, grad_feedforward_gain, grad_gate, grad_up, grad_down)
```

```python
import functools

import jax
import jax.numpy as jnp
from jax import lax
from jax.experimental import pallas as pl
from jax.experimental.pallas import tpu as pltpu
from jax.sharding import PartitionSpec as P

HEADS = 16
HEAD_DIM = 256


EPS = 1e-05
ROPE_BASE = 10000.0
NEGATIVE = -1e30
BF = jnp.bfloat16
F32 = jnp.float32


def rms_norm(values, norm_gain):
    return values * lax.rsqrt(jnp.mean(values * values, axis=-1, keepdims=True) + EPS) * norm_gain


def rope_tables(position, feature_width):
    half_width = feature_width // 2
    freqs = ROPE_BASE ** (-jnp.arange(half_width, dtype=F32) * 2.0 / feature_width)
    angles = position.astype(F32)[:, None] * freqs[None, :]
    return (jnp.cos(angles), jnp.sin(angles))


def rotate(values, cosine, sine_part):
    half_width = values.shape[-1] // 2
    first_half = values[..., :half_width]
    second_half = values[..., half_width:]
    return jnp.concatenate(
        [
            first_half * cosine - second_half * sine_part,
            second_half * cosine + first_half * sine_part,
        ],
        axis=-1,
    )


def document_starts(lengths_row, group_len):
    doc_ends = jnp.cumsum(lengths_row)
    places = jnp.arange(group_len, dtype=jnp.int32)
    past_ends = (places[:, None] >= doc_ends[None, :]).astype(jnp.int32)
    starts = jnp.sum(past_ends * lengths_row[None, :], axis=1)
    return (starts, places - starts)


def gated(gate_proj, upward):
    return jax.nn.silu(gate_proj) * upward


def matmul(left_side, right_side):
    return jnp.dot(left_side, right_side, preferred_element_type=F32)


def dot_rows(left_side, right_side):
    return lax.dot_general(
        left_side, right_side, (((1,), (1,)), ((), ())), preferred_element_type=F32
    )


def dot_cols(left_side, right_side):
    return lax.dot_general(
        left_side, right_side, (((0,), (0,)), ((), ())), preferred_element_type=F32
    )


def visible_block(key_at, query_at, starts_row, shape):
    keys = key_at + lax.broadcasted_iota(jnp.int32, shape, 0)
    queries = query_at + lax.broadcasted_iota(jnp.int32, shape, 1)
    return (keys <= queries) & (keys >= starts_row)


def attend_kernel(heads, block, starts_ref, q_ref, k_ref, vt_ref, out_ref, lse_ref):
    at = pl.program_id(0)
    starts_row = starts_ref[...]
    query_at = at * block
    for head in range(heads):
        q = q_ref[:, head * HEAD_DIM : (head + 1) * HEAD_DIM]

        def step(b, running, q=q):
            running_max, running_sum, total = running
            here = pl.ds(pl.multiple_of(b * block, block), block)
            scores = dot_rows(k_ref[here, :], q)
            visible = visible_block(b * block, query_at, starts_row, scores.shape)
            scores = jnp.where(visible, scores, NEGATIVE)
            new_max = jnp.maximum(running_max, jnp.max(scores, axis=0, keepdims=True))
            factor = jnp.exp(running_max - new_max)
            terms = jnp.where(visible, jnp.exp(scores - new_max), 0.0)
            running_sum = running_sum * factor + jnp.sum(terms, axis=0, keepdims=True)
            total = total * factor + matmul(vt_ref[:, here], terms.astype(BF))
            return (new_max, running_sum, total)

        start = (
            jnp.full((1, block), NEGATIVE, F32),
            jnp.zeros((1, block), F32),
            jnp.zeros((HEAD_DIM, block), F32),
        )
        running_max, running_sum, total = lax.fori_loop(0, at + 1, step, start)
        out_ref[:, head * HEAD_DIM : (head + 1) * HEAD_DIM] = (total / running_sum).T
        lse_ref[head : head + 1, :] = running_max + jnp.log(running_sum)


def attend(starts, queries, keys, values):
    group_len, width = queries.shape
    heads = width // HEAD_DIM
    block = 256
    return pl.pallas_call(
        functools.partial(attend_kernel, heads, block),
        grid=(group_len // block,),
        in_specs=[
            pl.BlockSpec((1, block), lambda i: (0, i)),
            pl.BlockSpec((block, width), lambda i: (i, 0)),
            pl.BlockSpec((group_len, HEAD_DIM), lambda i: (0, 0)),
            pl.BlockSpec((HEAD_DIM, group_len), lambda i: (0, 0)),
        ],
        out_specs=[
            pl.BlockSpec((block, width), lambda i: (i, 0)),
            pl.BlockSpec((heads, block), lambda i: (0, i)),
        ],
        out_shape=[
            jax.ShapeDtypeStruct((group_len, width), F32),
            jax.ShapeDtypeStruct((heads, group_len), F32),
        ],
        compiler_params=pltpu.CompilerParams(vmem_limit_bytes=32 * 2**20),
        cost_estimate=pl.CostEstimate(
            flops=2 * group_len * group_len * width,
            bytes_accessed=group_len * width * 8,
            transcendentals=heads * group_len * group_len // 2,
        ),
        name="attend",
    )(starts.reshape(1, group_len), queries, keys, values.T)


def attend_back_kernel(
    heads, block, starts_ref, q_ref, dm_ref, lse_ref, off_ref, k_ref, v_ref, dq_ref, dk_ref, dv_ref
):
    at = pl.program_id(0)

    @pl.when(at == 0)
    def _():
        dk_ref[...] = jnp.zeros_like(dk_ref)
        dv_ref[...] = jnp.zeros_like(dv_ref)

    starts_row = starts_ref[...]
    query_at = at * block
    for head in range(heads):
        columns = slice(head * HEAD_DIM, (head + 1) * HEAD_DIM)
        q = q_ref[:, columns]
        dm = dm_ref[:, columns]
        lse = lse_ref[head : head + 1, :]
        off = off_ref[head : head + 1, :]

        def step(b, dq, q=q, dm=dm, lse=lse, off=off):
            here = pl.ds(pl.multiple_of(b * block, block), block)
            keys = k_ref[here, :]
            scores = dot_rows(keys, q)
            visible = visible_block(b * block, query_at, starts_row, scores.shape)
            probs = jnp.where(visible, jnp.exp(jnp.where(visible, scores, NEGATIVE) - lse), 0.0)
            d_probs = dot_rows(v_ref[here, :], dm)
            d_scores = (probs * (d_probs - off)).astype(BF)
            dv_ref[here, :] += matmul(probs.astype(BF), dm)
            dk_ref[here, :] += matmul(d_scores, q)
            return dq + dot_cols(d_scores, keys)

        dq_ref[:, columns] = lax.fori_loop(0, at + 1, step, jnp.zeros((block, HEAD_DIM), F32))


def attend_back(starts, queries, d_mixed, lse, offset, keys, values):
    group_len, width = queries.shape
    heads = width // HEAD_DIM
    block = 256
    whole = pl.BlockSpec((group_len, HEAD_DIM), lambda i: (0, 0))
    rows = pl.BlockSpec((block, width), lambda i: (i, 0))
    lanes = pl.BlockSpec((heads, block), lambda i: (0, i))
    return pl.pallas_call(
        functools.partial(attend_back_kernel, heads, block),
        grid=(group_len // block,),
        in_specs=[pl.BlockSpec((1, block), lambda i: (0, i)), rows, rows, lanes, lanes, whole, whole],
        out_specs=[rows, whole, whole],
        out_shape=[
            jax.ShapeDtypeStruct((group_len, width), F32),
            jax.ShapeDtypeStruct((group_len, HEAD_DIM), F32),
            jax.ShapeDtypeStruct((group_len, HEAD_DIM), F32),
        ],
        compiler_params=pltpu.CompilerParams(vmem_limit_bytes=32 * 2**20),
        cost_estimate=pl.CostEstimate(
            flops=5 * group_len * group_len * width,
            bytes_accessed=group_len * width * 12,
            transcendentals=heads * group_len * group_len // 2,
        ),
        name="attend_back",
    )(starts.reshape(1, group_len), queries, d_mixed, lse, offset, keys, values)


def gather_seq(rows):
    return lax.all_gather(rows, "seq", axis=0, tiled=True)


def scatter_seq(terms):
    return lax.psum_scatter(terms.astype(BF), "seq", scatter_dimension=0, tiled=True).astype(F32)


def gather_dp(rows):
    return lax.all_gather(rows, "dp", axis=0, tiled=True)


def scatter_dp(terms):
    return lax.psum_scatter(terms.astype(BF), "dp", scatter_dimension=0, tiled=True)


def columns_of(shard):
    n_seq, n_dp = lax.axis_size("seq"), lax.axis_size("dp")
    rows, width = shard.shape
    mine = lax.all_to_all(shard, "seq", split_axis=1, concat_axis=0, tiled=True)
    everyone = gather_dp(mine).reshape(n_dp, n_seq, rows, width // n_seq)
    return everyone.transpose(1, 0, 2, 3).reshape(n_seq * n_dp * rows, width // n_seq)


def columns_grad(terms):
    n_seq, n_dp = lax.axis_size("seq"), lax.axis_size("dp")
    total, width = terms.shape
    rows = total // (n_seq * n_dp)
    ordered = terms.astype(BF).reshape(n_seq, n_dp, rows, width).transpose(1, 0, 2, 3)
    summed = scatter_dp(ordered.reshape(total, width))
    mine = lax.all_to_all(summed, "seq", split_axis=0, concat_axis=1, tiled=True)
    return mine.astype(F32)


def local(
    layer_input,
    doc_lengths,
    attention_gain,
    query_down,
    query_gain,
    query_up,
    keyvalue_weight,
    output_weight,
    feedforward_gain,
    gate_weight,
    up_weight,
    down_weight,
    cotangent,
):
    n_seq, n_dp = lax.axis_size("seq"), lax.axis_size("dp")
    n_all = n_seq * n_dp
    tokens = layer_input[0].astype(F32)
    tok_count, width = tokens.shape
    latent_width = query_down.shape[1]
    group_len = tok_count * n_seq
    heads = HEADS // n_seq
    first_tok = lax.axis_index("seq") * tok_count
    starts_all, position_all = document_starts(doc_lengths[0], group_len)
    local_position = lax.dynamic_slice_in_dim(position_all, first_tok, tok_count, 0)
    cosine_all, sine_all = rope_tables(position_all, HEAD_DIM)
    cosine = lax.dynamic_slice_in_dim(cosine_all, first_tok, tok_count, 0)
    sine_part = lax.dynamic_slice_in_dim(sine_all, first_tok, tok_count, 0)

    own_rows = query_down.shape[0]
    gains = jnp.zeros((own_rows, 128), BF)
    gains = gains.at[:, 0].set(attention_gain).at[:, 1].set(feedforward_gain)
    gains = gains.at[: query_gain.shape[0], 2].set(query_gain)
    first_set = jnp.concatenate([query_down, keyvalue_weight, gains], axis=1)
    first_all = lax.all_gather(first_set, ("seq", "dp"), axis=0, tiled=True)
    first_width = latent_width + 2 * HEAD_DIM
    gain_rows = first_all[:, first_width:].T[:8]
    attention_gain_f = gain_rows[0].astype(F32)
    feed_gain_f = gain_rows[1].astype(F32)
    query_gain_f = gain_rows[2].reshape(n_all, own_rows)[:, : query_gain.shape[0]].reshape(-1).astype(F32)

    full_output = gather_dp(output_weight)
    full_query_up = columns_of(query_up)
    full_gate = columns_of(gate_weight)
    full_upper = columns_of(up_weight)
    full_down = gather_dp(down_weight)

    normed_low = rms_norm(tokens, attention_gain_f).astype(BF)
    first_out = matmul(normed_low, first_all)
    latent = first_out[:, :latent_width]
    keyvalue = first_out[:, latent_width:first_width]
    latent_low = rms_norm(latent, query_gain_f).astype(BF)
    key_local = rotate(keyvalue[:, :HEAD_DIM], cosine, sine_part)
    pack = jnp.concatenate([latent_low, key_local.astype(BF), keyvalue[:, HEAD_DIM:].astype(BF)], axis=1)
    pack_all = gather_seq(pack)
    latent_all = pack_all[:, :latent_width]
    keys = pack_all[:, latent_width : latent_width + HEAD_DIM]
    values = pack_all[:, latent_width + HEAD_DIM :]

    query_raw = matmul(latent_all, full_query_up).reshape(group_len, heads, HEAD_DIM)
    query_scale = HEAD_DIM ** (-0.5)
    queries = (
        (rotate(query_raw, cosine_all[:, None, :], sine_all[:, None, :]) * query_scale)
        .astype(BF)
        .reshape(group_len, heads * HEAD_DIM)
    )
    attended, lse = attend(starts_all, queries, keys, values)
    mixed_low = attended.astype(BF)
    hidden = tokens + scatter_seq(matmul(mixed_low, full_output))

    feed_low = rms_norm(hidden, feed_gain_f).astype(BF)
    feed_all = gather_seq(feed_low)
    gate_proj = matmul(feed_all, full_gate)
    upward = matmul(feed_all, full_upper)
    active_low = gated(gate_proj, upward).astype(BF)
    result = hidden + scatter_seq(matmul(active_low, full_down))
    layer_output = result.astype(BF)[None]

    d_result = cotangent[0].astype(F32)
    d_feed_all = gather_seq(cotangent[0])
    d_active = dot_rows(d_feed_all, full_down)
    d_gate, d_upward = jax.vjp(gated, gate_proj, upward)[1](d_active)
    d_gate_low = d_gate.astype(BF)
    d_up_low = d_upward.astype(BF)
    d_feed_normed = scatter_seq(dot_rows(d_gate_low, full_gate) + dot_rows(d_up_low, full_upper))
    d_hidden_norm, grad_feed_gain_term = jax.vjp(rms_norm, hidden, feed_gain_f)[1](d_feed_normed)
    d_hidden = d_result + d_hidden_norm
    grad_down = scatter_dp(dot_cols(active_low, d_feed_all)).astype(F32)
    grad_gate = columns_grad(dot_cols(feed_all, d_gate_low))
    grad_up = columns_grad(dot_cols(feed_all, d_up_low))

    d_branch_all = gather_seq(d_hidden.astype(BF))
    d_mixed = dot_rows(d_branch_all, full_output)
    d_mixed_low = d_mixed.astype(BF)
    offset = jnp.sum(
        (d_mixed_low.astype(F32) * attended).reshape(group_len, heads, HEAD_DIM), axis=2
    ).T
    grad_output_weight = scatter_dp(dot_cols(mixed_low, d_branch_all)).astype(F32)
    d_queries, d_keys, d_values = attend_back(
        starts_all, queries, d_mixed_low, lse, offset, keys, values
    )
    d_query_raw = rotate(
        d_queries.reshape(group_len, heads, HEAD_DIM) * query_scale,
        cosine_all[:, None, :],
        -sine_all[:, None, :],
    )
    d_query_low = d_query_raw.reshape(group_len, heads * HEAD_DIM).astype(BF)
    back_pack = jnp.concatenate([dot_rows(d_query_low, full_query_up), d_keys, d_values], axis=1)
    back_local = scatter_seq(back_pack)
    grad_query_up = columns_grad(dot_cols(latent_all, d_query_low))
    d_latent_normed = back_local[:, :latent_width]
    d_pairs = back_local[:, latent_width:]
    d_key_raw = rotate(d_pairs[:, :HEAD_DIM], cosine, -sine_part)
    d_keyvalue_low = jnp.concatenate([d_key_raw, d_pairs[:, HEAD_DIM:]], axis=1).astype(BF)
    d_latent, grad_query_gain_term = jax.vjp(rms_norm, latent, query_gain_f)[1](d_latent_normed)
    d_first_low = jnp.concatenate(
        [d_latent.astype(BF), d_keyvalue_low, jnp.zeros((tok_count, 128), BF)], axis=1
    )
    d_normed = dot_rows(d_first_low, first_all)
    d_tokens, grad_attention_gain_term = jax.vjp(rms_norm, tokens, attention_gain_f)[1](d_normed)
    input_grad = (d_hidden + d_tokens)[None]

    grad_first_term = dot_cols(normed_low, d_first_low)
    query_gain_column = jnp.zeros((n_all, own_rows), F32)
    query_gain_column = query_gain_column.at[:, : query_gain.shape[0]].set(
        grad_query_gain_term.reshape(n_all, -1)
    )
    gain_columns = jnp.stack(
        [grad_attention_gain_term, grad_feed_gain_term, query_gain_column.reshape(-1)], axis=1
    )
    grad_first_term = grad_first_term.at[:, first_width : first_width + 3].set(gain_columns)
    grad_first = scatter_dp(scatter_seq(grad_first_term)).astype(F32)
    return (
        layer_output,
        input_grad,
        grad_first[:, first_width],
        grad_first[:, :latent_width],
        grad_first[: query_gain.shape[0], first_width + 2],
        grad_query_up,
        grad_first[:, latent_width:first_width],
        grad_output_weight,
        grad_first[:, first_width + 1],
        grad_gate,
        grad_up,
        grad_down,
    )


def solution(mesh):
    shards = P(("seq", "dp"))
    tokens = P("dp", "seq", None)
    weight = P(("seq", "dp"), None)
    return jax.shard_map(
        local,
        mesh=mesh,
        in_specs=(
            tokens,
            P("dp", None),
            shards,
            weight,
            shards,
            weight,
            weight,
            weight,
            shards,
            weight,
            weight,
            weight,
            tokens,
        ),
        out_specs=(
            tokens,
            tokens,
            shards,
            weight,
            shards,
            weight,
            weight,
            weight,
            shards,
            weight,
            weight,
            weight,
        ),
        check_vma=False,
    )
```

```python
import functools

import jax
import jax.numpy as jnp
from jax import lax
from jax.experimental import pallas as pl
from jax.experimental.pallas import tpu as pltpu
from jax.sharding import PartitionSpec as P

HEADS = 16
HEAD_DIM = 256


EPS = 1e-05
ROPE_BASE = 10000.0
NEGATIVE = -1e30
BF = jnp.bfloat16
F32 = jnp.float32


def rms_norm(values, norm_gain):
    return values * lax.rsqrt(jnp.mean(values * values, axis=-1, keepdims=True) + EPS) * norm_gain


def rope_tables(position, feature_width):
    half_width = feature_width // 2
    freqs = ROPE_BASE ** (-jnp.arange(half_width, dtype=F32) * 2.0 / feature_width)
    angles = position.astype(F32)[:, None] * freqs[None, :]
    return (jnp.cos(angles), jnp.sin(angles))


def rotate(values, cosine, sine_part):
    half_width = values.shape[-1] // 2
    first_half = values[..., :half_width]
    second_half = values[..., half_width:]
    return jnp.concatenate(
        [
            first_half * cosine - second_half * sine_part,
            second_half * cosine + first_half * sine_part,
        ],
        axis=-1,
    )


def document_starts(lengths_row, group_len):
    doc_ends = jnp.cumsum(lengths_row)
    places = jnp.arange(group_len, dtype=jnp.int32)
    past_ends = (places[:, None] >= doc_ends[None, :]).astype(jnp.int32)
    starts = jnp.sum(past_ends * lengths_row[None, :], axis=1)
    return (starts, places - starts)


def gated(gate_proj, upward):
    return jax.nn.silu(gate_proj) * upward


def matmul(left_side, right_side):
    return jnp.dot(left_side, right_side, preferred_element_type=F32)


def dot_rows(left_side, right_side):
    return lax.dot_general(
        left_side, right_side, (((1,), (1,)), ((), ())), preferred_element_type=F32
    )


def dot_cols(left_side, right_side):
    return lax.dot_general(
        left_side, right_side, (((0,), (0,)), ((), ())), preferred_element_type=F32
    )


def flip(block, bits):
    n_seq = lax.axis_size("seq")
    return lax.ppermute(block, "seq", [(i, i ^ bits) for i in range(n_seq)])


def gather_blocks(rows):
    n_seq = lax.axis_size("seq")
    blocks = {0: rows}
    if n_seq == 8:
        half = rows.shape[0] // 2
        blocks[2] = flip(rows, 2)
        blocks[4] = flip(rows, 4)
        blocks[6] = jnp.concatenate([flip(blocks[4][:half], 2), flip(blocks[2][half:], 4)], axis=0)
    else:
        for bits in range(2, n_seq, 2):
            blocks[bits] = flip(rows, bits)
    for bits in range(0, n_seq, 2):
        blocks[bits + 1] = flip(blocks[bits], 1)
    return [blocks[k] for k in range(n_seq)]


def gather_chips(rows):
    blocks = gather_blocks(rows)
    return [
        jnp.concatenate([blocks[k], blocks[k + 1]], axis=0) for k in range(0, len(blocks), 2)
    ]


def plus(first, second):
    return (first.astype(F32) + second.astype(F32)).astype(BF)


def scatter_blocks(terms):
    n_seq = lax.axis_size("seq")
    sums = {}
    for bits in range(n_seq - 2, -1, -2):
        sums[bits] = plus(terms[bits], flip(terms[bits + 1], 1))
    if n_seq == 8:
        half = terms[0].shape[0] // 2
        far_x = flip(sums[6][:half], 2)
        far_y = flip(sums[6][half:], 4)
        from_x = [flip(sums[2][:half], 2), flip(plus(sums[2][half:], far_y), 2)]
        from_y = [flip(plus(sums[4][:half], far_x), 4), flip(sums[4][half:], 4)]
        return sums[0].astype(F32) + jnp.concatenate(
            [x.astype(F32) + y.astype(F32) for x, y in zip(from_x, from_y, strict=True)], axis=0
        )
    total = sums[0].astype(F32)
    for bits in range(2, n_seq, 2):
        total = total + flip(sums[bits], bits).astype(F32)
    return total


def scatter_chips(terms):
    rows = terms[0].shape[0] // 2
    return scatter_blocks([part for term in terms for part in (term[:rows], term[rows:])])


def relative(values, axis):
    n_seq, me = lax.axis_size("seq"), lax.axis_index("seq")
    size = values.shape[axis] // n_seq
    parts = [
        lax.dynamic_slice_in_dim(values, (me ^ k) * size, size, axis) for k in range(n_seq)
    ]
    return jnp.concatenate(parts, axis=axis)


def gather_dp(rows):
    return lax.all_gather(rows, "dp", axis=0, tiled=True)


def scatter_dp(terms):
    return lax.psum_scatter(terms, "dp", scatter_dimension=0, tiled=True)


def split_columns(shard):
    n_seq = lax.axis_size("seq")
    rows, width = shard.shape
    parts = shard.reshape(rows, n_seq, width // n_seq).transpose(1, 0, 2)
    return lax.all_to_all(parts, "seq", 0, 0).reshape(n_seq * rows, width // n_seq)


def join_columns(parts):
    n_seq = lax.axis_size("seq")
    rows, width = parts.shape
    back = lax.all_to_all(parts.reshape(n_seq, rows // n_seq, width), "seq", 0, 0)
    return back.transpose(1, 0, 2)


def rows_in_order(gathered, rows):
    n_seq, n_dp = lax.axis_size("seq"), lax.axis_size("dp")
    width = gathered.shape[1]
    return (
        gathered.reshape(n_dp, n_seq, rows, width).transpose(1, 0, 2, 3).reshape(-1, width)
    )


def rows_by_dp(terms):
    n_seq, n_dp = lax.axis_size("seq"), lax.axis_size("dp")
    total, width = terms.shape
    rows = total // (n_seq * n_dp)
    return terms.reshape(n_seq, n_dp, rows, width).transpose(1, 0, 2, 3).reshape(total, width)


def block_places(shape, axis, core):
    rows = lax.broadcasted_iota(jnp.int32, shape, axis)
    half = shape[axis] // 2
    return rows + core * jnp.where(rows < half, half, -half)


def attend_kernel(heads, block, me_ref, starts_ref, q_ref, k_ref, vt_ref, out_ref, lse_ref):
    me = me_ref[0]
    chip, core = me >> 1, me & 1
    at = pl.program_id(0) ^ chip
    starts_row = starts_ref[...]
    key_place = block_places((block, 1), 0, core)
    query_place = at * block + block_places((1, block), 1, core)
    columns = [slice(h * HEAD_DIM, (h + 1) * HEAD_DIM) for h in range(heads)]

    def step(b, running):
        here = pl.ds(pl.multiple_of((b ^ chip) * block, block), block)
        keys_here = b * block + key_place
        visible = (keys_here <= query_place) & (keys_here >= starts_row)
        result = []
        for head in range(heads):
            running_max, running_sum, total = running[head]
            scores = dot_rows(k_ref[here, :], q_ref[:, columns[head]])
            scores = jnp.where(visible, scores, NEGATIVE)
            new_max = jnp.maximum(running_max, jnp.max(scores, axis=0, keepdims=True))
            factor = jnp.exp(running_max - new_max)
            terms = jnp.where(visible, jnp.exp(scores - new_max), 0.0)
            running_sum = running_sum * factor + jnp.sum(terms, axis=0, keepdims=True)
            total = total * factor + matmul(vt_ref[:, here], terms.astype(BF))
            result.append((new_max, running_sum, total))
        return tuple(result)

    start = (
        jnp.full((1, block), NEGATIVE, F32),
        jnp.zeros((1, block), F32),
        jnp.zeros((HEAD_DIM, block), F32),
    )
    running = lax.fori_loop(0, at + 1, step, (start,) * heads)
    for head in range(heads):
        running_max, running_sum, total = running[head]
        out_ref[:, columns[head]] = (total / running_sum).T
        lse_ref[head : head + 1, :] = running_max + jnp.log(running_sum)


def attend(me, starts, queries, keys, values, block):
    group_len, width = queries.shape
    heads = width // HEAD_DIM
    return pl.pallas_call(
        functools.partial(attend_kernel, heads, block),
        grid_spec=pltpu.PrefetchScalarGridSpec(
            num_scalar_prefetch=1,
            grid=(group_len // block,),
            in_specs=[
                pl.BlockSpec((1, block), lambda i, me: (0, i)),
                pl.BlockSpec((block, width), lambda i, me: (i, 0)),
                pl.BlockSpec((group_len, HEAD_DIM), lambda i, me: (0, 0)),
                pl.BlockSpec((HEAD_DIM, group_len), lambda i, me: (0, 0)),
            ],
            out_specs=[
                pl.BlockSpec((block, width), lambda i, me: (i, 0)),
                pl.BlockSpec((heads, block), lambda i, me: (0, i)),
            ],
        ),
        out_shape=[
            jax.ShapeDtypeStruct((group_len, width), F32),
            jax.ShapeDtypeStruct((heads, group_len), F32),
        ],
        compiler_params=pltpu.CompilerParams(vmem_limit_bytes=32 * 2**20),
        cost_estimate=pl.CostEstimate(
            flops=2 * group_len * group_len * width,
            bytes_accessed=group_len * width * 8,
            transcendentals=heads * group_len * group_len // 2,
        ),
        name="attend",
    )(me, starts.reshape(1, group_len), queries, keys, values.T)


def attend_back_kernel(
    heads,
    block,
    me_ref,
    starts_ref,
    q_ref,
    dm_ref,
    lse_ref,
    off_ref,
    k_ref,
    v_ref,
    dq_ref,
    dk_ref,
    dv_ref,
):
    me = me_ref[0]
    chip, core = me >> 1, me & 1
    at = pl.program_id(0) ^ chip

    @pl.when(pl.program_id(0) == 0)
    def _():
        dk_ref[...] = jnp.zeros_like(dk_ref)
        dv_ref[...] = jnp.zeros_like(dv_ref)

    starts_row = starts_ref[...]
    key_place = block_places((block, 1), 0, core)
    query_place = at * block + block_places((1, block), 1, core)
    columns = [slice(h * HEAD_DIM, (h + 1) * HEAD_DIM) for h in range(heads)]

    def step(b, running):
        here = pl.ds(pl.multiple_of((b ^ chip) * block, block), block)
        keys_here = b * block + key_place
        visible = (keys_here <= query_place) & (keys_here >= starts_row)
        keys, values = k_ref[here, :], v_ref[here, :]
        result = []
        for head in range(heads):
            q, dm = q_ref[:, columns[head]], dm_ref[:, columns[head]]
            scores = dot_rows(keys, q)
            scores = jnp.where(visible, scores, NEGATIVE)
            probs = jnp.where(visible, jnp.exp(scores - lse_ref[head : head + 1, :]), 0.0)
            d_probs = dot_rows(values, dm)
            d_scores = (probs * (d_probs - off_ref[head : head + 1, :])).astype(BF)
            dv_ref[here, :] += matmul(probs.astype(BF), dm)
            dk_ref[here, :] += matmul(d_scores, q)
            result.append(running[head] + dot_cols(d_scores, keys))
        return tuple(result)

    start = (jnp.zeros((block, HEAD_DIM), F32),) * heads
    d_queries = lax.fori_loop(0, at + 1, step, start)
    for head in range(heads):
        dq_ref[:, columns[head]] = d_queries[head]


def attend_back(me, starts, queries, d_mixed, lse, offset, keys, values, block):
    group_len, width = queries.shape
    heads = width // HEAD_DIM
    whole = pl.BlockSpec((group_len, HEAD_DIM), lambda i, me: (0, 0))
    rows = pl.BlockSpec((block, width), lambda i, me: (i, 0))
    lanes = pl.BlockSpec((heads, block), lambda i, me: (0, i))
    first = pl.BlockSpec((1, block), lambda i, me: (0, i))
    return pl.pallas_call(
        functools.partial(attend_back_kernel, heads, block),
        grid_spec=pltpu.PrefetchScalarGridSpec(
            num_scalar_prefetch=1,
            grid=(group_len // block,),
            in_specs=[first, rows, rows, lanes, lanes, whole, whole],
            out_specs=[rows, whole, whole],
        ),
        out_shape=[
            jax.ShapeDtypeStruct((group_len, width), F32),
            jax.ShapeDtypeStruct((group_len, HEAD_DIM), F32),
            jax.ShapeDtypeStruct((group_len, HEAD_DIM), F32),
        ],
        compiler_params=pltpu.CompilerParams(vmem_limit_bytes=32 * 2**20),
        cost_estimate=pl.CostEstimate(
            flops=5 * group_len * group_len * width,
            bytes_accessed=group_len * width * 12,
            transcendentals=heads * group_len * group_len // 2,
        ),
        name="attend_back",
    )(me, starts.reshape(1, group_len), queries, d_mixed, lse, offset, keys, values)


def local(
    layer_input,
    doc_lengths,
    attention_gain,
    query_down,
    query_gain,
    query_up,
    keyvalue_weight,
    output_weight,
    feedforward_gain,
    gate_weight,
    up_weight,
    down_weight,
    cotangent,
):
    n_seq, n_dp = lax.axis_size("seq"), lax.axis_size("dp")
    me = lax.axis_index("seq")
    chips = range(n_seq // 2)
    input_low = layer_input[0]
    tokens = input_low.astype(F32)
    tok_count, width = tokens.shape
    latent_width = query_down.shape[1]
    group_len = tok_count * n_seq
    heads = HEADS // n_seq
    hidden_units = gate_weight.shape[1] // n_seq

    starts_all, position_all = document_starts(doc_lengths[0], group_len)
    starts_all = relative(starts_all, 0)
    position_all = relative(position_all, 0)
    cosine_all, sine_all = rope_tables(position_all, HEAD_DIM)
    cosine, sine_part = cosine_all[:tok_count], sine_all[:tok_count]
    me_array = me.astype(jnp.int32).reshape(1)

    own_rows = query_down.shape[0]
    query_rows = query_gain.shape[0]
    gains = jnp.stack(
        [attention_gain, feedforward_gain, jnp.pad(query_gain, (0, own_rows - query_rows))], axis=1
    )
    first_set = jnp.concatenate(
        [query_down, keyvalue_weight, jnp.pad(gains, ((0, 0), (0, 125)))], axis=1
    )
    first_part = gather_dp(first_set)

    query_part = split_columns(query_up)
    fold = query_part.shape[0] * query_part.shape[1] // width
    attention_part = gather_dp(
        jnp.concatenate([output_weight, query_part.reshape(fold, width)], axis=0)
    ).reshape(n_dp, -1, width)
    out_rows = output_weight.shape[0]
    full_output = attention_part[:, :out_rows].reshape(-1, width)
    full_query_up = rows_in_order(
        attention_part[:, out_rows:].reshape(-1, query_part.shape[1]), query_up.shape[0]
    )
    gate_up = jnp.concatenate(
        [gate_weight.reshape(own_rows, n_seq, -1), up_weight.reshape(own_rows, n_seq, -1)], axis=2
    )
    full_gate_up = rows_in_order(
        gather_dp(split_columns(gate_up.reshape(own_rows, -1))), own_rows
    )
    full_down = gather_dp(down_weight)

    first_all = jnp.concatenate(gather_blocks(first_part), axis=0)
    first_width = latent_width + 2 * HEAD_DIM
    gain_rows = first_all[:, first_width:].T[:8].astype(F32)
    attention_gain_rel = gain_rows[0]
    feed_gain_f = relative(gain_rows[1], 0)
    query_gain_f = relative(gain_rows[2], 0).reshape(-1, own_rows)[:, :query_rows].reshape(-1)

    tokens_rel = relative(input_low, 1).astype(F32)
    normed_rel = rms_norm(tokens_rel, attention_gain_rel).astype(BF)
    first_out = matmul(normed_rel, first_all)
    latent = first_out[:, :latent_width]
    keyvalue = first_out[:, latent_width:first_width]
    latent_low = rms_norm(latent, query_gain_f).astype(BF)
    key_local = rotate(keyvalue[:, :HEAD_DIM], cosine, sine_part)
    pack = jnp.concatenate(
        [latent_low, key_local.astype(BF), keyvalue[:, HEAD_DIM:].astype(BF)], axis=1
    )
    pack_all = jnp.concatenate(gather_blocks(pack), axis=0)
    latent_all = pack_all[:, :latent_width]
    keys = pack_all[:, latent_width : latent_width + HEAD_DIM]
    values = pack_all[:, latent_width + HEAD_DIM :]

    query_raw = matmul(latent_all, full_query_up)
    query_scale = HEAD_DIM ** (-0.5)
    queries = jnp.concatenate(
        [
            rotate(query_raw[:, h * HEAD_DIM : (h + 1) * HEAD_DIM], cosine_all, sine_all)
            * query_scale
            for h in range(heads)
        ],
        axis=1,
    ).astype(BF)
    block = 2 * tok_count
    attended, lse = attend(me_array, starts_all, queries, keys, values, block)
    mixed_low = attended.astype(BF)
    spans = [slice(j * block, (j + 1) * block) for j in chips]
    hidden = tokens + scatter_chips(
        [matmul(mixed_low[span], full_output).astype(BF) for span in spans]
    )

    cotangent_low = lax.optimization_barrier((cotangent[0], pack_all))[0]
    d_feed = gather_chips(cotangent_low)
    d_result = cotangent_low.astype(F32)

    feed_low = rms_norm(hidden, feed_gain_f).astype(BF)
    feed = gather_chips(feed_low)
    gate_proj, upward, active_low = [], [], []
    for j in chips:
        both = matmul(feed[j], full_gate_up)
        gate_proj.append(both[:, :hidden_units])
        upward.append(both[:, hidden_units:])
        active_low.append(gated(gate_proj[j], upward[j]).astype(BF))
    d_gate_up = []
    for j in chips:
        d_active = dot_rows(d_feed[j], full_down)
        pair = jax.vjp(gated, gate_proj[j], upward[j])[1](d_active)
        d_gate_up.append(jnp.concatenate(pair, axis=1).astype(BF))
    d_feed_normed = scatter_chips(
        [dot_rows(d_gate_up[j], full_gate_up).astype(BF) for j in chips]
    )
    feed_all = jnp.concatenate(feed, axis=0)
    d_feed_all = jnp.concatenate(d_feed, axis=0)
    active_all = jnp.concatenate(active_low, axis=0)
    d_gate_up_all = jnp.concatenate(d_gate_up, axis=0)
    grad_down = scatter_dp(dot_cols(active_all, d_feed_all).astype(BF)).astype(F32)
    grad_gate_up = scatter_dp(rows_by_dp(dot_cols(feed_all, d_gate_up_all).astype(BF)))

    d_hidden_norm, grad_feed_gain_term = jax.vjp(rms_norm, hidden, feed_gain_f)[1](d_feed_normed)
    d_hidden = d_result + d_hidden_norm
    d_branch = gather_chips(d_hidden.astype(BF))
    result = hidden + scatter_chips(
        [
            matmul(lax.optimization_barrier((active_low[j], d_branch[j]))[0], full_down).astype(BF)
            for j in chips
        ]
    )
    layer_output = result.astype(BF)[None]

    d_mixed_low = jnp.concatenate(
        [dot_rows(d_branch[j], full_output).astype(BF) for j in chips], axis=0
    )
    offset = jnp.stack(
        [
            jnp.sum(
                d_mixed_low[:, h * HEAD_DIM : (h + 1) * HEAD_DIM].astype(F32)
                * attended[:, h * HEAD_DIM : (h + 1) * HEAD_DIM],
                axis=1,
            )
            for h in range(heads)
        ]
    )
    d_queries, d_keys, d_values = attend_back(
        me_array, starts_all, queries, d_mixed_low, lse, offset, keys, values, block
    )
    d_query_low = jnp.concatenate(
        [
            rotate(d_queries[:, h * HEAD_DIM : (h + 1) * HEAD_DIM], cosine_all, -sine_all)
            * query_scale
            for h in range(heads)
        ],
        axis=1,
    ).astype(BF)
    back_local = scatter_chips(
        [
            jnp.concatenate(
                [
                    dot_rows(d_query_low[span], full_query_up).astype(BF),
                    d_keys[span].astype(BF),
                    d_values[span].astype(BF),
                ],
                axis=1,
            )
            for span in spans
        ]
    )
    d_branch_all = jnp.concatenate(d_branch, axis=0)
    grad_output_term = dot_cols(mixed_low, d_branch_all).astype(BF)
    grad_query_term = rows_by_dp(dot_cols(latent_all, d_query_low).astype(BF))
    grad_attention = scatter_dp(
        jnp.concatenate(
            [
                grad_output_term.reshape(n_dp, out_rows, width),
                grad_query_term.reshape(n_dp, fold, width),
            ],
            axis=1,
        ).reshape(-1, width)
    )
    grad_output_weight = grad_attention[:out_rows].astype(F32)
    grad_query_up = join_columns(grad_attention[out_rows:].reshape(query_part.shape))
    grad_query_up = grad_query_up.astype(F32).reshape(query_rows, -1)

    d_latent_normed = back_local[:, :latent_width]
    d_pairs = back_local[:, latent_width:]
    d_key_raw = rotate(d_pairs[:, :HEAD_DIM], cosine, -sine_part)
    d_keyvalue_low = jnp.concatenate([d_key_raw, d_pairs[:, HEAD_DIM:]], axis=1).astype(BF)
    d_latent, grad_query_gain_term = jax.vjp(rms_norm, latent, query_gain_f)[1](d_latent_normed)
    d_first_low = jnp.concatenate(
        [d_latent.astype(BF), d_keyvalue_low, jnp.zeros((tok_count, 128), BF)], axis=1
    )
    d_normed_rel = dot_rows(d_first_low, first_all)
    d_tokens_rel, attention_gain_term = jax.vjp(rms_norm, tokens_rel, attention_gain_rel)[1](
        d_normed_rel
    )
    input_grad = (d_hidden + relative(d_tokens_rel, 1))[None]

    query_gain_term = jnp.pad(
        grad_query_gain_term.reshape(-1, query_rows), ((0, 0), (0, own_rows - query_rows))
    ).reshape(-1)
    gain_terms = jnp.stack(
        [attention_gain_term, relative(grad_feed_gain_term, 0), relative(query_gain_term, 0)],
        axis=1,
    )
    first_terms = jnp.concatenate(
        [
            dot_cols(normed_rel, d_first_low[:, :first_width]).astype(BF),
            jnp.pad(gain_terms, ((0, 0), (0, 125))).astype(BF),
        ],
        axis=1,
    )
    first_rows = first_terms.shape[0] // n_seq
    grad_first = scatter_dp(
        scatter_blocks(
            [first_terms[k * first_rows : (k + 1) * first_rows] for k in range(n_seq)]
        ).astype(BF)
    ).astype(F32)

    gate_up_rows = join_columns(grad_gate_up).astype(F32)
    return (
        layer_output,
        input_grad,
        grad_first[:, first_width],
        grad_first[:, :latent_width],
        grad_first[:query_rows, first_width + 2],
        grad_query_up,
        grad_first[:, latent_width:first_width],
        grad_output_weight,
        grad_first[:, first_width + 1],
        gate_up_rows[:, :, :hidden_units].reshape(own_rows, -1),
        gate_up_rows[:, :, hidden_units:].reshape(own_rows, -1),
        grad_down,
    )


def solution(mesh):
    shards = P(("seq", "dp"))
    tokens = P("dp", "seq", None)
    weight = P(("seq", "dp"), None)
    return jax.shard_map(
        local,
        mesh=mesh,
        in_specs=(
            tokens,
            P("dp", None),
            shards,
            weight,
            shards,
            weight,
            weight,
            weight,
            shards,
            weight,
            weight,
            weight,
            tokens,
        ),
        out_specs=(
            tokens,
            tokens,
            shards,
            weight,
            shards,
            weight,
            weight,
            weight,
            shards,
            weight,
            weight,
            weight,
        ),
        check_vma=False,
    )
```

```python
import functools

import jax
import jax.numpy as jnp
from jax import lax
from jax.experimental import pallas as pl
from jax.experimental.pallas import tpu as pltpu
from jax.sharding import PartitionSpec as P

HEADS = 16
HEAD_DIM = 256


EPS = 1e-05
ROPE_BASE = 10000.0
NEGATIVE = -1e30
BF = jnp.bfloat16
F32 = jnp.float32
SMALL = pl.CostEstimate(flops=1024, bytes_accessed=1024, transcendentals=0)


def rms_norm(values, norm_gain):
    return values * lax.rsqrt(jnp.mean(values * values, axis=-1, keepdims=True) + EPS) * norm_gain


def rope_tables(position, feature_width):
    half_width = feature_width // 2
    freqs = ROPE_BASE ** (-jnp.arange(half_width, dtype=F32) * 2.0 / feature_width)
    angles = position.astype(F32)[:, None] * freqs[None, :]
    return (jnp.cos(angles), jnp.sin(angles))


def rotate(values, cosine, sine_part):
    half_width = values.shape[-1] // 2
    first_half = values[..., :half_width]
    second_half = values[..., half_width:]
    return jnp.concatenate(
        [
            first_half * cosine - second_half * sine_part,
            second_half * cosine + first_half * sine_part,
        ],
        axis=-1,
    )


def document_starts(lengths_row, group_len):
    doc_ends = jnp.cumsum(lengths_row)
    places = jnp.arange(group_len, dtype=jnp.int32)
    past_ends = (places[:, None] >= doc_ends[None, :]).astype(jnp.int32)
    starts = jnp.sum(past_ends * lengths_row[None, :], axis=1)
    return (starts, places - starts)


def gated(gate_proj, upward):
    return jax.nn.silu(gate_proj) * upward


def matmul(left_side, right_side):
    return jnp.dot(left_side, right_side, preferred_element_type=F32)


def dot_rows(left_side, right_side):
    return lax.dot_general(
        left_side, right_side, (((1,), (1,)), ((), ())), preferred_element_type=F32
    )


def dot_cols(left_side, right_side):
    return lax.dot_general(
        left_side, right_side, (((0,), (0,)), ((), ())), preferred_element_type=F32
    )


def flip(block, bits):
    n_seq = lax.axis_size("seq")
    return lax.ppermute(block, "seq", [(i, i ^ bits) for i in range(n_seq)])


def gather_near(rows):
    n_seq = lax.axis_size("seq")
    hops = (2, 4) if n_seq == 8 else range(2, n_seq, 2)
    return {0: rows} | {bits: flip(rows, bits) for bits in hops}


def gather_far(blocks):
    if lax.axis_size("seq") != 8:
        return blocks
    half = blocks[0].shape[0] // 2
    far = [flip(blocks[4][:half], 2), flip(blocks[2][half:], 4)]
    return blocks | {6: jnp.concatenate(far, axis=0)}


def gather_cores(blocks):
    whole = []
    for bits in range(0, lax.axis_size("seq"), 2):
        whole += [blocks[bits], flip(blocks[bits], 1)]
    return whole


def gather_blocks(rows):
    return gather_cores(gather_far(gather_near(rows)))


def together(*values):
    flat, tree = jax.tree.flatten(values)
    return jax.tree.unflatten(tree, lax.optimization_barrier(flat))


def stack_kernel(count, *refs):
    sources, target, held, arrived, left = refs[:count], *refs[count:]
    rows = sources[0].shape[0]
    moves = []
    for k, source in enumerate(sources):
        here = pl.ds(k * rows, rows)
        moves.append(
            (
                pltpu.make_async_copy(source, held.at[here], arrived.at[k]),
                pltpu.make_async_copy(held.at[here], target.at[here], left.at[k]),
            )
        )
    for come, _ in moves:
        come.start()
    for come, go in moves:
        come.wait()
        go.start()
    for _, go in moves:
        go.wait()


def stack_blocks(blocks):
    rows, width = blocks[0].shape
    shape, dtype = (len(blocks) * rows, width), blocks[0].dtype
    size = shape[0] * width * dtype.itemsize
    return pl.pallas_call(
        functools.partial(stack_kernel, len(blocks)),
        in_specs=[pl.BlockSpec(memory_space=pl.ANY)] * len(blocks),
        out_specs=pl.BlockSpec(memory_space=pl.ANY),
        out_shape=jax.ShapeDtypeStruct(shape, dtype),
        scratch_shapes=[pltpu.VMEM(shape, dtype)]
        + [pltpu.SemaphoreType.DMA((len(blocks),))] * 2,
        compiler_params=pltpu.CompilerParams(vmem_limit_bytes=size + 4 * 2**20),
        cost_estimate=SMALL,
        name="stack_blocks",
    )(*blocks)


def gather_seq(rows):
    return stack_blocks(gather_blocks(rows))


def plus(first, second):
    return (first.astype(F32) + second.astype(F32)).astype(BF)


def chip_sums(even, odd, count):
    total = plus(even, flip(odd, 1))
    rows = total.shape[0] // count
    return [total[k * rows : (k + 1) * rows] for k in range(count)]


def scatter_relay(sums):
    n_seq = lax.axis_size("seq")
    if n_seq != 8:
        return {k: [part] for k, part in enumerate(sums)}
    half = sums[0].shape[0] // 2
    far_x = flip(sums[3][:half], 2)
    far_y = flip(sums[3][half:], 4)
    return {
        0: [sums[0]],
        1: [sums[1][:half], plus(sums[1][half:], far_y)],
        2: [sums[2][half:], plus(sums[2][:half], far_x)],
    }


def scatter_last(left):
    n_seq = lax.axis_size("seq")
    if n_seq != 8:
        return sum(
            (flip(parts[0], 2 * k) if k else parts[0]).astype(F32) for k, parts in left.items()
        )
    x_low, x_high = [flip(part, 2).astype(F32) for part in left[1]]
    y_high, y_low = [flip(part, 4).astype(F32) for part in left[2]]
    return left[0][0].astype(F32) + jnp.concatenate([x_low + y_low, x_high + y_high], axis=0)


def scatter_pairs(even, odd):
    count = lax.axis_size("seq") // 2
    return scatter_last(scatter_relay(chip_sums(even, odd, count)))


def relative(values, axis):
    n_seq, me = lax.axis_size("seq"), lax.axis_index("seq")
    size = values.shape[axis] // n_seq
    parts = [
        lax.dynamic_slice_in_dim(values, (me ^ k) * size, size, axis) for k in range(n_seq)
    ]
    return jnp.concatenate(parts, axis=axis)


def relative_vectors(values):
    n_seq, me = lax.axis_size("seq"), lax.axis_index("seq")
    count, length = values.shape
    values = values.reshape(count, n_seq, length // n_seq)
    bit = 1
    while bit < n_seq:
        pairs = values.reshape(count, n_seq // (2 * bit), 2, bit, length // n_seq)
        swapped = jnp.concatenate([pairs[:, :, 1:], pairs[:, :, :1]], axis=2)
        values = jnp.where((me & bit) != 0, swapped, pairs).reshape(values.shape)
        bit *= 2
    return values.reshape(count, length)


def gather_dp(rows):
    return lax.all_gather(rows, "dp", axis=0, tiled=True)


def gather_dp_steps(rows):
    n_dp, me = lax.axis_size("dp"), lax.axis_index("dp")
    size = rows.shape[0]
    whole = jnp.zeros((n_dp * size, rows.shape[1]), rows.dtype)
    for bits in range(n_dp):
        block = rows
        if bits:
            block = lax.ppermute(rows, "dp", [(i, i ^ bits) for i in range(n_dp)])
        whole = lax.dynamic_update_slice_in_dim(whole, block, (me ^ bits) * size, 0)
    return whole


def scatter_dp(terms):
    return lax.psum_scatter(terms, "dp", scatter_dimension=0, tiled=True)


def split_columns(shard):
    n_seq = lax.axis_size("seq")
    rows, width = shard.shape
    return shard.reshape(rows, n_seq, width // n_seq).transpose(1, 0, 2)


def exchange(parts):
    return lax.all_to_all(parts, "seq", 0, 0)


def rows_in_order(gathered, rows):
    n_seq, n_dp = lax.axis_size("seq"), lax.axis_size("dp")
    width = gathered.shape[-1]
    return gathered.reshape(n_dp, n_seq, rows, width).transpose(1, 0, 2, 3).reshape(-1, width)


def rows_by_dp(terms):
    n_seq, n_dp = lax.axis_size("seq"), lax.axis_size("dp")
    total, width = terms.shape
    rows = total // (n_seq * n_dp)
    return terms.reshape(n_seq, n_dp, rows, width).transpose(1, 0, 2, 3)


def first_kernel(count, low_width, x_ref, *refs):
    blocks, (out_ref, normed_ref, gains_ref) = refs[:count], refs[count:]
    rows = blocks[0].shape[0]
    x = x_ref[...].astype(F32)
    scale = lax.rsqrt(jnp.mean(x * x, axis=1, keepdims=True) + EPS)
    for k in range(count):
        here = slice(k * rows, (k + 1) * rows)
        gains = blocks[k][:, low_width:].astype(F32).T
        gains_ref[:, here] = gains[: gains_ref.shape[0]]
        normed = (x_ref[:, here].astype(F32) * scale * gains[:1]).astype(BF)
        normed_ref[:, here] = normed
        part = matmul(normed, blocks[k][:, :low_width])
        if k == 0:
            out_ref[...] = part
        else:
            out_ref[...] += part


def first_projections(x, blocks, low_width):
    tok_count, width = x.shape
    vmem = pl.BlockSpec(memory_space=pltpu.VMEM)
    return pl.pallas_call(
        functools.partial(first_kernel, len(blocks), low_width),
        in_specs=[vmem] * (1 + len(blocks)),
        out_specs=[vmem] * 3,
        out_shape=[
            jax.ShapeDtypeStruct((tok_count, low_width), F32),
            jax.ShapeDtypeStruct((tok_count, width), BF),
            jax.ShapeDtypeStruct((8, width), F32),
        ],
        compiler_params=pltpu.CompilerParams(vmem_limit_bytes=40 * 2**20),
        cost_estimate=SMALL,
        name="first_projections",
    )(x, *blocks)


def weights_in_order(raw_ref, gate_ref, up_ref):
    n_dp, n_seq, _, rows, _ = raw_ref.shape
    for s in range(n_seq):
        for z in range(n_dp):
            here = pl.ds((s * n_dp + z) * rows, rows)
            gate_ref[here, :] = raw_ref[z, s, 0]
            up_ref[here, :] = raw_ref[z, s, 1]


def feed_kernel(count, block, *refs):
    blocks, raw_ref = refs[:count], refs[count]
    x_ref, act_ref, silu_ref, slope_ref, gate_ref, up_ref = refs[count + 1 :]
    at = pl.program_id(0)

    @pl.when(at == 0)
    def _():
        rows = blocks[0].shape[0]
        for k, source in enumerate(blocks):
            x_ref[k * rows : (k + 1) * rows, :] = source[...]
        weights_in_order(raw_ref, gate_ref, up_ref)

    x = x_ref[pl.ds(pl.multiple_of(at * block, block), block), :]
    gate = matmul(x, gate_ref[...])
    upward = matmul(x, up_ref[...])
    sigmoid = 1.0 / (1.0 + jnp.exp(-gate))
    silu = gate * sigmoid
    act_ref[...] = (silu * upward).astype(BF)
    silu_ref[...] = silu.astype(BF)
    slope_ref[...] = (upward * (sigmoid + silu * (1.0 - sigmoid))).astype(BF)


def whole_spec(shape):
    return pl.BlockSpec(shape, lambda *_: (0,) * len(shape), pipeline_mode=pl.Buffered(1))


def feed_forward(blocks, raw, block):
    rows, width = blocks[0].shape
    group_len = rows * len(blocks)
    hidden = raw.shape[-1]
    units = pl.BlockSpec((block, hidden), lambda i: (i, 0))
    weight = jax.ShapeDtypeStruct((width, hidden), BF)
    return pl.pallas_call(
        functools.partial(feed_kernel, len(blocks), block),
        grid=(group_len // block,),
        in_specs=[whole_spec((rows, width))] * len(blocks) + [whole_spec(raw.shape)],
        out_specs=[whole_spec((group_len, width))]
        + [units] * 3
        + [whole_spec((width, hidden))] * 2,
        out_shape=[jax.ShapeDtypeStruct((group_len, width), BF)]
        + [jax.ShapeDtypeStruct((group_len, hidden), BF)] * 3
        + [weight] * 2,
        compiler_params=pltpu.CompilerParams(vmem_limit_bytes=52 * 2**20),
        cost_estimate=SMALL,
        name="feed_forward",
    )(*blocks, raw)


def feed_back_kernel(
    d_ref, silu_ref, slope_ref, gate_ref, up_ref, down_ref, dg_ref, du_ref, even_ref, odd_ref
):
    d_active = dot_rows(d_ref[...], down_ref[...])
    d_gate = (d_active * slope_ref[...].astype(F32)).astype(BF)
    d_up = (d_active * silu_ref[...].astype(F32)).astype(BF)
    dg_ref[...] = d_gate
    du_ref[...] = d_up
    terms = (dot_rows(d_gate, gate_ref[...]) + dot_rows(d_up, up_ref[...])).astype(BF)
    half = terms.shape[0] // 2
    even_ref[...] = terms[:half]
    odd_ref[...] = terms[half:]


def feed_back(d, silu, slope, gate, up, down, block, first, count):
    width, hidden = gate.shape
    tokens = pl.BlockSpec((block, width), lambda i: (i + first, 0))
    units = pl.BlockSpec((block, hidden), lambda i: (i + first, 0))
    half = pl.BlockSpec((block // 2, width), lambda i: (i, 0))
    return pl.pallas_call(
        feed_back_kernel,
        grid=(count,),
        in_specs=[tokens, units, units]
        + [whole_spec(gate.shape), whole_spec(up.shape), whole_spec(down.shape)],
        out_specs=[pl.BlockSpec((block, hidden), lambda i: (i, 0))] * 2 + [half] * 2,
        out_shape=[jax.ShapeDtypeStruct((count * block, hidden), BF)] * 2
        + [jax.ShapeDtypeStruct((count * block // 2, width), BF)] * 2,
        compiler_params=pltpu.CompilerParams(vmem_limit_bytes=44 * 2**20),
        cost_estimate=SMALL,
        name="feed_back",
    )(d, silu, slope, gate, up, down)


def gate_up_grad_kernel(x_ref, dg_low, du_low, dg_high, du_high, out_ref):
    n_dp, _, _, rows, _ = out_ref.shape
    middle = dg_low.shape[0]
    low, high = x_ref[:middle, :], x_ref[middle:, :]
    for which, (d_low, d_high) in enumerate(((dg_low, dg_high), (du_low, du_high))):
        terms = (dot_cols(low, d_low[...]) + dot_cols(high, d_high[...])).astype(BF)
        for z in range(n_dp):
            out_ref[z, 0, which] = terms[z * rows : (z + 1) * rows]


def gate_up_grad(x, low, high, n_dp, n_seq):
    group_len, width = x.shape
    hidden = low[0].shape[1]
    rows = width // (n_dp * n_seq)
    return pl.pallas_call(
        gate_up_grad_kernel,
        grid=(n_seq,),
        in_specs=[pl.BlockSpec((group_len, n_dp * rows), lambda i: (0, i))]
        + [whole_spec(part.shape) for part in (*low, *high)],
        out_specs=pl.BlockSpec((n_dp, 1, 2, rows, hidden), lambda i: (0, i, 0, 0, 0)),
        out_shape=jax.ShapeDtypeStruct((n_dp, n_seq, 2, rows, hidden), BF),
        compiler_params=pltpu.CompilerParams(vmem_limit_bytes=40 * 2**20),
        cost_estimate=SMALL,
        name="gate_up_grad",
    )(x, *low, *high)


def pair_product_kernel(left_ref, right_ref, even_ref, odd_ref):
    terms = matmul(left_ref[...], right_ref[...]).astype(BF)
    half = terms.shape[0] // 2
    even_ref[...] = terms[:half]
    odd_ref[...] = terms[half:]


def pair_product(left, right, block):
    rows, depth = left.shape
    width = right.shape[1]
    half = pl.BlockSpec((block // 2, width), lambda i: (i, 0))
    return pl.pallas_call(
        pair_product_kernel,
        grid=(rows // block,),
        in_specs=[pl.BlockSpec((block, depth), lambda i: (i, 0)), whole_spec(right.shape)],
        out_specs=[half] * 2,
        out_shape=[jax.ShapeDtypeStruct((rows // 2, width), BF)] * 2,
        compiler_params=pltpu.CompilerParams(vmem_limit_bytes=32 * 2**20),
        cost_estimate=SMALL,
        name="pair_product",
    )(left, right)


def last_kernel(
    count,
    back_ref,
    latent_ref,
    query_gain_ref,
    normed_ref,
    x_ref,
    gain_ref,
    cos_ref,
    sin_ref,
    *refs,
):
    blocks, (even_ref, odd_ref, dx_ref, query_term_ref, gain_term_ref) = refs[:count], refs[count:]
    latent_width = latent_ref.shape[1]
    first_width = back_ref.shape[1]
    rows = blocks[0].shape[0]

    def norm_back(v, e, gain):
        r = lax.rsqrt(jnp.mean(v * v, axis=1, keepdims=True) + EPS)
        u = v * r
        eg = e * gain
        grad = r * (eg - u * jnp.mean(eg * u, axis=1, keepdims=True))
        return grad, jnp.sum(e * u, axis=0, keepdims=True)

    d_latent, query_term_ref[...] = norm_back(
        latent_ref[...], back_ref[:, :latent_width], query_gain_ref[...]
    )
    half = HEAD_DIM // 2
    first_half = back_ref[:, latent_width : latent_width + half]
    second_half = back_ref[:, latent_width + half : latent_width + HEAD_DIM]
    cosine, sine_part = cos_ref[...], sin_ref[...]
    d_first = jnp.concatenate(
        [
            d_latent,
            first_half * cosine + second_half * sine_part,
            second_half * cosine - first_half * sine_part,
            back_ref[:, latent_width + HEAD_DIM :],
        ],
        axis=1,
    ).astype(BF)
    for k in range(count):
        here = slice(k * rows, (k + 1) * rows)
        target = odd_ref if k % 2 else even_ref
        at = slice(k // 2 * rows, (k // 2 + 1) * rows)
        target[at, :first_width] = dot_cols(normed_ref[:, here], d_first).astype(BF)
        dx_ref[:, here] = dot_rows(d_first, blocks[k][:, :first_width])
    dx_ref[...], gain_term_ref[...] = norm_back(
        x_ref[...].astype(F32), dx_ref[...], gain_ref[...]
    )


def last_products(back, latent, query_gain, normed, x, gain, cosine, sine_part, blocks):
    tok_count, width = x.shape
    rows, first_width = blocks[0].shape
    vmem = pl.BlockSpec(memory_space=pltpu.VMEM)
    half = jax.ShapeDtypeStruct((len(blocks) // 2 * rows, first_width), BF)
    return pl.pallas_call(
        functools.partial(last_kernel, len(blocks)),
        in_specs=[vmem] * (8 + len(blocks)),
        out_specs=[vmem] * 5,
        out_shape=[
            half,
            half,
            jax.ShapeDtypeStruct((tok_count, width), F32),
            jax.ShapeDtypeStruct((1, latent.shape[1]), F32),
            jax.ShapeDtypeStruct((1, width), F32),
        ],
        compiler_params=pltpu.CompilerParams(vmem_limit_bytes=44 * 2**20),
        cost_estimate=SMALL,
        name="last_products",
    )(back, latent, query_gain, normed, x, gain, cosine, sine_part, *blocks)


def block_places(shape, axis, core):
    rows = lax.broadcasted_iota(jnp.int32, shape, axis)
    half = shape[axis] // 2
    return rows + core * jnp.where(rows < half, half, -half)


def rotate_heads(values, cosine, sine_part, scale):
    half = HEAD_DIM // 2
    parts = []
    for at in range(0, values.shape[1], HEAD_DIM):
        first_half = values[:, at : at + half]
        second_half = values[:, at + half : at + HEAD_DIM]
        parts.append((first_half * cosine - second_half * sine_part) * scale)
        parts.append((second_half * cosine + first_half * sine_part) * scale)
    return jnp.concatenate(parts, axis=1)


def attend_kernel(
    count,
    heads,
    block,
    me_ref,
    starts_ref,
    cos_ref,
    sin_ref,
    wq_ref,
    wo_ref,
    *refs,
):
    packs = refs[:count]
    lat_ref, k_ref, v_ref, q_ref, mixed_ref, lse_ref, even_ref, odd_ref, vt_ref = refs[count:]
    me = me_ref[0]
    chip, core = me >> 1, me & 1
    index = pl.program_id(0)
    at = index ^ chip
    latent_width = lat_ref.shape[1]

    @pl.when(index == 0)
    def _():
        rows = packs[0].shape[0]
        for k, pack in enumerate(packs):
            here = slice(k * rows, (k + 1) * rows)
            lat_ref[here, :] = pack[:, :latent_width]
            k_ref[here, :] = pack[:, latent_width : latent_width + HEAD_DIM]
            v_ref[here, :] = pack[:, latent_width + HEAD_DIM :]
        for j in range(count // 2):
            here = slice(j * block, (j + 1) * block)
            vt_ref[:, here] = v_ref[here, :].T

    own = pl.ds(pl.multiple_of(index * block, block), block)
    query_raw = matmul(lat_ref[own, :], wq_ref[...])
    q_ref[...] = rotate_heads(
        query_raw, cos_ref[...], sin_ref[...], HEAD_DIM ** (-0.5)
    ).astype(BF)
    starts_row = starts_ref[...]
    key_place = block_places((block, 1), 0, core)
    query_place = at * block + block_places((1, block), 1, core)
    columns = [slice(h * HEAD_DIM, (h + 1) * HEAD_DIM) for h in range(heads)]

    def step(b, running):
        here = pl.ds(pl.multiple_of((b ^ chip) * block, block), block)
        keys_here = b * block + key_place
        visible = (keys_here <= query_place) & (keys_here >= starts_row)
        result = []
        for head in range(heads):
            running_max, running_sum, total = running[head]
            scores = dot_rows(k_ref[here, :], q_ref[:, columns[head]])
            scores = jnp.where(visible, scores, NEGATIVE)
            new_max = jnp.maximum(running_max, jnp.max(scores, axis=0, keepdims=True))
            factor = jnp.exp(running_max - new_max)
            terms = jnp.where(visible, jnp.exp(scores - new_max), 0.0)
            running_sum = running_sum * factor + jnp.sum(terms, axis=0, keepdims=True)
            total = total * factor + matmul(vt_ref[:, here], terms.astype(BF))
            result.append((new_max, running_sum, total))
        return tuple(result)

    start = (
        jnp.full((1, block), NEGATIVE, F32),
        jnp.zeros((1, block), F32),
        jnp.zeros((HEAD_DIM, block), F32),
    )
    running = lax.fori_loop(0, at + 1, step, (start,) * heads)
    for head in range(heads):
        running_max, running_sum, total = running[head]
        mixed_ref[:, columns[head]] = (total / running_sum).T.astype(BF)
        lse_ref[head : head + 1, :] = running_max + jnp.log(running_sum)
    terms = matmul(mixed_ref[...], wo_ref[...]).astype(BF)
    even_ref[...] = terms[: block // 2]
    odd_ref[...] = terms[block // 2 :]


def attend(me, starts, cosine, sine_part, query_up, output, packs, latent_width, block):
    rows, pack_width = packs[0].shape
    group_len = rows * len(packs)
    width = query_up.shape[1]
    heads = width // HEAD_DIM
    out_width = output.shape[1]
    tokens = pl.BlockSpec((block, width), lambda i, me: (i, 0))
    half = pl.BlockSpec((block // 2, out_width), lambda i, me: (i, 0))
    angle = pl.BlockSpec((block, HEAD_DIM // 2), lambda i, me: (i, 0))
    lanes = pl.BlockSpec((heads, block), lambda i, me: (0, i))
    shape = jax.ShapeDtypeStruct
    return pl.pallas_call(
        functools.partial(attend_kernel, len(packs), heads, block),
        grid_spec=pltpu.PrefetchScalarGridSpec(
            num_scalar_prefetch=1,
            grid=(group_len // block,),
            in_specs=[
                pl.BlockSpec((1, block), lambda i, me: (0, i)),
                angle,
                angle,
                whole_spec(query_up.shape),
                whole_spec(output.shape),
            ]
            + [whole_spec((rows, pack_width))] * len(packs),
            out_specs=[
                whole_spec((group_len, latent_width)),
                whole_spec((group_len, HEAD_DIM)),
                whole_spec((group_len, HEAD_DIM)),
                tokens,
                tokens,
                lanes,
                half,
                half,
            ],
            scratch_shapes=[pltpu.VMEM((HEAD_DIM, group_len), BF)],
        ),
        out_shape=[
            shape((group_len, latent_width), BF),
            shape((group_len, HEAD_DIM), BF),
            shape((group_len, HEAD_DIM), BF),
            shape((group_len, width), BF),
            shape((group_len, width), BF),
            shape((heads, group_len), F32),
            shape((group_len // 2, out_width), BF),
            shape((group_len // 2, out_width), BF),
        ],
        compiler_params=pltpu.CompilerParams(vmem_limit_bytes=44 * 2**20),
        cost_estimate=SMALL,
        name="attend",
    )(me, starts.reshape(1, group_len), cosine, sine_part, query_up, output, *packs)


def attend_back_kernel(
    count,
    heads,
    block,
    me_ref,
    starts_ref,
    cos_ref,
    sin_ref,
    q_ref,
    mixed_ref,
    lse_ref,
    k_ref,
    v_ref,
    wq_ref,
    wo_ref,
    *refs,
):
    blocks = refs[:count]
    d_ref, dq_ref, even_ref, odd_ref, dk_ref, dv_ref = refs[count:]
    me = me_ref[0]
    chip, core = me >> 1, me & 1
    index = pl.program_id(0)
    at = index ^ chip
    half = block // 2
    latent_width = wq_ref.shape[0]

    @pl.when(index == 0)
    def _():
        rows = blocks[0].shape[0]
        for k, source in enumerate(blocks):
            d_ref[k * rows : (k + 1) * rows, :] = source[...]
        dk_ref[...] = jnp.zeros_like(dk_ref)
        dv_ref[...] = jnp.zeros_like(dv_ref)

    own = pl.ds(pl.multiple_of(index * block, block), block)
    d_mixed = dot_rows(d_ref[own, :], wo_ref[...]).astype(BF)
    starts_row = starts_ref[...]
    key_place = block_places((block, 1), 0, core)
    query_place = at * block + block_places((1, block), 1, core)
    columns = [slice(h * HEAD_DIM, (h + 1) * HEAD_DIM) for h in range(heads)]
    offsets = [
        jnp.sum(
            (d_mixed[:, cols].astype(F32) * mixed_ref[:, cols].astype(F32)).T,
            axis=0,
            keepdims=True,
        )
        for cols in columns
    ]

    def step(b, running):
        here = pl.ds(pl.multiple_of((b ^ chip) * block, block), block)
        keys_here = b * block + key_place
        visible = (keys_here <= query_place) & (keys_here >= starts_row)
        keys, values = k_ref[here, :], v_ref[here, :]
        result = []
        for head in range(heads):
            q, dm = q_ref[:, columns[head]], d_mixed[:, columns[head]]
            scores = dot_rows(keys, q)
            scores = jnp.where(visible, scores, NEGATIVE)
            probs = jnp.where(visible, jnp.exp(scores - lse_ref[head : head + 1, :]), 0.0)
            d_probs = dot_rows(values, dm)
            d_scores = (probs * (d_probs - offsets[head])).astype(BF)
            dv_ref[here, :] += matmul(probs.astype(BF), dm)
            dk_ref[here, :] += matmul(d_scores, q)
            result.append(running[head] + dot_cols(d_scores, keys))
        return tuple(result)

    start = (jnp.zeros((block, HEAD_DIM), F32),) * heads
    d_queries = jnp.concatenate(lax.fori_loop(0, at + 1, step, start), axis=1)
    dq_ref[...] = rotate_heads(
        d_queries, cos_ref[...], -sin_ref[...], HEAD_DIM ** (-0.5)
    ).astype(BF)
    terms = dot_rows(dq_ref[...], wq_ref[...]).astype(BF)
    rows_here = pl.ds(pl.multiple_of(index * half, half), half)
    even_ref[rows_here, :latent_width] = terms[:half]
    odd_ref[rows_here, :latent_width] = terms[half:]

    @pl.when(index == pl.num_programs(0) - 1)
    def _():
        for j in range(count // 2):
            to = slice(j * half, (j + 1) * half)
            for target, first in ((even_ref, j * block), (odd_ref, j * block + half)):
                rows = slice(first, first + half)
                target[to, latent_width : latent_width + HEAD_DIM] = dk_ref[rows, :].astype(BF)
                target[to, latent_width + HEAD_DIM :] = dv_ref[rows, :].astype(BF)


def attend_back(
    me, starts, cosine, sine_part, queries, mixed, lse, keys, values, query_up, output, blocks, block
):
    group_len, width = queries.shape
    heads = width // HEAD_DIM
    rows, out_width = blocks[0].shape
    latent_width = query_up.shape[0]
    pack_width = latent_width + 2 * HEAD_DIM
    tokens = pl.BlockSpec((block, width), lambda i, me: (i, 0))
    angle = pl.BlockSpec((block, HEAD_DIM // 2), lambda i, me: (i, 0))
    lanes = pl.BlockSpec((heads, block), lambda i, me: (0, i))
    half = (group_len // 2, pack_width)
    shape = jax.ShapeDtypeStruct
    return pl.pallas_call(
        functools.partial(attend_back_kernel, len(blocks), heads, block),
        grid_spec=pltpu.PrefetchScalarGridSpec(
            num_scalar_prefetch=1,
            grid=(group_len // block,),
            in_specs=[
                pl.BlockSpec((1, block), lambda i, me: (0, i)),
                angle,
                angle,
                tokens,
                tokens,
                lanes,
                whole_spec(keys.shape),
                whole_spec(values.shape),
                whole_spec(query_up.shape),
                whole_spec(output.shape),
            ]
            + [whole_spec((rows, out_width))] * len(blocks),
            out_specs=[
                whole_spec((group_len, out_width)),
                tokens,
                whole_spec(half),
                whole_spec(half),
            ],
            scratch_shapes=[pltpu.VMEM((group_len, HEAD_DIM), F32)] * 2,
        ),
        out_shape=[
            shape((group_len, out_width), BF),
            shape((group_len, width), BF),
            shape(half, BF),
            shape(half, BF),
        ],
        compiler_params=pltpu.CompilerParams(vmem_limit_bytes=48 * 2**20),
        cost_estimate=SMALL,
        name="attend_back",
    )(
        me,
        starts.reshape(1, group_len),
        cosine,
        sine_part,
        queries,
        mixed,
        lse,
        keys,
        values,
        query_up,
        output,
        *blocks,
    )


def local(
    layer_input,
    doc_lengths,
    attention_gain,
    query_down,
    query_gain,
    query_up,
    keyvalue_weight,
    output_weight,
    feedforward_gain,
    gate_weight,
    up_weight,
    down_weight,
    cotangent,
):
    n_seq, n_dp = lax.axis_size("seq"), lax.axis_size("dp")
    me = lax.axis_index("seq")
    input_low = layer_input[0]
    tokens = input_low.astype(F32)
    tok_count, width = tokens.shape
    latent_width = query_down.shape[1]
    group_len = tok_count * n_seq
    heads = HEADS // n_seq
    hidden_units = gate_weight.shape[1] // n_seq

    starts_all, position_all = document_starts(doc_lengths[0], group_len)
    starts_all = relative(starts_all, 0)
    position_all = relative(position_all, 0)
    cosine_all, sine_all = rope_tables(position_all, HEAD_DIM)
    me_array = me.astype(jnp.int32).reshape(1)

    own_rows = query_down.shape[0]
    query_rows = query_gain.shape[0]
    gains = jnp.stack(
        [attention_gain, feedforward_gain, jnp.pad(query_gain, (0, own_rows - query_rows))], axis=1
    )
    first_set = jnp.concatenate(
        [query_down, keyvalue_weight, jnp.pad(gains, ((0, 0), (0, 125)))], axis=1
    )
    first_set, query_up = together(first_set, query_up)
    first_part = gather_dp_steps(first_set)
    d_feed_blocks = gather_near(cotangent[0])
    query_part = exchange(split_columns(query_up)).reshape(-1, query_up.shape[1] // n_seq)
    fold = query_part.shape[0] * query_part.shape[1] // width
    attention_set = jnp.concatenate([output_weight, query_part.reshape(fold, width)], axis=0)
    first_part, d_feed_blocks, cosine_all, sine_all, attention_set = together(
        first_part, d_feed_blocks, cosine_all, sine_all, attention_set
    )
    cosine, sine_part = cosine_all[:tok_count], sine_all[:tok_count]
    attention_part = gather_dp(attention_set)
    gate_weight, up_weight, first_part = together(gate_weight, up_weight, first_part)
    gate_up = exchange(jnp.stack([split_columns(gate_weight), split_columns(up_weight)], axis=1))
    first_blocks, gate_up, d_feed_blocks = together(
        gather_blocks(first_part), gate_up, d_feed_blocks
    )
    full_gate_up = gather_dp(gate_up.reshape(-1, hidden_units)).reshape(n_dp, *gate_up.shape)
    full_down = gather_dp(down_weight)
    d_feed_blocks = gather_far(d_feed_blocks)
    tokens_low_rel = relative(input_low, 1)
    first_width = latent_width + 2 * HEAD_DIM
    first_out, normed_rel, gain_rows = first_projections(
        tokens_low_rel, first_blocks, first_width
    )
    tokens_rel = tokens_low_rel.astype(F32)
    attention_gain_rel = gain_rows[0]
    other_gains = relative_vectors(gain_rows[1:3])
    feed_gain_f = other_gains[0]
    query_gain_f = other_gains[1].reshape(-1, own_rows)[:, :query_rows].reshape(-1)

    latent = first_out[:, :latent_width]
    keyvalue = first_out[:, latent_width:first_width]
    latent_low = rms_norm(latent, query_gain_f).astype(BF)
    key_local = rotate(keyvalue[:, :HEAD_DIM], cosine, sine_part)
    pack = jnp.concatenate(
        [latent_low, key_local.astype(BF), keyvalue[:, HEAD_DIM:].astype(BF)], axis=1
    )
    pack, attention_part = together(pack, attention_part)
    out_rows = output_weight.shape[0]
    attention_part = attention_part.reshape(n_dp, -1, width)
    full_output = attention_part[:, :out_rows].reshape(-1, width)
    full_query_up = rows_in_order(
        attention_part[:, out_rows:].reshape(-1, query_part.shape[1]), query_up.shape[0]
    )
    packs = gather_blocks(pack)
    d_feed = stack_blocks(gather_cores(d_feed_blocks))
    packs, full_query_up, full_output, d_feed = together(
        packs, full_query_up, full_output, d_feed
    )
    block = 2 * tok_count
    latent_all, keys, values, queries, mixed_low, lse, out_even, out_odd = attend(
        me_array,
        starts_all,
        cosine_all,
        sine_all,
        full_query_up,
        full_output,
        packs,
        latent_width,
        block,
    )

    d_result = cotangent[0].astype(F32)
    hidden = tokens + scatter_pairs(out_even, out_odd)
    hidden, full_gate_up = together(hidden, full_gate_up)

    feed_low = rms_norm(hidden, feed_gain_f).astype(BF)
    feed_blocks = gather_blocks(feed_low)
    feed, active_low, silu_low, slope_low, gate_ordered, up_ordered = feed_forward(
        feed_blocks, full_gate_up, block
    )
    grad_down_term = dot_cols(active_low, d_feed).astype(BF)
    silu_low, grad_down_term = lax.optimization_barrier((silu_low, grad_down_term))
    grad_down = scatter_dp(grad_down_term)
    half_chips = n_seq // 4
    dg_high, du_high, *terms_high = feed_back(
        d_feed,
        silu_low,
        slope_low,
        gate_ordered,
        up_ordered,
        full_down,
        block,
        half_chips,
        half_chips,
    )
    silu_again, terms_high = together(silu_low, terms_high)
    dg_low, du_low, *terms_low = feed_back(
        d_feed, silu_again, slope_low, gate_ordered, up_ordered, full_down, block, 0, half_chips
    )
    feed_sums = chip_sums(*terms_low, half_chips) + chip_sums(*terms_high, half_chips)
    feed_sums, feed = together(feed_sums, feed)
    d_feed_normed = scatter_last(scatter_relay(feed_sums))
    grad_gate_up_term = gate_up_grad(feed, (dg_low, du_low), (dg_high, du_high), n_dp, n_seq)
    d_feed_normed, grad_gate_up_term = together(d_feed_normed, grad_gate_up_term)
    grad_gate_up = scatter_dp(grad_gate_up_term.reshape(-1, hidden_units))

    d_hidden_norm, grad_feed_gain_term = jax.vjp(rms_norm, hidden, feed_gain_f)[1](d_feed_normed)
    d_hidden = d_result + d_hidden_norm
    d_branch_blocks = gather_blocks(d_hidden.astype(BF))
    result_terms = pair_product(active_low, full_down, block)
    result_sums = chip_sums(*result_terms, n_seq // 2)
    d_branch_blocks, result_sums = together(d_branch_blocks, result_sums)
    result_left = scatter_relay(result_sums)
    d_branch, d_query_low, back_even, back_odd = attend_back(
        me_array,
        starts_all,
        cosine_all,
        sine_all,
        queries,
        mixed_low,
        lse,
        keys,
        values,
        full_query_up,
        full_output,
        d_branch_blocks,
        block,
    )
    back_even, back_odd, grad_down, result_left = together(
        back_even, back_odd, grad_down, result_left
    )
    back_local = scatter_pairs(back_even, back_odd)
    grad_output_term = dot_cols(mixed_low, d_branch).astype(BF)
    grad_query_term = rows_by_dp(dot_cols(latent_all, d_query_low).astype(BF))
    grad_attention_term = jnp.concatenate(
        [
            grad_output_term.reshape(n_dp, out_rows, width),
            grad_query_term.reshape(n_dp, fold, width),
        ],
        axis=1,
    ).reshape(-1, width)
    back_local, grad_attention_term, grad_gate_up = together(
        back_local, grad_attention_term, grad_gate_up
    )
    grad_attention = scatter_dp(grad_attention_term)

    first_even, first_odd, d_tokens_rel, query_term, gain_term = last_products(
        back_local,
        latent,
        query_gain_f.reshape(1, -1),
        normed_rel,
        tokens_low_rel,
        gain_rows[:1],
        cosine,
        sine_part,
        first_blocks,
    )
    input_grad = (d_hidden + relative(d_tokens_rel, 1))[None]
    query_column = jnp.pad(
        query_term.reshape(-1, query_rows), ((0, 0), (0, own_rows - query_rows))
    ).reshape(1, -1)
    other_terms = relative_vectors(
        jnp.concatenate([grad_feed_gain_term.reshape(1, -1), query_column], axis=0)
    )
    gain_terms = jnp.concatenate([gain_term, other_terms], axis=0)
    columns = jnp.pad(gain_terms, ((0, 125), (0, 0))).T.astype(BF).reshape(n_seq, -1, 128)
    first_even = lax.dynamic_update_slice(
        first_even, columns[0::2].reshape(-1, 128), (0, first_width)
    )
    first_odd = lax.dynamic_update_slice(
        first_odd, columns[1::2].reshape(-1, 128), (0, first_width)
    )
    first_sum = scatter_pairs(first_even, first_odd).astype(BF)
    first_sum, grad_attention = lax.optimization_barrier((first_sum, grad_attention))
    grad_first = scatter_dp(first_sum).astype(F32)
    result_left, first_sum = together(result_left, first_sum)
    result = hidden + scatter_last(result_left)
    layer_output = result.astype(BF)[None]

    grad_output_weight = grad_attention[:out_rows].astype(F32)
    grad_query_up = exchange(grad_attention[out_rows:].reshape(n_seq, query_rows, -1))
    grad_query_up = grad_query_up.transpose(1, 0, 2).reshape(query_rows, -1).astype(F32)

    gate_up_rows = exchange(grad_gate_up.reshape(n_seq, 2, own_rows, -1)).astype(F32)
    grad_gate = gate_up_rows[:, 0].transpose(1, 0, 2).reshape(own_rows, -1)
    grad_up = gate_up_rows[:, 1].transpose(1, 0, 2).reshape(own_rows, -1)
    return (
        layer_output,
        input_grad,
        grad_first[:, first_width],
        grad_first[:, :latent_width],
        grad_first[:query_rows, first_width + 2],
        grad_query_up,
        grad_first[:, latent_width:first_width],
        grad_output_weight,
        grad_first[:, first_width + 1],
        grad_gate,
        grad_up,
        grad_down.astype(F32),
    )


def solution(mesh):
    shards = P(("seq", "dp"))
    tokens = P("dp", "seq", None)
    weight = P(("seq", "dp"), None)
    return jax.shard_map(
        local,
        mesh=mesh,
        in_specs=(
            tokens,
            P("dp", None),
            shards,
            weight,
            shards,
            weight,
            weight,
            weight,
            shards,
            weight,
            weight,
            weight,
            tokens,
        ),
        out_specs=(
            tokens,
            tokens,
            shards,
            weight,
            shards,
            weight,
            weight,
            weight,
            shards,
            weight,
            weight,
            weight,
        ),
        check_vma=False,
    )
```

```python
import functools

import jax
import jax.numpy as jnp
from jax import lax
from jax.experimental import pallas as pl
from jax.experimental.pallas import tpu as pltpu
from jax.sharding import PartitionSpec as P

HEADS = 16
HEAD_DIM = 256


EPS = 1e-05
ROPE_BASE = 10000.0
NEGATIVE = -1e30
BF = jnp.bfloat16
F32 = jnp.float32
KERNEL_VMEM = 60 * 2**20


KERNEL_COST = dict(
    stack_blocks=0.01,
    first_projections=0.01,
    attend=0.01,
    feed_forward=0.01,
    feed_back=0.01,
    gate_up_grad=0.01,
    pair_product=3,
    attend_back=0.01,
    last_products=0.01,
    first_grads=0.01,
    columns_back=0.01,
    attention_grads=0.01,
)
(
    FIRST_PART,
    FIRST_NEAR,
    FIRST_FAR,
    FIRST_BLOCKS,
    PACK,
    PACK_NEAR,
    PACKS,
    ATTENDED,
    OUT_LEFT,
    HIDDEN,
    FEED_NEAR,
    FEED_BLOCKS,
    ACTIVE,
    TERMS_HIGH,
    TERMS_LOW,
    FEED_SUMS,
    FEED_LEFT,
    D_NORMED,
    BRANCH_NEAR,
    BRANCH_BLOCKS,
    BRANCH_ALL,
    BACK_TERMS,
    BACK_SUMS,
    BACK_LEFT,
    BACK_LOCAL,
    FIRST_TERMS,
    LAST_NEAR,
    LAST_BLOCKS,
    FIRST_SUM,
) = range(29)
DUE = dict(
    tables=FIRST_BLOCKS,
    feed_step=FIRST_PART,
    query_part=FIRST_PART,
    gate_up_parts=FIRST_NEAR,
    gate_up=PACK,
    gate_up_all=FEED_NEAR,
    feed_far=ATTENDED,
    feed_stack=FEED_NEAR,
    grad_down_term=ACTIVE,
    down_all=TERMS_HIGH,
    high_swap=TERMS_LOW,
    grad_down=D_NORMED,
    grad_gate_up_term=D_NORMED,
    result_terms=BRANCH_NEAR,
    result_sums=BRANCH_BLOCKS,
    result_left=BRANCH_ALL,
    grad_gate_up=BACK_LEFT,
    grad_attention_term=BACK_LEFT,
    grad_attention=FIRST_SUM,
    attention=PACK,
    attention_weights=PACK_NEAR,
    normed_columns=ACTIVE,
    result_hops=BACK_TERMS,
)
BEGIN = dict(
    output=FIRST_PART,
    gate_up=FIRST_FAR,
    feed_far=PACKS,
    grad_gate_up_term=FEED_LEFT,
    result_terms=D_NORMED,
    result_left=BRANCH_NEAR,
    result_last=FIRST_SUM,
    grad_attention_term=BACK_SUMS,
    normed_columns=FEED_BLOCKS,
    feed_stack=HIDDEN,
    gate_up_rows=FIRST_SUM,
)


def takes(kernel):
    microseconds = KERNEL_COST[kernel]
    return pl.CostEstimate(
        flops=int(microseconds * 1e9), bytes_accessed=int(microseconds * 2e6), transcendentals=0
    )


class Chain:
    def __init__(self):
        self.stages = {}
        self.side = {}

    def add(self, **made):
        self.side.update(made)

    def begin(self, **waiting):
        ((name, value),) = waiting.items()
        return after(value, self.stages[BEGIN[name]]) if name in BEGIN else value

    def stage(self, at, value):
        due = [name for name in self.side if DUE.get(name) == at]
        if due:
            value, there = together(value, [self.side[name] for name in due])
            self.side.update(zip(due, there, strict=True))
        self.stages[at] = value
        return value

    def __getattr__(self, name):
        return self.side[name]


def rms_norm(values, norm_gain):
    return values * lax.rsqrt(jnp.mean(values * values, axis=-1, keepdims=True) + EPS) * norm_gain


def rope_tables(position, feature_width):
    half_width = feature_width // 2
    freqs = ROPE_BASE ** (-jnp.arange(half_width, dtype=F32) * 2.0 / feature_width)
    angles = position.astype(F32)[:, None] * freqs[None, :]
    return (jnp.cos(angles), jnp.sin(angles))


def rotate(values, cosine, sine_part):
    half_width = values.shape[-1] // 2
    first_half = values[..., :half_width]
    second_half = values[..., half_width:]
    return jnp.concatenate(
        [
            first_half * cosine - second_half * sine_part,
            second_half * cosine + first_half * sine_part,
        ],
        axis=-1,
    )


def document_starts(lengths_row, group_len):
    doc_ends = jnp.cumsum(lengths_row)
    places = jnp.arange(group_len, dtype=jnp.int32)
    past_ends = (places[:, None] >= doc_ends[None, :]).astype(jnp.int32)
    starts = jnp.sum(past_ends * lengths_row[None, :], axis=1)
    return (starts, places - starts)


def gated(gate_proj, upward):
    return jax.nn.silu(gate_proj) * upward


def matmul(left_side, right_side):
    return jnp.dot(left_side, right_side, preferred_element_type=F32)


def dot_rows(left_side, right_side):
    return lax.dot_general(
        left_side, right_side, (((1,), (1,)), ((), ())), preferred_element_type=F32
    )


def dot_cols(left_side, right_side):
    return lax.dot_general(
        left_side, right_side, (((0,), (0,)), ((), ())), preferred_element_type=F32
    )


def flip(block, bits):
    n_seq = lax.axis_size("seq")
    return lax.ppermute(block, "seq", [(i, i ^ bits) for i in range(n_seq)])


def gather_near(rows):
    n_seq = lax.axis_size("seq")
    hops = (2, 4) if n_seq == 8 else range(2, n_seq, 2)
    return {0: rows} | {bits: flip(rows, bits) for bits in hops}


def gather_far(blocks):
    if lax.axis_size("seq") != 8:
        return blocks
    half = blocks[0].shape[0] // 2
    return blocks | {6: [flip(blocks[4][:half], 2), flip(blocks[2][half:], 4)]}


def gather_cores(blocks):
    whole = []
    for bits in range(0, lax.axis_size("seq"), 2):
        own = blocks[bits] if isinstance(blocks[bits], list) else [blocks[bits]]
        whole += own + [flip(piece, 1) for piece in own]
    return whole


def piece_slices(pieces):
    slices, first = [], 0
    for piece in pieces:
        slices.append(slice(first, first + piece.shape[0]))
        first += piece.shape[0]
    return slices


def gather_blocks(rows):
    return gather_cores(gather_far(gather_near(rows)))


def together(*values):
    flat, tree = jax.tree.flatten(values)
    return jax.tree.unflatten(tree, lax.optimization_barrier(flat))


def after(values, *first):
    return together(values, *first)[0]


def stack_kernel(count, *refs):
    sources, target, held, arrived, left = refs[:count], *refs[count:]
    moves = []
    for k, (source, rows) in enumerate(zip(sources, piece_slices(sources), strict=True)):
        here = pl.ds(rows.start, rows.stop - rows.start)
        moves.append(
            (
                pltpu.make_async_copy(source, held.at[here], arrived.at[k]),
                pltpu.make_async_copy(held.at[here], target.at[here], left.at[k]),
            )
        )
    for come, _ in moves:
        come.start()
    for come, go in moves:
        come.wait()
        go.start()
    for _, go in moves:
        go.wait()


def stack_blocks(pieces):
    width, dtype = pieces[0].shape[1], pieces[0].dtype
    shape = (sum(piece.shape[0] for piece in pieces), width)
    return pl.pallas_call(
        functools.partial(stack_kernel, len(pieces)),
        in_specs=[pl.BlockSpec(memory_space=pl.ANY)] * len(pieces),
        out_specs=pl.BlockSpec(memory_space=pl.ANY),
        out_shape=jax.ShapeDtypeStruct(shape, dtype),
        scratch_shapes=[pltpu.VMEM(shape, dtype)]
        + [pltpu.SemaphoreType.DMA((len(pieces),))] * 2,
        compiler_params=pltpu.CompilerParams(vmem_limit_bytes=KERNEL_VMEM),
        cost_estimate=takes("stack_blocks"),
        name="stack_blocks",
    )(*pieces)


def plus(first, second):
    return (first.astype(F32) + second.astype(F32)).astype(BF)


def split_chips(total, count):
    rows = total.shape[0] // count
    return [total[k * rows : (k + 1) * rows] for k in range(count)]


def chip_sums(even, odd, count):
    return split_chips(plus(even, flip(odd, 1)), count)


def scatter_relay(sums):
    n_seq = lax.axis_size("seq")
    if n_seq != 8:
        return {k: [part] for k, part in enumerate(sums)}
    half = sums[0].shape[0] // 2
    far_x = flip(sums[3][:half], 2)
    far_y = flip(sums[3][half:], 4)
    return {
        0: [sums[0]],
        1: [sums[1][:half], plus(sums[1][half:], far_y)],
        2: [sums[2][half:], plus(sums[2][:half], far_x)],
    }


def last_hops(left):
    if lax.axis_size("seq") != 8:
        return [flip(parts[0], 2 * k) for k, parts in left.items() if k]
    return [flip(part, 2) for part in left[1]] + [flip(part, 4) for part in left[2]]


def hops_sum(left, hops):
    own = left[0][0].astype(F32)
    if lax.axis_size("seq") != 8:
        return sum((hop.astype(F32) for hop in hops), own)
    x_low, x_high, y_high, y_low = [hop.astype(F32) for hop in hops]
    return own + jnp.concatenate([x_low + y_low, x_high + y_high], axis=0)


def scatter_last(left):
    return hops_sum(left, last_hops(left))


def scatter_pairs(even, odd):
    count = lax.axis_size("seq") // 2
    return scatter_last(scatter_relay(chip_sums(even, odd, count)))


def relative(values, axis):
    n_seq, me = lax.axis_size("seq"), lax.axis_index("seq")
    size = values.shape[axis] // n_seq
    parts = [
        lax.dynamic_slice_in_dim(values, (me ^ k) * size, size, axis) for k in range(n_seq)
    ]
    return jnp.concatenate(parts, axis=axis)


def relative_vectors(values):
    n_seq, me = lax.axis_size("seq"), lax.axis_index("seq")
    count, length = values.shape
    values = values.reshape(count, n_seq, length // n_seq)
    bit = 1
    while bit < n_seq:
        pairs = values.reshape(count, n_seq // (2 * bit), 2, bit, length // n_seq)
        swapped = jnp.concatenate([pairs[:, :, 1:], pairs[:, :, :1]], axis=2)
        values = jnp.where((me & bit) != 0, swapped, pairs).reshape(values.shape)
        bit *= 2
    return values.reshape(count, length)


def gather_dp(rows):
    return lax.all_gather(rows, "dp", axis=0, tiled=True)


def gather_dp_steps(rows):
    n_dp, me = lax.axis_size("dp"), lax.axis_index("dp")
    size = rows.shape[0]
    whole = jnp.zeros((n_dp * size, rows.shape[1]), rows.dtype)
    for bits in range(n_dp):
        block = rows
        if bits:
            block = lax.ppermute(rows, "dp", [(i, i ^ bits) for i in range(n_dp)])
        whole = lax.dynamic_update_slice_in_dim(whole, block, (me ^ bits) * size, 0)
    return whole


def scatter_dp(terms):
    return lax.psum_scatter(terms, "dp", scatter_dimension=0, tiled=True)


def split_columns(shard):
    n_seq = lax.axis_size("seq")
    rows, width = shard.shape
    return shard.reshape(rows, n_seq, width // n_seq).transpose(1, 0, 2)


def exchange(parts):
    return lax.all_to_all(parts, "seq", 0, 0)


def rows_in_order(gathered, rows):
    n_seq, n_dp = lax.axis_size("seq"), lax.axis_size("dp")
    width = gathered.shape[-1]
    return gathered.reshape(n_dp, n_seq, rows, width).transpose(1, 0, 2, 3).reshape(-1, width)


def rows_by_dp(terms):
    n_seq, n_dp = lax.axis_size("seq"), lax.axis_size("dp")
    total, width = terms.shape
    rows = total // (n_seq * n_dp)
    return terms.reshape(n_seq, n_dp, rows, width).transpose(1, 0, 2, 3)


def spread(n_dp, own, rows):
    shape = (n_dp * own, n_dp * rows)
    at = lax.broadcasted_iota(jnp.int32, shape, 0)
    to = lax.broadcasted_iota(jnp.int32, shape, 1)
    hit = to == at // own * rows + at % own
    return jnp.where(hit, 1.0, 0.0).astype(BF)


def exchanged_rows(rows, me):
    count = len(rows)
    result = []
    for k in range(count):
        row = rows[0]
        for at in range(1, count):
            row = jnp.where((me ^ k) == at, rows[at], row)
        result.append(row)
    return result


def first_kernel(count, n_seq, n_dp, me_ref, x_ref, cos_ref, sin_ref, *refs):
    pieces = refs[:count]
    pack_ref, latent_ref, parts_ref, gain_ref, feed_gain_ref, query_gain_ref, out_ref = refs[count:]
    me = me_ref[0]
    latent_width = latent_ref.shape[1]
    low_width = pack_ref.shape[1]
    x = x_ref[...].astype(F32)
    scale = lax.rsqrt(jnp.mean(x * x, axis=1, keepdims=True) + EPS)
    size = x_ref.shape[1] // n_seq
    gains = []
    for k, here in enumerate(piece_slices(pieces)):
        gains.append(pieces[k][:, low_width:].astype(F32).T[:8])
        owner, first = me ^ (here.start // size), here.start % size
        rows = here.stop - here.start
        own = pl.ds(pl.multiple_of(owner * size + first, rows), rows)
        normed = (x_ref[:, own].astype(F32) * scale * gains[k][:1]).astype(BF)
        parts_ref[owner, :, first : first + rows] = normed
        gain_ref[:, own] = gains[k][:1]
        feed_gain_ref[:, own] = gains[k][1:2]
        part = matmul(normed, pieces[k][:, :low_width])
        if k == 0:
            out_ref[...] = part
        else:
            out_ref[...] += part
    gains = jnp.concatenate(gains, axis=1)
    own = latent_width // (n_seq * n_dp)
    query_rows = []
    for k in range(n_seq):
        query_rows.append(gains[2:3, k * size : (k + 1) * size])
    query_rows = exchanged_rows(query_rows, me)
    query_rows = dot_rows(
        jnp.concatenate(query_rows, axis=0).astype(BF), spread(n_dp, own, size // n_dp)
    )
    query_gain = jnp.concatenate([query_rows[k : k + 1] for k in range(n_seq)], axis=1)
    query_gain_ref[...] = query_gain
    latent = out_ref[:, :latent_width]
    latent_ref[...] = latent
    latent_scale = lax.rsqrt(jnp.mean(latent * latent, axis=1, keepdims=True) + EPS)
    pack_ref[:, :latent_width] = (latent * latent_scale * query_gain).astype(BF)
    keyvalue = out_ref[:, latent_width:]
    pack_ref[:, latent_width : latent_width + HEAD_DIM] = rotate_heads(
        keyvalue[:, :HEAD_DIM], cos_ref[...], sin_ref[...], 1.0
    ).astype(BF)
    pack_ref[:, latent_width + HEAD_DIM :] = keyvalue[:, HEAD_DIM:].astype(BF)


def first_projections(me, x, cosine, sine_part, pieces, latent_width):
    n_seq = lax.axis_size("seq")
    tok_count, width = x.shape
    low_width = pieces[0].shape[1] - 128
    vmem = pl.BlockSpec(memory_space=pltpu.VMEM)
    shape = jax.ShapeDtypeStruct
    return pl.pallas_call(
        functools.partial(
            first_kernel, len(pieces), lax.axis_size("seq"), lax.axis_size("dp")
        ),
        in_specs=[pl.BlockSpec(memory_space=pltpu.SMEM)] + [vmem] * (3 + len(pieces)),
        out_specs=[vmem] * 6,
        out_shape=[
            shape((tok_count, low_width), BF),
            shape((tok_count, latent_width), F32),
            shape((n_seq, tok_count, width // n_seq), BF),
            shape((1, width), F32),
            shape((1, width), F32),
            shape((1, latent_width), F32),
        ],
        scratch_shapes=[pltpu.VMEM((tok_count, low_width), F32)],
        compiler_params=pltpu.CompilerParams(vmem_limit_bytes=KERNEL_VMEM),
        cost_estimate=takes("first_projections"),
        name="first_projections",
    )(me, x, cosine, sine_part, *pieces)


def weights_in_order(raw_ref, gate_ref, up_ref):
    n_dp, n_seq, _, rows, _ = raw_ref.shape
    for s in range(n_seq):
        for z in range(n_dp):
            here = pl.ds((s * n_dp + z) * rows, rows)
            gate_ref[here, :] = raw_ref[z, s, 0]
            up_ref[here, :] = raw_ref[z, s, 1]


def feed_kernel(count, block, *refs):
    blocks, raw_ref = refs[:count], refs[count]
    x_ref, act_ref, silu_ref, slope_ref, gate_ref, up_ref = refs[count + 1 :]
    at = pl.program_id(0)

    @pl.when(at == 0)
    def _():
        for source, here in zip(blocks, piece_slices(blocks), strict=True):
            x_ref[here, :] = source[...]
        weights_in_order(raw_ref, gate_ref, up_ref)

    x = x_ref[pl.ds(pl.multiple_of(at * block, block), block), :]
    gate = matmul(x, gate_ref[...])
    upward = matmul(x, up_ref[...])
    sigmoid = 1.0 / (1.0 + jnp.exp(-gate))
    silu = gate * sigmoid
    act_ref[...] = (silu * upward).astype(BF)
    silu_ref[...] = silu.astype(BF)
    slope_ref[...] = (upward * (sigmoid + silu * (1.0 - sigmoid))).astype(BF)


def whole_spec(shape):
    return pl.BlockSpec(shape, lambda *_: (0,) * len(shape), pipeline_mode=pl.Buffered(1))


def feed_forward(blocks, raw, block):
    width = blocks[0].shape[1]
    group_len = sum(piece.shape[0] for piece in blocks)
    hidden = raw.shape[-1]
    units = pl.BlockSpec((block, hidden), lambda i: (i, 0))
    weight = jax.ShapeDtypeStruct((width, hidden), BF)
    return pl.pallas_call(
        functools.partial(feed_kernel, len(blocks), block),
        grid=(group_len // block,),
        in_specs=[whole_spec(piece.shape) for piece in blocks] + [whole_spec(raw.shape)],
        out_specs=[whole_spec((group_len, width))]
        + [units] * 3
        + [whole_spec((width, hidden))] * 2,
        out_shape=[jax.ShapeDtypeStruct((group_len, width), BF)]
        + [jax.ShapeDtypeStruct((group_len, hidden), BF)] * 3
        + [weight] * 2,
        compiler_params=pltpu.CompilerParams(vmem_limit_bytes=KERNEL_VMEM),
        cost_estimate=takes("feed_forward"),
        name="feed_forward",
    )(*blocks, raw)


def feed_back_kernel(
    d_ref, silu_ref, slope_ref, gate_ref, up_ref, down_ref, dg_ref, du_ref, even_ref, odd_ref
):
    d_active = dot_rows(d_ref[...], down_ref[...])
    d_gate = (d_active * slope_ref[...].astype(F32)).astype(BF)
    d_up = (d_active * silu_ref[...].astype(F32)).astype(BF)
    dg_ref[...] = d_gate
    du_ref[...] = d_up
    terms = (dot_rows(d_gate, gate_ref[...]) + dot_rows(d_up, up_ref[...])).astype(BF)
    half = terms.shape[0] // 2
    even_ref[...] = terms[:half]
    odd_ref[...] = terms[half:]


def feed_back(d, silu, slope, gate, up, down, block, first, count):
    width, hidden = gate.shape
    tokens = pl.BlockSpec((block, width), lambda i: (i + first, 0))
    units = pl.BlockSpec((block, hidden), lambda i: (i + first, 0))
    half = pl.BlockSpec((block // 2, width), lambda i: (i, 0))
    return pl.pallas_call(
        feed_back_kernel,
        grid=(count,),
        in_specs=[tokens, units, units]
        + [whole_spec(gate.shape), whole_spec(up.shape), whole_spec(down.shape)],
        out_specs=[pl.BlockSpec((block, hidden), lambda i: (i, 0))] * 2 + [half] * 2,
        out_shape=[jax.ShapeDtypeStruct((count * block, hidden), BF)] * 2
        + [jax.ShapeDtypeStruct((count * block // 2, width), BF)] * 2,
        compiler_params=pltpu.CompilerParams(vmem_limit_bytes=KERNEL_VMEM),
        cost_estimate=takes("feed_back"),
        name="feed_back",
    )(d, silu, slope, gate, up, down)


def gate_up_grad_kernel(x_ref, dg_low, du_low, dg_high, du_high, out_ref):
    n_dp, _, _, rows, _ = out_ref.shape
    middle = dg_low.shape[0]
    low, high = x_ref[:middle, :], x_ref[middle:, :]
    for which, (d_low, d_high) in enumerate(((dg_low, dg_high), (du_low, du_high))):
        terms = (dot_cols(low, d_low[...]) + dot_cols(high, d_high[...])).astype(BF)
        for z in range(n_dp):
            out_ref[z, 0, which] = terms[z * rows : (z + 1) * rows]


def gate_up_grad(x, low, high, n_dp, n_seq):
    group_len, width = x.shape
    hidden = low[0].shape[1]
    rows = width // (n_dp * n_seq)
    return pl.pallas_call(
        gate_up_grad_kernel,
        grid=(n_seq,),
        in_specs=[pl.BlockSpec((group_len, n_dp * rows), lambda i: (0, i))]
        + [whole_spec(part.shape) for part in (*low, *high)],
        out_specs=pl.BlockSpec((n_dp, 1, 2, rows, hidden), lambda i: (0, i, 0, 0, 0)),
        out_shape=jax.ShapeDtypeStruct((n_dp, n_seq, 2, rows, hidden), BF),
        compiler_params=pltpu.CompilerParams(vmem_limit_bytes=KERNEL_VMEM),
        cost_estimate=takes("gate_up_grad"),
        name="gate_up_grad",
    )(x, *low, *high)


def pair_product_kernel(left_ref, right_ref, even_ref, odd_ref):
    terms = matmul(left_ref[...], right_ref[...]).astype(BF)
    half = terms.shape[0] // 2
    even_ref[...] = terms[:half]
    odd_ref[...] = terms[half:]


def pair_product(left, right, block):
    rows, depth = left.shape
    width = right.shape[1]
    half = pl.BlockSpec((block // 2, width), lambda i: (i, 0))
    return pl.pallas_call(
        pair_product_kernel,
        grid=(rows // block,),
        in_specs=[pl.BlockSpec((block, depth), lambda i: (i, 0)), whole_spec(right.shape)],
        out_specs=[half] * 2,
        out_shape=[jax.ShapeDtypeStruct((rows // 2, width), BF)] * 2,
        compiler_params=pltpu.CompilerParams(vmem_limit_bytes=KERNEL_VMEM),
        cost_estimate=takes("pair_product"),
        name="pair_product",
    )(left, right)


GAIN_ROWS = 32


def last_kernel(
    count,
    n_seq,
    me_ref,
    back_ref,
    latent_ref,
    query_gain_ref,
    x_ref,
    gain_ref,
    cos_ref,
    sin_ref,
    feed_term_ref,
    *refs,
):
    blocks, (load_ref, dx_ref) = refs[:count], refs[count:]
    me = me_ref[0]
    latent_width = latent_ref.shape[1]
    tok_count, first_width = back_ref.shape
    width = x_ref.shape[1]
    size = width // n_seq

    def norm_back(v, e, gain):
        r = lax.rsqrt(jnp.mean(v * v, axis=1, keepdims=True) + EPS)
        u = v * r
        eg = e * gain
        grad = r * (eg - u * jnp.mean(eg * u, axis=1, keepdims=True))
        return grad, jnp.sum(e * u, axis=0, keepdims=True)

    d_latent, query_term = norm_back(
        latent_ref[...], back_ref[:, :latent_width], query_gain_ref[...]
    )
    half = HEAD_DIM // 2
    first_half = back_ref[:, latent_width : latent_width + half]
    second_half = back_ref[:, latent_width + half : latent_width + HEAD_DIM]
    cosine, sine_part = cos_ref[...], sin_ref[...]
    d_first = jnp.concatenate(
        [
            d_latent,
            first_half * cosine + second_half * sine_part,
            second_half * cosine - first_half * sine_part,
            back_ref[:, latent_width + HEAD_DIM :],
        ],
        axis=1,
    ).astype(BF)
    load_ref[:tok_count, :] = d_first
    for piece, here in zip(blocks, piece_slices(blocks), strict=True):
        rows = here.stop - here.start
        place = (me ^ (here.start // size)) * size + here.start % size
        own = pl.ds(pl.multiple_of(place, rows), rows)
        dx_ref[:, own] = dot_rows(d_first, piece[:, :first_width])
    dx_ref[...], gain_term = norm_back(x_ref[...].astype(F32), dx_ref[...], gain_ref[...])
    pad = jnp.zeros((1, 2 * first_width - width), F32)
    rows = [
        gain_term[:, :first_width],
        jnp.concatenate([gain_term[:, first_width:], pad], axis=1),
        feed_term_ref[:, :first_width],
        jnp.concatenate([feed_term_ref[:, first_width:], pad], axis=1),
        jnp.concatenate([query_term, jnp.zeros((1, first_width - latent_width), F32)], axis=1),
        jnp.zeros((GAIN_ROWS - 5, first_width), F32),
    ]
    load_ref[tok_count:, :] = jnp.concatenate(rows, axis=0).astype(BF)


def last_products(me, back, latent, query_gain, x, gain, cosine, sine_part, feed_term, blocks):
    tok_count, width = x.shape
    vmem = pl.BlockSpec(memory_space=pltpu.VMEM)
    return pl.pallas_call(
        functools.partial(last_kernel, len(blocks), lax.axis_size("seq")),
        in_specs=[pl.BlockSpec(memory_space=pltpu.SMEM)] + [vmem] * (8 + len(blocks)),
        out_specs=[vmem] * 2,
        out_shape=[
            jax.ShapeDtypeStruct((tok_count + GAIN_ROWS, back.shape[1]), BF),
            jax.ShapeDtypeStruct((tok_count, width), F32),
        ],
        compiler_params=pltpu.CompilerParams(vmem_limit_bytes=KERNEL_VMEM),
        cost_estimate=takes("last_products"),
        name="last_products",
    )(me, back, latent, query_gain, x, gain, cosine, sine_part, feed_term, *blocks)


def first_grads_kernel(count, n_seq, n_dp, latent_width, me_ref, normed_ref, *refs):
    pieces, (out_ref, d_ref, x_ref) = refs[:count], refs[count:]
    me = me_ref[0]
    tok_count, size = normed_ref.shape[1:]
    first_width = d_ref.shape[1]
    block = tok_count + GAIN_ROWS
    terms = jnp.zeros((8, first_width), F32)
    for piece, here in zip(pieces, piece_slices(pieces), strict=True):
        k, first = here.start // block, here.start % block
        tokens = min(tok_count - first, piece.shape[0])
        d_ref[k * tok_count + first : k * tok_count + first + tokens, :] = piece[:tokens, :]
        if tokens < piece.shape[0]:
            terms = terms + piece[tokens : tokens + 16, :].astype(F32)[:8]
    for k in range(n_seq):
        x_ref[k * tok_count : (k + 1) * tok_count, :] = normed_ref[me ^ k]
    out_ref[:, :first_width] = dot_cols(x_ref[...], d_ref[...]).astype(BF)
    width = size * n_seq
    rest = width - first_width

    def share(row, length):
        own = row[:, :length]
        for k in range(1, n_seq):
            own = jnp.where(me == k, row[:, k * length : (k + 1) * length], own)
        return own

    gain = jnp.concatenate([terms[0:1], terms[1:2, :rest]], axis=1)
    feed = jnp.concatenate([terms[2:3], terms[3:4, :rest]], axis=1)
    query = share(terms[4:5, :latent_width], latent_width // n_seq)
    query = matmul(
        jnp.concatenate([query] * 8, axis=0).astype(BF),
        spread(n_dp, query.shape[1] // n_dp, size // n_dp),
    )[:1]
    rows = [share(gain, size), share(feed, size), query, jnp.zeros((125, size), F32)]
    out_ref[:, first_width:] = jnp.concatenate(rows, axis=0).T.astype(BF)


def first_grads(me, normed, pieces, latent_width):
    n_seq, tok_count, size = normed.shape
    first_width = pieces[0].shape[1]
    vmem = pl.BlockSpec(memory_space=pltpu.VMEM)
    return pl.pallas_call(
        functools.partial(
            first_grads_kernel, len(pieces), n_seq, lax.axis_size("dp"), latent_width
        ),
        in_specs=[pl.BlockSpec(memory_space=pltpu.SMEM)] + [vmem] * (1 + len(pieces)),
        out_specs=vmem,
        out_shape=jax.ShapeDtypeStruct((size, first_width + 128), BF),
        scratch_shapes=[
            pltpu.VMEM((n_seq * tok_count, first_width), BF),
            pltpu.VMEM((n_seq * tok_count, size), BF),
        ],
        compiler_params=pltpu.CompilerParams(vmem_limit_bytes=KERNEL_VMEM),
        cost_estimate=takes("first_grads"),
        name="first_grads",
    )(me, normed, *pieces)


def block_places(shape, axis, core):
    rows = lax.broadcasted_iota(jnp.int32, shape, axis)
    half = shape[axis] // 2
    return rows + core * jnp.where(rows < half, half, -half)


def rotate_heads(values, cosine, sine_part, scale):
    half = HEAD_DIM // 2
    parts = []
    for at in range(0, values.shape[1], HEAD_DIM):
        first_half = values[:, at : at + half]
        second_half = values[:, at + half : at + HEAD_DIM]
        parts.append((first_half * cosine - second_half * sine_part) * scale)
        parts.append((second_half * cosine + first_half * sine_part) * scale)
    return jnp.concatenate(parts, axis=1)


def attend_kernel(
    count,
    heads,
    block,
    me_ref,
    starts_ref,
    cos_ref,
    sin_ref,
    wq_ref,
    wo_ref,
    *refs,
):
    packs = refs[:count]
    lat_ref, k_ref, v_ref, q_ref, mixed_ref, lse_ref, even_ref, odd_ref, vt_ref = refs[count:]
    me = me_ref[0]
    chip, core = me >> 1, me & 1
    index = pl.program_id(0)
    at = index ^ chip
    latent_width = lat_ref.shape[1]

    @pl.when(index == 0)
    def _():
        for pack, here in zip(packs, piece_slices(packs), strict=True):
            lat_ref[here, :] = pack[:, :latent_width]
            k_ref[here, :] = pack[:, latent_width : latent_width + HEAD_DIM]
            v_ref[here, :] = pack[:, latent_width + HEAD_DIM :]
        for j in range(k_ref.shape[0] // block):
            here = slice(j * block, (j + 1) * block)
            vt_ref[:, here] = v_ref[here, :].T

    own = pl.ds(pl.multiple_of(index * block, block), block)
    query_raw = matmul(lat_ref[own, :], wq_ref[...])
    q_ref[...] = rotate_heads(
        query_raw, cos_ref[...], sin_ref[...], HEAD_DIM ** (-0.5)
    ).astype(BF)
    starts_row = starts_ref[...]
    key_place = block_places((block, 1), 0, core)
    query_place = at * block + block_places((1, block), 1, core)
    columns = [slice(h * HEAD_DIM, (h + 1) * HEAD_DIM) for h in range(heads)]

    def step(b, running):
        here = pl.ds(pl.multiple_of((b ^ chip) * block, block), block)
        keys_here = b * block + key_place
        visible = (keys_here <= query_place) & (keys_here >= starts_row)
        result = []
        for head in range(heads):
            running_max, running_sum, total = running[head]
            scores = dot_rows(k_ref[here, :], q_ref[:, columns[head]])
            scores = jnp.where(visible, scores, NEGATIVE)
            new_max = jnp.maximum(running_max, jnp.max(scores, axis=0, keepdims=True))
            factor = jnp.exp(running_max - new_max)
            terms = jnp.where(visible, jnp.exp(scores - new_max), 0.0)
            running_sum = running_sum * factor + jnp.sum(terms, axis=0, keepdims=True)
            total = total * factor + matmul(vt_ref[:, here], terms.astype(BF))
            result.append((new_max, running_sum, total))
        return tuple(result)

    start = (
        jnp.full((1, block), NEGATIVE, F32),
        jnp.zeros((1, block), F32),
        jnp.zeros((HEAD_DIM, block), F32),
    )
    running = lax.fori_loop(0, at + 1, step, (start,) * heads)
    for head in range(heads):
        running_max, running_sum, total = running[head]
        mixed_ref[:, columns[head]] = (total / running_sum).T.astype(BF)
        lse_ref[head : head + 1, :] = running_max + jnp.log(running_sum)
    terms = matmul(mixed_ref[...], wo_ref[...]).astype(BF)
    even_ref[...] = terms[: block // 2]
    odd_ref[...] = terms[block // 2 :]


def attend(me, starts, cosine, sine_part, query_up, output, packs, latent_width, block):
    pack_width = packs[0].shape[1]
    group_len = sum(piece.shape[0] for piece in packs)
    width = query_up.shape[1]
    heads = width // HEAD_DIM
    out_width = output.shape[1]
    tokens = pl.BlockSpec((block, width), lambda i, me: (i, 0))
    half = pl.BlockSpec((block // 2, out_width), lambda i, me: (i, 0))
    angle = pl.BlockSpec((block, HEAD_DIM // 2), lambda i, me: (i, 0))
    lanes = pl.BlockSpec((heads, block), lambda i, me: (0, i))
    shape = jax.ShapeDtypeStruct
    return pl.pallas_call(
        functools.partial(attend_kernel, len(packs), heads, block),
        grid_spec=pltpu.PrefetchScalarGridSpec(
            num_scalar_prefetch=1,
            grid=(group_len // block,),
            in_specs=[
                pl.BlockSpec((1, block), lambda i, me: (0, i)),
                angle,
                angle,
                whole_spec(query_up.shape),
                whole_spec(output.shape),
            ]
            + [whole_spec(piece.shape) for piece in packs],
            out_specs=[
                whole_spec((group_len, latent_width)),
                whole_spec((group_len, HEAD_DIM)),
                whole_spec((group_len, HEAD_DIM)),
                tokens,
                tokens,
                lanes,
                half,
                half,
            ],
            scratch_shapes=[pltpu.VMEM((HEAD_DIM, group_len), BF)],
        ),
        out_shape=[
            shape((group_len, latent_width), BF),
            shape((group_len, HEAD_DIM), BF),
            shape((group_len, HEAD_DIM), BF),
            shape((group_len, width), BF),
            shape((group_len, width), BF),
            shape((heads, group_len), F32),
            shape((group_len // 2, out_width), BF),
            shape((group_len // 2, out_width), BF),
        ],
        compiler_params=pltpu.CompilerParams(vmem_limit_bytes=KERNEL_VMEM),
        cost_estimate=takes("attend"),
        name="attend",
    )(me, starts, cosine, sine_part, query_up, output, *packs)


def attend_back_kernel(
    count,
    heads,
    block,
    me_ref,
    starts_ref,
    cos_ref,
    sin_ref,
    q_ref,
    mixed_ref,
    lse_ref,
    k_ref,
    v_ref,
    wq_ref,
    wo_ref,
    *refs,
):
    blocks = refs[:count]
    d_ref, dq_ref, even_ref, odd_ref, dk_ref, dv_ref = refs[count:]
    me = me_ref[0]
    chip, core = me >> 1, me & 1
    index = pl.program_id(0)
    at = index ^ chip
    half = block // 2
    latent_width = wq_ref.shape[0]

    @pl.when(index == 0)
    def _():
        for source, here in zip(blocks, piece_slices(blocks), strict=True):
            d_ref[here, :] = source[...]
        dk_ref[...] = jnp.zeros_like(dk_ref)
        dv_ref[...] = jnp.zeros_like(dv_ref)

    own = pl.ds(pl.multiple_of(index * block, block), block)
    d_mixed = dot_rows(d_ref[own, :], wo_ref[...]).astype(BF)
    starts_row = starts_ref[...]
    key_place = block_places((block, 1), 0, core)
    query_place = at * block + block_places((1, block), 1, core)
    columns = [slice(h * HEAD_DIM, (h + 1) * HEAD_DIM) for h in range(heads)]
    offsets = [
        jnp.sum(
            (d_mixed[:, cols].astype(F32) * mixed_ref[:, cols].astype(F32)).T,
            axis=0,
            keepdims=True,
        )
        for cols in columns
    ]

    def step(b, running):
        here = pl.ds(pl.multiple_of((b ^ chip) * block, block), block)
        keys_here = b * block + key_place
        visible = (keys_here <= query_place) & (keys_here >= starts_row)
        keys, values = k_ref[here, :], v_ref[here, :]
        result = []
        for head in range(heads):
            q, dm = q_ref[:, columns[head]], d_mixed[:, columns[head]]
            scores = dot_rows(keys, q)
            scores = jnp.where(visible, scores, NEGATIVE)
            probs = jnp.where(visible, jnp.exp(scores - lse_ref[head : head + 1, :]), 0.0)
            d_probs = dot_rows(values, dm)
            d_scores = (probs * (d_probs - offsets[head])).astype(BF)
            dv_ref[here, :] += matmul(probs.astype(BF), dm)
            dk_ref[here, :] += matmul(d_scores, q)
            result.append(running[head] + dot_cols(d_scores, keys))
        return tuple(result)

    start = (jnp.zeros((block, HEAD_DIM), F32),) * heads
    d_queries = jnp.concatenate(lax.fori_loop(0, at + 1, step, start), axis=1)
    dq_ref[...] = rotate_heads(
        d_queries, cos_ref[...], -sin_ref[...], HEAD_DIM ** (-0.5)
    ).astype(BF)
    terms = dot_rows(dq_ref[...], wq_ref[...]).astype(BF)
    rows_here = pl.ds(pl.multiple_of(index * half, half), half)
    even_ref[rows_here, :latent_width] = terms[:half]
    odd_ref[rows_here, :latent_width] = terms[half:]

    @pl.when(index == pl.num_programs(0) - 1)
    def _():
        for j in range(k_ref.shape[0] // block):
            to = slice(j * half, (j + 1) * half)
            for target, first in ((even_ref, j * block), (odd_ref, j * block + half)):
                rows = slice(first, first + half)
                target[to, latent_width : latent_width + HEAD_DIM] = dk_ref[rows, :].astype(BF)
                target[to, latent_width + HEAD_DIM :] = dv_ref[rows, :].astype(BF)


def attend_back(
    me, starts, cosine, sine_part, queries, mixed, lse, keys, values, query_up, output, blocks, block
):
    group_len, width = queries.shape
    heads = width // HEAD_DIM
    out_width = blocks[0].shape[1]
    latent_width = query_up.shape[0]
    pack_width = latent_width + 2 * HEAD_DIM
    tokens = pl.BlockSpec((block, width), lambda i, me: (i, 0))
    angle = pl.BlockSpec((block, HEAD_DIM // 2), lambda i, me: (i, 0))
    lanes = pl.BlockSpec((heads, block), lambda i, me: (0, i))
    half = (group_len // 2, pack_width)
    shape = jax.ShapeDtypeStruct
    return pl.pallas_call(
        functools.partial(attend_back_kernel, len(blocks), heads, block),
        grid_spec=pltpu.PrefetchScalarGridSpec(
            num_scalar_prefetch=1,
            grid=(group_len // block,),
            in_specs=[
                pl.BlockSpec((1, block), lambda i, me: (0, i)),
                angle,
                angle,
                tokens,
                tokens,
                lanes,
                whole_spec(keys.shape),
                whole_spec(values.shape),
                whole_spec(query_up.shape),
                whole_spec(output.shape),
            ]
            + [whole_spec(piece.shape) for piece in blocks],
            out_specs=[
                whole_spec((group_len, out_width)),
                tokens,
                whole_spec(half),
                whole_spec(half),
            ],
            scratch_shapes=[pltpu.VMEM((group_len, HEAD_DIM), F32)] * 2,
        ),
        out_shape=[
            shape((group_len, out_width), BF),
            shape((group_len, width), BF),
            shape(half, BF),
            shape(half, BF),
        ],
        compiler_params=pltpu.CompilerParams(vmem_limit_bytes=KERNEL_VMEM),
        cost_estimate=takes("attend_back"),
        name="attend_back",
    )(
        me,
        starts,
        cosine,
        sine_part,
        queries,
        mixed,
        lse,
        keys,
        values,
        query_up,
        output,
        *blocks,
    )


def attention_grads_kernel(n_dp, query_rows, mixed_ref, latent_ref, dq_ref, d_ref, out_ref):
    out_rows = mixed_ref.shape[1] // n_dp
    output_terms = dot_cols(mixed_ref[...], d_ref[...]).astype(BF)
    query_terms = dot_cols(latent_ref[...], dq_ref[...])
    for z in range(n_dp):
        out_ref[z, :out_rows, :] = output_terms[z * out_rows : (z + 1) * out_rows]
        parts = [
            query_terms[first : first + query_rows]
            for first in range(z * query_rows, query_terms.shape[0], n_dp * query_rows)
        ]
        out_ref[z, out_rows:, :] = jnp.concatenate(parts, axis=0).astype(BF)


def attention_grads(mixed, latent, d_query, d_branch, n_dp, query_rows):
    group_len, width = d_branch.shape
    heads_width = mixed.shape[1]
    sets = width // heads_width
    part = latent.shape[1] // sets
    rows = heads_width // n_dp + part // n_dp
    return pl.pallas_call(
        functools.partial(attention_grads_kernel, n_dp, query_rows),
        grid=(sets,),
        in_specs=[
            whole_spec(mixed.shape),
            pl.BlockSpec((group_len, part), lambda j: (0, j)),
            whole_spec(d_query.shape),
            pl.BlockSpec((group_len, heads_width), lambda j: (0, j)),
        ],
        out_specs=pl.BlockSpec((n_dp, rows, heads_width), lambda j: (0, 0, j)),
        out_shape=jax.ShapeDtypeStruct((n_dp, rows, width), BF),
        compiler_params=pltpu.CompilerParams(vmem_limit_bytes=KERNEL_VMEM),
        cost_estimate=takes("attention_grads"),
        name="attention_grads",
    )(mixed, latent, d_query, d_branch)


def columns_back_kernel(parts_ref, *targets):
    for which, target in enumerate(targets):
        parts = [parts_ref[k, which].astype(F32) for k in range(parts_ref.shape[0])]
        target[...] = jnp.concatenate(parts, axis=1)


def columns_back(parts):
    n_seq, kinds, rows, columns = parts.shape
    vmem = pl.BlockSpec(memory_space=pltpu.VMEM)
    return pl.pallas_call(
        columns_back_kernel,
        in_specs=[vmem],
        out_specs=[vmem] * kinds,
        out_shape=[jax.ShapeDtypeStruct((rows, n_seq * columns), F32)] * kinds,
        compiler_params=pltpu.CompilerParams(vmem_limit_bytes=KERNEL_VMEM),
        cost_estimate=takes("columns_back"),
        name="columns_back",
    )(parts)


def local(
    layer_input,
    doc_lengths,
    attention_gain,
    query_down,
    query_gain,
    query_up,
    keyvalue_weight,
    output_weight,
    feedforward_gain,
    gate_weight,
    up_weight,
    down_weight,
    cotangent,
):
    n_seq, n_dp = lax.axis_size("seq"), lax.axis_size("dp")
    me = lax.axis_index("seq")
    input_low = layer_input[0]
    tokens = input_low.astype(F32)
    tok_count, width = tokens.shape
    latent_width = query_down.shape[1]
    group_len = tok_count * n_seq
    heads = HEADS // n_seq
    hidden_units = gate_weight.shape[1] // n_seq

    starts_all, position_all = document_starts(doc_lengths[0], group_len)
    starts_all = relative(starts_all, 0)
    position_all = relative(position_all, 0)
    cosine_all, sine_all = rope_tables(position_all, HEAD_DIM)
    me_array = me.astype(jnp.int32).reshape(1)

    own_rows = query_down.shape[0]
    query_rows = query_gain.shape[0]
    gains = jnp.stack(
        [attention_gain, feedforward_gain, jnp.pad(query_gain, (0, own_rows - query_rows))], axis=1
    )
    first_set = jnp.concatenate(
        [query_down, keyvalue_weight, jnp.pad(gains, ((0, 0), (0, 125)))], axis=1
    )
    chain = Chain()
    block = 2 * tok_count
    half_chips = n_seq // 4
    first_width = latent_width + 2 * HEAD_DIM
    out_rows = output_weight.shape[0]

    chain.add(tables=(cosine_all, sine_all, starts_all.reshape(1, group_len)))
    first_set, query_up = together(first_set, query_up)
    chain.add(query_part=exchange(split_columns(query_up)))
    chain.add(feed_step=gather_near(cotangent[0]))
    first_part = chain.stage(FIRST_PART, gather_dp_steps(first_set))
    query_part = chain.query_part.reshape(-1, query_up.shape[1] // n_seq)
    fold = query_part.shape[0] * query_part.shape[1] // width
    attention_set = jnp.concatenate([output_weight, query_part.reshape(fold, width)], axis=0)
    chain.add(attention=gather_dp(chain.begin(attention=attention_set)))
    chain.add(gate_up_parts=jnp.stack([split_columns(gate_weight), split_columns(up_weight)], axis=1),
    )
    near = chain.stage(FIRST_NEAR, gather_near(first_part))
    far = chain.stage(FIRST_FAR, gather_far(near))
    chain.add(gate_up=exchange(chain.begin(gate_up=chain.gate_up_parts)))
    first_blocks = chain.stage(FIRST_BLOCKS, gather_cores(far))
    cosine_all, sine_all, starts_all = chain.tables
    cosine, sine_part = cosine_all[:tok_count], sine_all[:tok_count]
    pack, latent, normed_parts, attention_gain_row, feed_gain_row, query_gain_row = first_projections(
        me_array, input_low, cosine, sine_part, first_blocks, latent_width
    )
    feed_gain_f = feed_gain_row[0]
    pack = chain.stage(PACK, pack)
    attention_part = chain.attention.reshape(n_dp, -1, width)
    full_output = attention_part[:, :out_rows].reshape(-1, width)
    full_query_up = rows_in_order(
        attention_part[:, out_rows:].reshape(-1, query_part.shape[1]), query_up.shape[0]
    )
    chain.add(attention_weights=(full_output, full_query_up))
    near = chain.stage(PACK_NEAR, gather_near(pack))
    gate_up = chain.gate_up
    chain.add(gate_up_all=gather_dp(gate_up.reshape(-1, hidden_units)).reshape(n_dp, *gate_up.shape),
    )
    chain.add(down_all=gather_dp(down_weight))
    packs = chain.stage(PACKS, gather_cores(gather_far(near)))
    full_output, full_query_up = chain.attention_weights
    chain.add(feed_far=gather_far(chain.begin(feed_far=chain.feed_step)))
    latent_all, keys, values, queries, mixed_low, lse, out_even, out_odd = attend(
        me_array,
        starts_all,
        cosine_all,
        sine_all,
        full_query_up,
        full_output,
        packs,
        latent_width,
        block,
    )
    out_even, out_odd = chain.stage(ATTENDED, (out_even, out_odd))
    feed_pieces = gather_cores(chain.feed_far)
    out_left = chain.stage(OUT_LEFT, scatter_relay(chip_sums(out_even, out_odd, n_seq // 2))
    )
    hidden = chain.stage(HIDDEN, tokens + scatter_last(out_left))

    chain.add(feed_stack=stack_blocks(chain.begin(feed_stack=feed_pieces)))
    feed_low = rms_norm(hidden, feed_gain_f).astype(BF)
    near = chain.stage(FEED_NEAR, gather_near(feed_low))
    feed_blocks = chain.stage(FEED_BLOCKS, gather_cores(gather_far(near)))
    chain.add(normed_columns=exchange(chain.begin(normed_columns=normed_parts)))
    feed, active_low, silu_low, slope_low, gate_ordered, up_ordered = feed_forward(
        feed_blocks, chain.gate_up_all, block
    )
    chain.add(grad_down_term=dot_cols(active_low, chain.feed_stack).astype(BF))
    silu_low = chain.stage(ACTIVE, silu_low)
    d_feed = chain.feed_stack
    chain.add(grad_down=scatter_dp(chain.grad_down_term))
    weights = (gate_ordered, up_ordered, chain.down_all)
    dg_high, du_high, even_high, odd_high = feed_back(
        d_feed, silu_low, slope_low, *weights, block, half_chips, half_chips
    )
    even_high, odd_high = chain.stage(TERMS_HIGH, (even_high, odd_high))
    chain.add(high_swap=flip(odd_high, 1))
    dg_low, du_low, *terms_low = feed_back(
        d_feed, after(silu_low, odd_high), slope_low, *weights, block, 0, half_chips
    )
    terms_low = chain.stage(TERMS_LOW, terms_low)
    feed_sums = chip_sums(*terms_low, half_chips) + split_chips(
        plus(even_high, chain.high_swap), half_chips
    )
    feed_sums = chain.stage(FEED_SUMS, feed_sums)
    feed_left = chain.stage(FEED_LEFT, scatter_relay(feed_sums))
    chain.add(grad_gate_up_term=gate_up_grad(
            chain.begin(grad_gate_up_term=feed),
            (dg_low, du_low),
            (dg_high, du_high),
            n_dp,
            n_seq,
        ),
    )
    d_feed_normed = chain.stage(D_NORMED, scatter_last(feed_left))
    chain.add(grad_gate_up=scatter_dp(chain.grad_gate_up_term.reshape(-1, hidden_units)))

    d_result = cotangent[0].astype(F32)
    d_hidden_norm, grad_feed_gain_term = jax.vjp(rms_norm, hidden, feed_gain_f)[1](d_feed_normed)
    d_hidden = d_result + d_hidden_norm
    chain.add(result_terms=pair_product(chain.begin(result_terms=active_low), chain.down_all, block),
    )
    near = chain.stage(BRANCH_NEAR, gather_near(d_hidden.astype(BF)))
    chain.add(result_sums=chip_sums(*chain.result_terms, n_seq // 2))
    d_branch_blocks = gather_cores(gather_far(near))
    d_branch_blocks, feed_gain_term = chain.stage(BRANCH_BLOCKS, (d_branch_blocks, grad_feed_gain_term.reshape(1, -1))
    )
    chain.add(result_left=scatter_relay(chain.begin(result_left=chain.result_sums)))
    d_branch_blocks = chain.stage(BRANCH_ALL, d_branch_blocks)
    result_left = chain.result_left
    chain.add(result_hops=last_hops(result_left))
    d_branch, d_query_low, back_even, back_odd = attend_back(
        me_array,
        starts_all,
        cosine_all,
        sine_all,
        queries,
        mixed_low,
        lse,
        keys,
        values,
        full_query_up,
        full_output,
        d_branch_blocks,
        block,
    )
    back_even, back_odd = chain.stage(BACK_TERMS, (back_even, back_odd))
    back_sums = chain.stage(BACK_SUMS, chip_sums(back_even, back_odd, n_seq // 2))
    d_branch, latent_all = chain.begin(grad_attention_term=(d_branch, latent_all))
    chain.add(grad_attention_term=attention_grads(mixed_low, latent_all, d_query_low, d_branch, n_dp, query_rows),
    )
    back_left = chain.stage(BACK_LEFT, scatter_relay(back_sums))
    back_local = chain.stage(BACK_LOCAL, scatter_last(back_left))
    chain.add(grad_attention=scatter_dp(chain.grad_attention_term.reshape(-1, width)))
    load, d_tokens = last_products(
        me_array,
        back_local,
        latent,
        query_gain_row,
        input_low,
        attention_gain_row,
        cosine,
        sine_part,
        feed_gain_term,
        first_blocks,
    )
    load = chain.stage(FIRST_TERMS, load)
    near = chain.stage(LAST_NEAR, gather_near(load))
    d_tokens = after(d_tokens, load)
    input_grad = (d_hidden + d_tokens)[None]
    chain.add(input_grad=input_grad)
    loads = chain.stage(LAST_BLOCKS, gather_cores(gather_far(near)))
    first_sum = chain.stage(FIRST_SUM, first_grads(me_array, chain.normed_columns, loads, latent_width)
    )
    gate_up_rows = chain.begin(gate_up_rows=chain.grad_gate_up)
    gate_up_rows = exchange(gate_up_rows.reshape(n_seq, 2, own_rows, -1))
    grad_first = scatter_dp(first_sum).astype(F32)
    result = hidden + hops_sum(result_left, chain.begin(result_last=chain.result_hops))
    layer_output = result.astype(BF)[None]

    grad_down = chain.grad_down
    grad_attention = chain.grad_attention
    grad_output_weight = grad_attention[:out_rows].astype(F32)
    grad_query_up = grad_attention[out_rows:].reshape(fold, -1, heads * HEAD_DIM)
    grad_query_up = grad_query_up.transpose(1, 0, 2).reshape(n_seq, query_rows, -1)
    grad_query_up = exchange(after(grad_query_up, gate_up_rows))
    grad_query_up = grad_query_up.transpose(1, 0, 2).reshape(query_rows, -1).astype(F32)

    grad_gate, grad_up = columns_back(gate_up_rows)
    return (
        layer_output,
        input_grad,
        grad_first[:, first_width],
        grad_first[:, :latent_width],
        grad_first[:query_rows, first_width + 2],
        grad_query_up,
        grad_first[:, latent_width:first_width],
        grad_output_weight,
        grad_first[:, first_width + 1],
        grad_gate,
        grad_up,
        grad_down.astype(F32),
    )


def solution(mesh):
    shards = P(("seq", "dp"))
    tokens = P("dp", "seq", None)
    weight = P(("seq", "dp"), None)
    return jax.shard_map(
        local,
        mesh=mesh,
        in_specs=(
            tokens,
            P("dp", None),
            shards,
            weight,
            shards,
            weight,
            weight,
            weight,
            shards,
            weight,
            weight,
            weight,
            tokens,
        ),
        out_specs=(
            tokens,
            tokens,
            shards,
            weight,
            shards,
            weight,
            weight,
            weight,
            shards,
            weight,
            weight,
            weight,
        ),
        check_vma=False,
    )
```

```python
import functools

import jax
import jax.numpy as jnp
from jax import lax
from jax.experimental import pallas as pl
from jax.experimental.pallas import tpu as pltpu
from jax.sharding import PartitionSpec as P

HEADS = 16
HEAD_DIM = 256


EPS = 1e-05
ROPE_BASE = 10000.0
NEGATIVE = -1e30
BF = jnp.bfloat16
F32 = jnp.float32
KERNEL_VMEM = 60 * 2**20


KERNEL_COST = dict(
    stack_blocks=0.01,
    first_projections=0.01,
    attend=0.01,
    feed_forward=0.01,
    feed_back=0.01,
    gate_up_grad=0.01,
    pair_product=3,
    attend_back=0.01,
    last_products=0.01,
    first_grads=0.01,
    columns_back=0.01,
    attention_grads=0.01,
)
(
    FIRST_PART,
    FIRST_NEAR,
    FIRST_FAR,
    FIRST_BLOCKS,
    PACK,
    PACK_NEAR,
    PACKS,
    ATTENDED,
    OUT_LEFT,
    HIDDEN,
    FEED_NEAR,
    FEED_BLOCKS,
    ACTIVE,
    TERMS_HIGH,
    TERMS_LOW,
    FEED_SUMS,
    FEED_LEFT,
    D_NORMED,
    BRANCH_NEAR,
    BRANCH_BLOCKS,
    BRANCH_ALL,
    BACK_TERMS,
    BACK_SUMS,
    BACK_LEFT,
    BACK_LOCAL,
    FIRST_TERMS,
    LAST_NEAR,
    LAST_BLOCKS,
    FIRST_SUM,
) = range(29)
DUE = dict(
    tables=FIRST_BLOCKS,
    feed_step=FIRST_PART,
    query_part=FIRST_PART,
    gate_up_parts=FIRST_NEAR,
    gate_up=PACK,
    gate_up_all=FEED_NEAR,
    feed_far=ATTENDED,
    feed_stack=FEED_NEAR,
    grad_down_term=ACTIVE,
    down_all=TERMS_HIGH,
    high_swap=TERMS_LOW,
    grad_down=D_NORMED,
    grad_gate_up_term=D_NORMED,
    result_terms=BRANCH_NEAR,
    result_sums=BRANCH_BLOCKS,
    result_left=BACK_TERMS,
    grad_gate_up=BACK_LEFT,
    grad_attention_term=BACK_LEFT,
    grad_attention=FIRST_SUM,
    attention=PACK,
    attention_weights=PACK_NEAR,
    normed_columns=ACTIVE,
    result_hops=BACK_TERMS,
    result_late=FIRST_TERMS,
    layer_output=LAST_NEAR,
    input_grad=LAST_NEAR,
)
BEGIN = dict(
    output=FIRST_PART,
    gate_up=FIRST_FAR,
    feed_far=PACKS,
    grad_gate_up_term=FEED_LEFT,
    result_terms=D_NORMED,
    result_left=BRANCH_NEAR,
    result_last=BACK_LOCAL,
    grad_attention_term=BACK_SUMS,
    normed_columns=FEED_BLOCKS,
    feed_stack=HIDDEN,
    gate_up_rows=FIRST_SUM,
)


def takes(kernel):
    microseconds = KERNEL_COST[kernel]
    return pl.CostEstimate(
        flops=int(microseconds * 1e9), bytes_accessed=int(microseconds * 2e6), transcendentals=0
    )


class Chain:
    def __init__(self):
        self.stages = {}
        self.side = {}

    def add(self, **made):
        self.side.update(made)

    def begin(self, **waiting):
        ((name, value),) = waiting.items()
        return after(value, self.stages[BEGIN[name]]) if name in BEGIN else value

    def stage(self, at, value):
        due = [name for name in self.side if DUE.get(name) == at]
        if due:
            value, there = together(value, [self.side[name] for name in due])
            self.side.update(zip(due, there, strict=True))
        self.stages[at] = value
        return value

    def __getattr__(self, name):
        return self.side[name]


def rms_norm(values, norm_gain):
    return values * lax.rsqrt(jnp.mean(values * values, axis=-1, keepdims=True) + EPS) * norm_gain


def rope_tables(position, feature_width):
    half_width = feature_width // 2
    freqs = ROPE_BASE ** (-jnp.arange(half_width, dtype=F32) * 2.0 / feature_width)
    angles = position.astype(F32)[:, None] * freqs[None, :]
    return (jnp.cos(angles), jnp.sin(angles))


def rotate(values, cosine, sine_part):
    half_width = values.shape[-1] // 2
    first_half = values[..., :half_width]
    second_half = values[..., half_width:]
    return jnp.concatenate(
        [
            first_half * cosine - second_half * sine_part,
            second_half * cosine + first_half * sine_part,
        ],
        axis=-1,
    )


def document_starts(lengths_row, group_len):
    doc_ends = jnp.cumsum(lengths_row)
    places = jnp.arange(group_len, dtype=jnp.int32)
    past_ends = (places[:, None] >= doc_ends[None, :]).astype(jnp.int32)
    starts = jnp.sum(past_ends * lengths_row[None, :], axis=1)
    return (starts, places - starts)


def gated(gate_proj, upward):
    return jax.nn.silu(gate_proj) * upward


def matmul(left_side, right_side):
    return jnp.dot(left_side, right_side, preferred_element_type=F32)


def dot_rows(left_side, right_side):
    return lax.dot_general(
        left_side, right_side, (((1,), (1,)), ((), ())), preferred_element_type=F32
    )


def dot_cols(left_side, right_side):
    return lax.dot_general(
        left_side, right_side, (((0,), (0,)), ((), ())), preferred_element_type=F32
    )


def flip(block, bits):
    n_seq = lax.axis_size("seq")
    return lax.ppermute(block, "seq", [(i, i ^ bits) for i in range(n_seq)])


def gather_near(rows):
    n_seq = lax.axis_size("seq")
    hops = (2, 4) if n_seq == 8 else range(2, n_seq, 2)
    return {0: rows} | {bits: flip(rows, bits) for bits in hops}


def gather_far(blocks):
    if lax.axis_size("seq") != 8:
        return blocks
    half = blocks[0].shape[0] // 2
    return blocks | {6: [flip(blocks[4][:half], 2), flip(blocks[2][half:], 4)]}


def gather_cores(blocks):
    whole = []
    for bits in range(0, lax.axis_size("seq"), 2):
        own = blocks[bits] if isinstance(blocks[bits], list) else [blocks[bits]]
        whole += own + [flip(piece, 1) for piece in own]
    return whole


def piece_slices(pieces):
    slices, first = [], 0
    for piece in pieces:
        slices.append(slice(first, first + piece.shape[0]))
        first += piece.shape[0]
    return slices


def gather_blocks(rows):
    return gather_cores(gather_far(gather_near(rows)))


def together(*values):
    flat, tree = jax.tree.flatten(values)
    return jax.tree.unflatten(tree, lax.optimization_barrier(flat))


def after(values, *first):
    return together(values, *first)[0]


def stack_kernel(count, *refs):
    sources, target, held, arrived, left = refs[:count], *refs[count:]
    moves = []
    for k, (source, rows) in enumerate(zip(sources, piece_slices(sources), strict=True)):
        here = pl.ds(rows.start, rows.stop - rows.start)
        moves.append(
            (
                pltpu.make_async_copy(source, held.at[here], arrived.at[k]),
                pltpu.make_async_copy(held.at[here], target.at[here], left.at[k]),
            )
        )
    for come, _ in moves:
        come.start()
    for come, go in moves:
        come.wait()
        go.start()
    for _, go in moves:
        go.wait()


def stack_blocks(pieces):
    width, dtype = pieces[0].shape[1], pieces[0].dtype
    shape = (sum(piece.shape[0] for piece in pieces), width)
    return pl.pallas_call(
        functools.partial(stack_kernel, len(pieces)),
        in_specs=[pl.BlockSpec(memory_space=pl.ANY)] * len(pieces),
        out_specs=pl.BlockSpec(memory_space=pl.ANY),
        out_shape=jax.ShapeDtypeStruct(shape, dtype),
        scratch_shapes=[pltpu.VMEM(shape, dtype)]
        + [pltpu.SemaphoreType.DMA((len(pieces),))] * 2,
        compiler_params=pltpu.CompilerParams(vmem_limit_bytes=KERNEL_VMEM),
        cost_estimate=takes("stack_blocks"),
        name="stack_blocks",
    )(*pieces)


def plus(first, second):
    return (first.astype(F32) + second.astype(F32)).astype(BF)


def split_chips(total, count):
    rows = total.shape[0] // count
    return [total[k * rows : (k + 1) * rows] for k in range(count)]


def chip_sums(even, odd, count):
    return split_chips(plus(even, flip(odd, 1)), count)


def scatter_relay(sums):
    n_seq = lax.axis_size("seq")
    if n_seq != 8:
        return {k: [part] for k, part in enumerate(sums)}
    half = sums[0].shape[0] // 2
    far_x = flip(sums[3][:half], 2)
    far_y = flip(sums[3][half:], 4)
    return {
        0: [sums[0]],
        1: [sums[1][:half], plus(sums[1][half:], far_y)],
        2: [sums[2][half:], plus(sums[2][:half], far_x)],
    }


def early_hops(left):
    if lax.axis_size("seq") != 8:
        return [flip(parts[0], 2 * k) for k, parts in left.items() if k]
    return [flip(left[1][0], 2), flip(left[2][0], 4)]


def late_hops(left):
    if lax.axis_size("seq") != 8:
        return []
    return [flip(left[1][1], 2), flip(left[2][1], 4)]


def hops_sum(left, hops):
    own = left[0][0].astype(F32)
    if lax.axis_size("seq") != 8:
        return sum((hop.astype(F32) for hop in hops), own)
    x_low, y_high, x_high, y_low = [hop.astype(F32) for hop in hops]
    return own + jnp.concatenate([x_low + y_low, x_high + y_high], axis=0)


def scatter_last(left):
    return hops_sum(left, early_hops(left) + late_hops(left))


def scatter_pairs(even, odd):
    count = lax.axis_size("seq") // 2
    return scatter_last(scatter_relay(chip_sums(even, odd, count)))


def relative(values, axis):
    n_seq, me = lax.axis_size("seq"), lax.axis_index("seq")
    size = values.shape[axis] // n_seq
    parts = [
        lax.dynamic_slice_in_dim(values, (me ^ k) * size, size, axis) for k in range(n_seq)
    ]
    return jnp.concatenate(parts, axis=axis)


def relative_vectors(values):
    n_seq, me = lax.axis_size("seq"), lax.axis_index("seq")
    count, length = values.shape
    values = values.reshape(count, n_seq, length // n_seq)
    bit = 1
    while bit < n_seq:
        pairs = values.reshape(count, n_seq // (2 * bit), 2, bit, length // n_seq)
        swapped = jnp.concatenate([pairs[:, :, 1:], pairs[:, :, :1]], axis=2)
        values = jnp.where((me & bit) != 0, swapped, pairs).reshape(values.shape)
        bit *= 2
    return values.reshape(count, length)


def gather_dp(rows):
    return lax.all_gather(rows, "dp", axis=0, tiled=True)


def gather_dp_steps(rows):
    n_dp, me = lax.axis_size("dp"), lax.axis_index("dp")
    size = rows.shape[0]
    whole = jnp.zeros((n_dp * size, rows.shape[1]), rows.dtype)
    for bits in range(n_dp):
        block = rows
        if bits:
            block = lax.ppermute(rows, "dp", [(i, i ^ bits) for i in range(n_dp)])
        whole = lax.dynamic_update_slice_in_dim(whole, block, (me ^ bits) * size, 0)
    return whole


def scatter_dp(terms):
    return lax.psum_scatter(terms, "dp", scatter_dimension=0, tiled=True)


def split_columns(shard):
    n_seq = lax.axis_size("seq")
    rows, width = shard.shape
    return shard.reshape(rows, n_seq, width // n_seq).transpose(1, 0, 2)


def exchange(parts):
    return lax.all_to_all(parts, "seq", 0, 0)


def rows_in_order(gathered, rows):
    n_seq, n_dp = lax.axis_size("seq"), lax.axis_size("dp")
    width = gathered.shape[-1]
    return gathered.reshape(n_dp, n_seq, rows, width).transpose(1, 0, 2, 3).reshape(-1, width)


def rows_by_dp(terms):
    n_seq, n_dp = lax.axis_size("seq"), lax.axis_size("dp")
    total, width = terms.shape
    rows = total // (n_seq * n_dp)
    return terms.reshape(n_seq, n_dp, rows, width).transpose(1, 0, 2, 3)


def spread(n_dp, own, rows):
    shape = (n_dp * own, n_dp * rows)
    at = lax.broadcasted_iota(jnp.int32, shape, 0)
    to = lax.broadcasted_iota(jnp.int32, shape, 1)
    hit = to == at // own * rows + at % own
    return jnp.where(hit, 1.0, 0.0).astype(BF)


def exchanged_rows(rows, me):
    count = len(rows)
    result = []
    for k in range(count):
        row = rows[0]
        for at in range(1, count):
            row = jnp.where((me ^ k) == at, rows[at], row)
        result.append(row)
    return result


def first_kernel(count, n_seq, n_dp, me_ref, x_ref, cos_ref, sin_ref, *refs):
    pieces = refs[:count]
    pack_ref, latent_ref, parts_ref, gain_ref, feed_gain_ref, query_gain_ref, out_ref = refs[count:]
    me = me_ref[0]
    latent_width = latent_ref.shape[1]
    low_width = pack_ref.shape[1]
    x = x_ref[...].astype(F32)
    scale = lax.rsqrt(jnp.mean(x * x, axis=1, keepdims=True) + EPS)
    size = x_ref.shape[1] // n_seq
    gains = []
    for k, here in enumerate(piece_slices(pieces)):
        gains.append(pieces[k][:, low_width:].astype(F32).T[:8])
        owner, first = me ^ (here.start // size), here.start % size
        rows = here.stop - here.start
        own = pl.ds(pl.multiple_of(owner * size + first, rows), rows)
        normed = (x_ref[:, own].astype(F32) * scale * gains[k][:1]).astype(BF)
        parts_ref[owner, :, first : first + rows] = normed
        gain_ref[:, own] = gains[k][:1]
        feed_gain_ref[:, own] = gains[k][1:2]
        part = matmul(normed, pieces[k][:, :low_width])
        if k == 0:
            out_ref[...] = part
        else:
            out_ref[...] += part
    gains = jnp.concatenate(gains, axis=1)
    own = latent_width // (n_seq * n_dp)
    query_rows = []
    for k in range(n_seq):
        query_rows.append(gains[2:3, k * size : (k + 1) * size])
    query_rows = exchanged_rows(query_rows, me)
    query_rows = dot_rows(
        jnp.concatenate(query_rows, axis=0).astype(BF), spread(n_dp, own, size // n_dp)
    )
    query_gain = jnp.concatenate([query_rows[k : k + 1] for k in range(n_seq)], axis=1)
    query_gain_ref[...] = query_gain
    latent = out_ref[:, :latent_width]
    latent_ref[...] = latent
    latent_scale = lax.rsqrt(jnp.mean(latent * latent, axis=1, keepdims=True) + EPS)
    pack_ref[:, :latent_width] = (latent * latent_scale * query_gain).astype(BF)
    keyvalue = out_ref[:, latent_width:]
    pack_ref[:, latent_width : latent_width + HEAD_DIM] = rotate_heads(
        keyvalue[:, :HEAD_DIM], cos_ref[...], sin_ref[...], 1.0
    ).astype(BF)
    pack_ref[:, latent_width + HEAD_DIM :] = keyvalue[:, HEAD_DIM:].astype(BF)


def first_projections(me, x, cosine, sine_part, pieces, latent_width):
    n_seq = lax.axis_size("seq")
    tok_count, width = x.shape
    low_width = pieces[0].shape[1] - 128
    vmem = pl.BlockSpec(memory_space=pltpu.VMEM)
    shape = jax.ShapeDtypeStruct
    return pl.pallas_call(
        functools.partial(
            first_kernel, len(pieces), lax.axis_size("seq"), lax.axis_size("dp")
        ),
        in_specs=[pl.BlockSpec(memory_space=pltpu.SMEM)] + [vmem] * (3 + len(pieces)),
        out_specs=[vmem] * 6,
        out_shape=[
            shape((tok_count, low_width), BF),
            shape((tok_count, latent_width), F32),
            shape((n_seq, tok_count, width // n_seq), BF),
            shape((1, width), F32),
            shape((1, width), F32),
            shape((1, latent_width), F32),
        ],
        scratch_shapes=[pltpu.VMEM((tok_count, low_width), F32)],
        compiler_params=pltpu.CompilerParams(vmem_limit_bytes=KERNEL_VMEM),
        cost_estimate=takes("first_projections"),
        name="first_projections",
    )(me, x, cosine, sine_part, *pieces)


def weights_in_order(raw_ref, gate_ref, up_ref):
    n_dp, n_seq, _, rows, _ = raw_ref.shape
    for s in range(n_seq):
        for z in range(n_dp):
            here = pl.ds((s * n_dp + z) * rows, rows)
            gate_ref[here, :] = raw_ref[z, s, 0]
            up_ref[here, :] = raw_ref[z, s, 1]


def feed_kernel(count, block, *refs):
    blocks, raw_ref = refs[:count], refs[count]
    x_ref, act_ref, silu_ref, slope_ref, gate_ref, up_ref = refs[count + 1 :]
    at = pl.program_id(0)

    @pl.when(at == 0)
    def _():
        for source, here in zip(blocks, piece_slices(blocks), strict=True):
            x_ref[here, :] = source[...]
        weights_in_order(raw_ref, gate_ref, up_ref)

    x = x_ref[pl.ds(pl.multiple_of(at * block, block), block), :]
    gate = matmul(x, gate_ref[...])
    upward = matmul(x, up_ref[...])
    sigmoid = 1.0 / (1.0 + jnp.exp(-gate))
    silu = gate * sigmoid
    act_ref[...] = (silu * upward).astype(BF)
    silu_ref[...] = silu.astype(BF)
    slope_ref[...] = (upward * (sigmoid + silu * (1.0 - sigmoid))).astype(BF)


def whole_spec(shape):
    return pl.BlockSpec(shape, lambda *_: (0,) * len(shape), pipeline_mode=pl.Buffered(1))


def feed_forward(blocks, raw, block):
    width = blocks[0].shape[1]
    group_len = sum(piece.shape[0] for piece in blocks)
    hidden = raw.shape[-1]
    units = pl.BlockSpec((block, hidden), lambda i: (i, 0))
    weight = jax.ShapeDtypeStruct((width, hidden), BF)
    return pl.pallas_call(
        functools.partial(feed_kernel, len(blocks), block),
        grid=(group_len // block,),
        in_specs=[whole_spec(piece.shape) for piece in blocks] + [whole_spec(raw.shape)],
        out_specs=[whole_spec((group_len, width))]
        + [units] * 3
        + [whole_spec((width, hidden))] * 2,
        out_shape=[jax.ShapeDtypeStruct((group_len, width), BF)]
        + [jax.ShapeDtypeStruct((group_len, hidden), BF)] * 3
        + [weight] * 2,
        compiler_params=pltpu.CompilerParams(vmem_limit_bytes=KERNEL_VMEM),
        cost_estimate=takes("feed_forward"),
        name="feed_forward",
    )(*blocks, raw)


def feed_back_kernel(
    d_ref, silu_ref, slope_ref, gate_ref, up_ref, down_ref, dg_ref, du_ref, even_ref, odd_ref
):
    d_active = dot_rows(d_ref[...], down_ref[...])
    d_gate = (d_active * slope_ref[...].astype(F32)).astype(BF)
    d_up = (d_active * silu_ref[...].astype(F32)).astype(BF)
    dg_ref[...] = d_gate
    du_ref[...] = d_up
    terms = (dot_rows(d_gate, gate_ref[...]) + dot_rows(d_up, up_ref[...])).astype(BF)
    half = terms.shape[0] // 2
    even_ref[...] = terms[:half]
    odd_ref[...] = terms[half:]


def feed_back(d, silu, slope, gate, up, down, block, first, count):
    width, hidden = gate.shape
    tokens = pl.BlockSpec((block, width), lambda i: (i + first, 0))
    units = pl.BlockSpec((block, hidden), lambda i: (i + first, 0))
    half = pl.BlockSpec((block // 2, width), lambda i: (i, 0))
    return pl.pallas_call(
        feed_back_kernel,
        grid=(count,),
        in_specs=[tokens, units, units]
        + [whole_spec(gate.shape), whole_spec(up.shape), whole_spec(down.shape)],
        out_specs=[pl.BlockSpec((block, hidden), lambda i: (i, 0))] * 2 + [half] * 2,
        out_shape=[jax.ShapeDtypeStruct((count * block, hidden), BF)] * 2
        + [jax.ShapeDtypeStruct((count * block // 2, width), BF)] * 2,
        compiler_params=pltpu.CompilerParams(vmem_limit_bytes=KERNEL_VMEM),
        cost_estimate=takes("feed_back"),
        name="feed_back",
    )(d, silu, slope, gate, up, down)


def gate_up_grad_kernel(x_ref, dg_low, du_low, dg_high, du_high, out_ref):
    n_dp, _, _, rows, _ = out_ref.shape
    middle = dg_low.shape[0]
    low, high = x_ref[:middle, :], x_ref[middle:, :]
    for which, (d_low, d_high) in enumerate(((dg_low, dg_high), (du_low, du_high))):
        terms = (dot_cols(low, d_low[...]) + dot_cols(high, d_high[...])).astype(BF)
        for z in range(n_dp):
            out_ref[z, 0, which] = terms[z * rows : (z + 1) * rows]


def gate_up_grad(x, low, high, n_dp, n_seq):
    group_len, width = x.shape
    hidden = low[0].shape[1]
    rows = width // (n_dp * n_seq)
    return pl.pallas_call(
        gate_up_grad_kernel,
        grid=(n_seq,),
        in_specs=[pl.BlockSpec((group_len, n_dp * rows), lambda i: (0, i))]
        + [whole_spec(part.shape) for part in (*low, *high)],
        out_specs=pl.BlockSpec((n_dp, 1, 2, rows, hidden), lambda i: (0, i, 0, 0, 0)),
        out_shape=jax.ShapeDtypeStruct((n_dp, n_seq, 2, rows, hidden), BF),
        compiler_params=pltpu.CompilerParams(vmem_limit_bytes=KERNEL_VMEM),
        cost_estimate=takes("gate_up_grad"),
        name="gate_up_grad",
    )(x, *low, *high)


def pair_product_kernel(left_ref, right_ref, even_ref, odd_ref):
    terms = matmul(left_ref[...], right_ref[...]).astype(BF)
    half = terms.shape[0] // 2
    even_ref[...] = terms[:half]
    odd_ref[...] = terms[half:]


def pair_product(left, right, block):
    rows, depth = left.shape
    width = right.shape[1]
    half = pl.BlockSpec((block // 2, width), lambda i: (i, 0))
    return pl.pallas_call(
        pair_product_kernel,
        grid=(rows // block,),
        in_specs=[pl.BlockSpec((block, depth), lambda i: (i, 0)), whole_spec(right.shape)],
        out_specs=[half] * 2,
        out_shape=[jax.ShapeDtypeStruct((rows // 2, width), BF)] * 2,
        compiler_params=pltpu.CompilerParams(vmem_limit_bytes=KERNEL_VMEM),
        cost_estimate=takes("pair_product"),
        name="pair_product",
    )(left, right)


GAIN_ROWS = 32


def last_kernel(
    count,
    n_seq,
    me_ref,
    back_ref,
    latent_ref,
    query_gain_ref,
    x_ref,
    gain_ref,
    cos_ref,
    sin_ref,
    feed_term_ref,
    *refs,
):
    blocks, (load_ref, dx_ref) = refs[:count], refs[count:]
    me = me_ref[0]
    latent_width = latent_ref.shape[1]
    tok_count, first_width = back_ref.shape
    width = x_ref.shape[1]
    size = width // n_seq

    def norm_back(v, e, gain):
        r = lax.rsqrt(jnp.mean(v * v, axis=1, keepdims=True) + EPS)
        u = v * r
        eg = e * gain
        grad = r * (eg - u * jnp.mean(eg * u, axis=1, keepdims=True))
        return grad, jnp.sum(e * u, axis=0, keepdims=True)

    d_latent, query_term = norm_back(
        latent_ref[...], back_ref[:, :latent_width], query_gain_ref[...]
    )
    half = HEAD_DIM // 2
    first_half = back_ref[:, latent_width : latent_width + half]
    second_half = back_ref[:, latent_width + half : latent_width + HEAD_DIM]
    cosine, sine_part = cos_ref[...], sin_ref[...]
    d_first = jnp.concatenate(
        [
            d_latent,
            first_half * cosine + second_half * sine_part,
            second_half * cosine - first_half * sine_part,
            back_ref[:, latent_width + HEAD_DIM :],
        ],
        axis=1,
    ).astype(BF)
    load_ref[:tok_count, :] = d_first
    for piece, here in zip(blocks, piece_slices(blocks), strict=True):
        rows = here.stop - here.start
        place = (me ^ (here.start // size)) * size + here.start % size
        own = pl.ds(pl.multiple_of(place, rows), rows)
        dx_ref[:, own] = dot_rows(d_first, piece[:, :first_width])
    dx_ref[...], gain_term = norm_back(x_ref[...].astype(F32), dx_ref[...], gain_ref[...])
    pad = jnp.zeros((1, 2 * first_width - width), F32)
    rows = [
        gain_term[:, :first_width],
        jnp.concatenate([gain_term[:, first_width:], pad], axis=1),
        feed_term_ref[:, :first_width],
        jnp.concatenate([feed_term_ref[:, first_width:], pad], axis=1),
        jnp.concatenate([query_term, jnp.zeros((1, first_width - latent_width), F32)], axis=1),
        jnp.zeros((GAIN_ROWS - 5, first_width), F32),
    ]
    load_ref[tok_count:, :] = jnp.concatenate(rows, axis=0).astype(BF)


def last_products(me, back, latent, query_gain, x, gain, cosine, sine_part, feed_term, blocks):
    tok_count, width = x.shape
    vmem = pl.BlockSpec(memory_space=pltpu.VMEM)
    return pl.pallas_call(
        functools.partial(last_kernel, len(blocks), lax.axis_size("seq")),
        in_specs=[pl.BlockSpec(memory_space=pltpu.SMEM)] + [vmem] * (8 + len(blocks)),
        out_specs=[vmem] * 2,
        out_shape=[
            jax.ShapeDtypeStruct((tok_count + GAIN_ROWS, back.shape[1]), BF),
            jax.ShapeDtypeStruct((tok_count, width), F32),
        ],
        compiler_params=pltpu.CompilerParams(vmem_limit_bytes=KERNEL_VMEM),
        cost_estimate=takes("last_products"),
        name="last_products",
    )(me, back, latent, query_gain, x, gain, cosine, sine_part, feed_term, *blocks)


def first_grads_kernel(count, n_seq, n_dp, latent_width, me_ref, normed_ref, *refs):
    pieces, (out_ref, d_ref, x_ref) = refs[:count], refs[count:]
    me = me_ref[0]
    tok_count, size = normed_ref.shape[1:]
    first_width = d_ref.shape[1]
    block = tok_count + GAIN_ROWS
    terms = jnp.zeros((8, first_width), F32)
    for piece, here in zip(pieces, piece_slices(pieces), strict=True):
        k, first = here.start // block, here.start % block
        tokens = min(tok_count - first, piece.shape[0])
        d_ref[k * tok_count + first : k * tok_count + first + tokens, :] = piece[:tokens, :]
        if tokens < piece.shape[0]:
            terms = terms + piece[tokens : tokens + 16, :].astype(F32)[:8]
    for k in range(n_seq):
        x_ref[k * tok_count : (k + 1) * tok_count, :] = normed_ref[me ^ k]
    out_ref[:, :first_width] = dot_cols(x_ref[...], d_ref[...]).astype(BF)
    width = size * n_seq
    rest = width - first_width

    def share(row, length):
        own = row[:, :length]
        for k in range(1, n_seq):
            own = jnp.where(me == k, row[:, k * length : (k + 1) * length], own)
        return own

    gain = jnp.concatenate([terms[0:1], terms[1:2, :rest]], axis=1)
    feed = jnp.concatenate([terms[2:3], terms[3:4, :rest]], axis=1)
    query = share(terms[4:5, :latent_width], latent_width // n_seq)
    query = matmul(
        jnp.concatenate([query] * 8, axis=0).astype(BF),
        spread(n_dp, query.shape[1] // n_dp, size // n_dp),
    )[:1]
    rows = [share(gain, size), share(feed, size), query, jnp.zeros((125, size), F32)]
    out_ref[:, first_width:] = jnp.concatenate(rows, axis=0).T.astype(BF)


def first_grads(me, normed, pieces, latent_width):
    n_seq, tok_count, size = normed.shape
    first_width = pieces[0].shape[1]
    vmem = pl.BlockSpec(memory_space=pltpu.VMEM)
    return pl.pallas_call(
        functools.partial(
            first_grads_kernel, len(pieces), n_seq, lax.axis_size("dp"), latent_width
        ),
        in_specs=[pl.BlockSpec(memory_space=pltpu.SMEM)] + [vmem] * (1 + len(pieces)),
        out_specs=vmem,
        out_shape=jax.ShapeDtypeStruct((size, first_width + 128), BF),
        scratch_shapes=[
            pltpu.VMEM((n_seq * tok_count, first_width), BF),
            pltpu.VMEM((n_seq * tok_count, size), BF),
        ],
        compiler_params=pltpu.CompilerParams(vmem_limit_bytes=KERNEL_VMEM),
        cost_estimate=takes("first_grads"),
        name="first_grads",
    )(me, normed, *pieces)


def block_places(shape, axis, core):
    rows = lax.broadcasted_iota(jnp.int32, shape, axis)
    half = shape[axis] // 2
    return rows + core * jnp.where(rows < half, half, -half)


def rotate_heads(values, cosine, sine_part, scale):
    half = HEAD_DIM // 2
    parts = []
    for at in range(0, values.shape[1], HEAD_DIM):
        first_half = values[:, at : at + half]
        second_half = values[:, at + half : at + HEAD_DIM]
        parts.append((first_half * cosine - second_half * sine_part) * scale)
        parts.append((second_half * cosine + first_half * sine_part) * scale)
    return jnp.concatenate(parts, axis=1)


def attend_kernel(
    count,
    heads,
    block,
    me_ref,
    starts_ref,
    cos_ref,
    sin_ref,
    wq_ref,
    wo_ref,
    *refs,
):
    packs = refs[:count]
    lat_ref, k_ref, v_ref, q_ref, mixed_ref, lse_ref, even_ref, odd_ref, vt_ref = refs[count:]
    me = me_ref[0]
    chip, core = me >> 1, me & 1
    index = pl.program_id(0)
    at = index ^ chip
    latent_width = lat_ref.shape[1]

    @pl.when(index == 0)
    def _():
        for pack, here in zip(packs, piece_slices(packs), strict=True):
            lat_ref[here, :] = pack[:, :latent_width]
            k_ref[here, :] = pack[:, latent_width : latent_width + HEAD_DIM]
            v_ref[here, :] = pack[:, latent_width + HEAD_DIM :]
        for j in range(k_ref.shape[0] // block):
            here = slice(j * block, (j + 1) * block)
            vt_ref[:, here] = v_ref[here, :].T

    own = pl.ds(pl.multiple_of(index * block, block), block)
    query_raw = matmul(lat_ref[own, :], wq_ref[...])
    q_ref[...] = rotate_heads(
        query_raw, cos_ref[...], sin_ref[...], HEAD_DIM ** (-0.5)
    ).astype(BF)
    starts_row = starts_ref[...]
    key_place = block_places((block, 1), 0, core)
    query_place = at * block + block_places((1, block), 1, core)
    columns = [slice(h * HEAD_DIM, (h + 1) * HEAD_DIM) for h in range(heads)]

    def step(b, running):
        here = pl.ds(pl.multiple_of((b ^ chip) * block, block), block)
        keys_here = b * block + key_place
        visible = (keys_here <= query_place) & (keys_here >= starts_row)
        result = []
        for head in range(heads):
            running_max, running_sum, total = running[head]
            scores = dot_rows(k_ref[here, :], q_ref[:, columns[head]])
            scores = jnp.where(visible, scores, NEGATIVE)
            new_max = jnp.maximum(running_max, jnp.max(scores, axis=0, keepdims=True))
            factor = jnp.exp(running_max - new_max)
            terms = jnp.where(visible, jnp.exp(scores - new_max), 0.0)
            running_sum = running_sum * factor + jnp.sum(terms, axis=0, keepdims=True)
            total = total * factor + matmul(vt_ref[:, here], terms.astype(BF))
            result.append((new_max, running_sum, total))
        return tuple(result)

    start = (
        jnp.full((1, block), NEGATIVE, F32),
        jnp.zeros((1, block), F32),
        jnp.zeros((HEAD_DIM, block), F32),
    )
    running = lax.fori_loop(0, at + 1, step, (start,) * heads)
    for head in range(heads):
        running_max, running_sum, total = running[head]
        mixed_ref[:, columns[head]] = (total / running_sum).T.astype(BF)
        lse_ref[head : head + 1, :] = running_max + jnp.log(running_sum)
    terms = matmul(mixed_ref[...], wo_ref[...]).astype(BF)
    even_ref[...] = terms[: block // 2]
    odd_ref[...] = terms[block // 2 :]


def attend(me, starts, cosine, sine_part, query_up, output, packs, latent_width, block):
    pack_width = packs[0].shape[1]
    group_len = sum(piece.shape[0] for piece in packs)
    width = query_up.shape[1]
    heads = width // HEAD_DIM
    out_width = output.shape[1]
    tokens = pl.BlockSpec((block, width), lambda i, me: (i, 0))
    half = pl.BlockSpec((block // 2, out_width), lambda i, me: (i, 0))
    angle = pl.BlockSpec((block, HEAD_DIM // 2), lambda i, me: (i, 0))
    lanes = pl.BlockSpec((heads, block), lambda i, me: (0, i))
    shape = jax.ShapeDtypeStruct
    return pl.pallas_call(
        functools.partial(attend_kernel, len(packs), heads, block),
        grid_spec=pltpu.PrefetchScalarGridSpec(
            num_scalar_prefetch=1,
            grid=(group_len // block,),
            in_specs=[
                pl.BlockSpec((1, block), lambda i, me: (0, i)),
                angle,
                angle,
                whole_spec(query_up.shape),
                whole_spec(output.shape),
            ]
            + [whole_spec(piece.shape) for piece in packs],
            out_specs=[
                whole_spec((group_len, latent_width)),
                whole_spec((group_len, HEAD_DIM)),
                whole_spec((group_len, HEAD_DIM)),
                tokens,
                tokens,
                lanes,
                half,
                half,
            ],
            scratch_shapes=[pltpu.VMEM((HEAD_DIM, group_len), BF)],
        ),
        out_shape=[
            shape((group_len, latent_width), BF),
            shape((group_len, HEAD_DIM), BF),
            shape((group_len, HEAD_DIM), BF),
            shape((group_len, width), BF),
            shape((group_len, width), BF),
            shape((heads, group_len), F32),
            shape((group_len // 2, out_width), BF),
            shape((group_len // 2, out_width), BF),
        ],
        compiler_params=pltpu.CompilerParams(vmem_limit_bytes=KERNEL_VMEM),
        cost_estimate=takes("attend"),
        name="attend",
    )(me, starts, cosine, sine_part, query_up, output, *packs)


def attend_back_kernel(
    count,
    heads,
    block,
    me_ref,
    starts_ref,
    cos_ref,
    sin_ref,
    q_ref,
    mixed_ref,
    lse_ref,
    k_ref,
    v_ref,
    wq_ref,
    wo_ref,
    *refs,
):
    blocks = refs[:count]
    d_ref, dq_ref, even_ref, odd_ref, dk_ref, dv_ref = refs[count:]
    me = me_ref[0]
    chip, core = me >> 1, me & 1
    index = pl.program_id(0)
    at = index ^ chip
    half = block // 2
    latent_width = wq_ref.shape[0]

    @pl.when(index == 0)
    def _():
        for source, here in zip(blocks, piece_slices(blocks), strict=True):
            d_ref[here, :] = source[...]
        dk_ref[...] = jnp.zeros_like(dk_ref)
        dv_ref[...] = jnp.zeros_like(dv_ref)

    own = pl.ds(pl.multiple_of(index * block, block), block)
    d_mixed = dot_rows(d_ref[own, :], wo_ref[...]).astype(BF)
    starts_row = starts_ref[...]
    key_place = block_places((block, 1), 0, core)
    query_place = at * block + block_places((1, block), 1, core)
    columns = [slice(h * HEAD_DIM, (h + 1) * HEAD_DIM) for h in range(heads)]
    offsets = [
        jnp.sum(
            (d_mixed[:, cols].astype(F32) * mixed_ref[:, cols].astype(F32)).T,
            axis=0,
            keepdims=True,
        )
        for cols in columns
    ]

    def step(b, running):
        here = pl.ds(pl.multiple_of((b ^ chip) * block, block), block)
        keys_here = b * block + key_place
        visible = (keys_here <= query_place) & (keys_here >= starts_row)
        keys, values = k_ref[here, :], v_ref[here, :]
        result = []
        for head in range(heads):
            q, dm = q_ref[:, columns[head]], d_mixed[:, columns[head]]
            scores = dot_rows(keys, q)
            scores = jnp.where(visible, scores, NEGATIVE)
            probs = jnp.where(visible, jnp.exp(scores - lse_ref[head : head + 1, :]), 0.0)
            d_probs = dot_rows(values, dm)
            d_scores = (probs * (d_probs - offsets[head])).astype(BF)
            dv_ref[here, :] += matmul(probs.astype(BF), dm)
            dk_ref[here, :] += matmul(d_scores, q)
            result.append(running[head] + dot_cols(d_scores, keys))
        return tuple(result)

    start = (jnp.zeros((block, HEAD_DIM), F32),) * heads
    d_queries = jnp.concatenate(lax.fori_loop(0, at + 1, step, start), axis=1)
    dq_ref[...] = rotate_heads(
        d_queries, cos_ref[...], -sin_ref[...], HEAD_DIM ** (-0.5)
    ).astype(BF)
    terms = dot_rows(dq_ref[...], wq_ref[...]).astype(BF)
    rows_here = pl.ds(pl.multiple_of(index * half, half), half)
    even_ref[rows_here, :latent_width] = terms[:half]
    odd_ref[rows_here, :latent_width] = terms[half:]

    @pl.when(index == pl.num_programs(0) - 1)
    def _():
        for j in range(k_ref.shape[0] // block):
            to = slice(j * half, (j + 1) * half)
            for target, first in ((even_ref, j * block), (odd_ref, j * block + half)):
                rows = slice(first, first + half)
                target[to, latent_width : latent_width + HEAD_DIM] = dk_ref[rows, :].astype(BF)
                target[to, latent_width + HEAD_DIM :] = dv_ref[rows, :].astype(BF)


def attend_back(
    me, starts, cosine, sine_part, queries, mixed, lse, keys, values, query_up, output, blocks, block
):
    group_len, width = queries.shape
    heads = width // HEAD_DIM
    out_width = blocks[0].shape[1]
    latent_width = query_up.shape[0]
    pack_width = latent_width + 2 * HEAD_DIM
    tokens = pl.BlockSpec((block, width), lambda i, me: (i, 0))
    angle = pl.BlockSpec((block, HEAD_DIM // 2), lambda i, me: (i, 0))
    lanes = pl.BlockSpec((heads, block), lambda i, me: (0, i))
    half = (group_len // 2, pack_width)
    shape = jax.ShapeDtypeStruct
    return pl.pallas_call(
        functools.partial(attend_back_kernel, len(blocks), heads, block),
        grid_spec=pltpu.PrefetchScalarGridSpec(
            num_scalar_prefetch=1,
            grid=(group_len // block,),
            in_specs=[
                pl.BlockSpec((1, block), lambda i, me: (0, i)),
                angle,
                angle,
                tokens,
                tokens,
                lanes,
                whole_spec(keys.shape),
                whole_spec(values.shape),
                whole_spec(query_up.shape),
                whole_spec(output.shape),
            ]
            + [whole_spec(piece.shape) for piece in blocks],
            out_specs=[
                whole_spec((group_len, out_width)),
                tokens,
                whole_spec(half),
                whole_spec(half),
            ],
            scratch_shapes=[pltpu.VMEM((group_len, HEAD_DIM), F32)] * 2,
        ),
        out_shape=[
            shape((group_len, out_width), BF),
            shape((group_len, width), BF),
            shape(half, BF),
            shape(half, BF),
        ],
        compiler_params=pltpu.CompilerParams(vmem_limit_bytes=KERNEL_VMEM),
        cost_estimate=takes("attend_back"),
        name="attend_back",
    )(
        me,
        starts,
        cosine,
        sine_part,
        queries,
        mixed,
        lse,
        keys,
        values,
        query_up,
        output,
        *blocks,
    )


def attention_grads_kernel(n_dp, query_rows, mixed_ref, latent_ref, dq_ref, d_ref, out_ref):
    out_rows = mixed_ref.shape[1] // n_dp
    output_terms = dot_cols(mixed_ref[...], d_ref[...]).astype(BF)
    query_terms = dot_cols(latent_ref[...], dq_ref[...])
    for z in range(n_dp):
        out_ref[z, :out_rows, :] = output_terms[z * out_rows : (z + 1) * out_rows]
        parts = [
            query_terms[first : first + query_rows]
            for first in range(z * query_rows, query_terms.shape[0], n_dp * query_rows)
        ]
        out_ref[z, out_rows:, :] = jnp.concatenate(parts, axis=0).astype(BF)


def attention_grads(mixed, latent, d_query, d_branch, n_dp, query_rows):
    group_len, width = d_branch.shape
    heads_width = mixed.shape[1]
    sets = width // heads_width
    part = latent.shape[1] // sets
    rows = heads_width // n_dp + part // n_dp
    return pl.pallas_call(
        functools.partial(attention_grads_kernel, n_dp, query_rows),
        grid=(sets,),
        in_specs=[
            whole_spec(mixed.shape),
            pl.BlockSpec((group_len, part), lambda j: (0, j)),
            whole_spec(d_query.shape),
            pl.BlockSpec((group_len, heads_width), lambda j: (0, j)),
        ],
        out_specs=pl.BlockSpec((n_dp, rows, heads_width), lambda j: (0, 0, j)),
        out_shape=jax.ShapeDtypeStruct((n_dp, rows, width), BF),
        compiler_params=pltpu.CompilerParams(vmem_limit_bytes=KERNEL_VMEM),
        cost_estimate=takes("attention_grads"),
        name="attention_grads",
    )(mixed, latent, d_query, d_branch)


def columns_back_kernel(parts_ref, *targets):
    for which, target in enumerate(targets):
        parts = [parts_ref[k, which].astype(F32) for k in range(parts_ref.shape[0])]
        target[...] = jnp.concatenate(parts, axis=1)


def columns_back(parts):
    n_seq, kinds, rows, columns = parts.shape
    vmem = pl.BlockSpec(memory_space=pltpu.VMEM)
    return pl.pallas_call(
        columns_back_kernel,
        in_specs=[vmem],
        out_specs=[vmem] * kinds,
        out_shape=[jax.ShapeDtypeStruct((rows, n_seq * columns), F32)] * kinds,
        compiler_params=pltpu.CompilerParams(vmem_limit_bytes=KERNEL_VMEM),
        cost_estimate=takes("columns_back"),
        name="columns_back",
    )(parts)


def local(
    layer_input,
    doc_lengths,
    attention_gain,
    query_down,
    query_gain,
    query_up,
    keyvalue_weight,
    output_weight,
    feedforward_gain,
    gate_weight,
    up_weight,
    down_weight,
    cotangent,
):
    n_seq, n_dp = lax.axis_size("seq"), lax.axis_size("dp")
    me = lax.axis_index("seq")
    input_low = layer_input[0]
    tokens = input_low.astype(F32)
    tok_count, width = tokens.shape
    latent_width = query_down.shape[1]
    group_len = tok_count * n_seq
    heads = HEADS // n_seq
    hidden_units = gate_weight.shape[1] // n_seq

    starts_all, position_all = document_starts(doc_lengths[0], group_len)
    starts_all = relative(starts_all, 0)
    position_all = relative(position_all, 0)
    cosine_all, sine_all = rope_tables(position_all, HEAD_DIM)
    me_array = me.astype(jnp.int32).reshape(1)

    own_rows = query_down.shape[0]
    query_rows = query_gain.shape[0]
    gains = jnp.stack(
        [attention_gain, feedforward_gain, jnp.pad(query_gain, (0, own_rows - query_rows))], axis=1
    )
    first_set = jnp.concatenate(
        [query_down, keyvalue_weight, jnp.pad(gains, ((0, 0), (0, 125)))], axis=1
    )
    chain = Chain()
    block = 2 * tok_count
    half_chips = n_seq // 4
    first_width = latent_width + 2 * HEAD_DIM
    out_rows = output_weight.shape[0]

    chain.add(tables=(cosine_all, sine_all, starts_all.reshape(1, group_len)))
    first_set, query_up = together(first_set, query_up)
    chain.add(query_part=exchange(split_columns(query_up)))
    chain.add(feed_step=gather_near(cotangent[0]))
    first_part = chain.stage(FIRST_PART, gather_dp_steps(first_set))
    query_part = chain.query_part.reshape(-1, query_up.shape[1] // n_seq)
    fold = query_part.shape[0] * query_part.shape[1] // width
    attention_set = jnp.concatenate([output_weight, query_part.reshape(fold, width)], axis=0)
    chain.add(attention=gather_dp(chain.begin(attention=attention_set)))
    chain.add(gate_up_parts=jnp.stack([split_columns(gate_weight), split_columns(up_weight)], axis=1),
    )
    near = chain.stage(FIRST_NEAR, gather_near(first_part))
    far = chain.stage(FIRST_FAR, gather_far(near))
    chain.add(gate_up=exchange(chain.begin(gate_up=chain.gate_up_parts)))
    first_blocks = chain.stage(FIRST_BLOCKS, gather_cores(far))
    cosine_all, sine_all, starts_all = chain.tables
    cosine, sine_part = cosine_all[:tok_count], sine_all[:tok_count]
    pack, latent, normed_parts, attention_gain_row, feed_gain_row, query_gain_row = first_projections(
        me_array, input_low, cosine, sine_part, first_blocks, latent_width
    )
    feed_gain_f = feed_gain_row[0]
    pack = chain.stage(PACK, pack)
    attention_part = chain.attention.reshape(n_dp, -1, width)
    full_output = attention_part[:, :out_rows].reshape(-1, width)
    full_query_up = rows_in_order(
        attention_part[:, out_rows:].reshape(-1, query_part.shape[1]), query_up.shape[0]
    )
    chain.add(attention_weights=(full_output, full_query_up))
    near = chain.stage(PACK_NEAR, gather_near(pack))
    gate_up = chain.gate_up
    chain.add(gate_up_all=gather_dp(gate_up.reshape(-1, hidden_units)).reshape(n_dp, *gate_up.shape),
    )
    chain.add(down_all=gather_dp(down_weight))
    packs = chain.stage(PACKS, gather_cores(gather_far(near)))
    full_output, full_query_up = chain.attention_weights
    chain.add(feed_far=gather_far(chain.begin(feed_far=chain.feed_step)))
    latent_all, keys, values, queries, mixed_low, lse, out_even, out_odd = attend(
        me_array,
        starts_all,
        cosine_all,
        sine_all,
        full_query_up,
        full_output,
        packs,
        latent_width,
        block,
    )
    out_even, out_odd = chain.stage(ATTENDED, (out_even, out_odd))
    feed_pieces = gather_cores(chain.feed_far)
    out_left = chain.stage(OUT_LEFT, scatter_relay(chip_sums(out_even, out_odd, n_seq // 2))
    )
    hidden = chain.stage(HIDDEN, tokens + scatter_last(out_left))

    chain.add(feed_stack=stack_blocks(chain.begin(feed_stack=feed_pieces)))
    feed_low = rms_norm(hidden, feed_gain_f).astype(BF)
    near = chain.stage(FEED_NEAR, gather_near(feed_low))
    feed_blocks = chain.stage(FEED_BLOCKS, gather_cores(gather_far(near)))
    chain.add(normed_columns=exchange(chain.begin(normed_columns=normed_parts)))
    feed, active_low, silu_low, slope_low, gate_ordered, up_ordered = feed_forward(
        feed_blocks, chain.gate_up_all, block
    )
    chain.add(grad_down_term=dot_cols(active_low, chain.feed_stack).astype(BF))
    silu_low = chain.stage(ACTIVE, silu_low)
    d_feed = chain.feed_stack
    chain.add(grad_down=scatter_dp(chain.grad_down_term))
    weights = (gate_ordered, up_ordered, chain.down_all)
    dg_high, du_high, even_high, odd_high = feed_back(
        d_feed, silu_low, slope_low, *weights, block, half_chips, half_chips
    )
    even_high, odd_high = chain.stage(TERMS_HIGH, (even_high, odd_high))
    chain.add(high_swap=flip(odd_high, 1))
    dg_low, du_low, *terms_low = feed_back(
        d_feed, after(silu_low, odd_high), slope_low, *weights, block, 0, half_chips
    )
    terms_low = chain.stage(TERMS_LOW, terms_low)
    feed_sums = chip_sums(*terms_low, half_chips) + split_chips(
        plus(even_high, chain.high_swap), half_chips
    )
    feed_sums = chain.stage(FEED_SUMS, feed_sums)
    feed_left = chain.stage(FEED_LEFT, scatter_relay(feed_sums))
    grad_gate_up_term = gate_up_grad(
        chain.begin(grad_gate_up_term=feed), (dg_low, du_low), (dg_high, du_high), n_dp, n_seq
    )
    chain.add(grad_gate_up_term=grad_gate_up_term)
    chain.add(grad_gate_up=scatter_dp(grad_gate_up_term.reshape(-1, hidden_units)))
    d_feed_normed = chain.stage(D_NORMED, scatter_last(feed_left))

    d_result = cotangent[0].astype(F32)
    d_hidden_norm, grad_feed_gain_term = jax.vjp(rms_norm, hidden, feed_gain_f)[1](d_feed_normed)
    d_hidden = d_result + d_hidden_norm
    chain.add(result_terms=pair_product(chain.begin(result_terms=active_low), chain.down_all, block),
    )
    near = chain.stage(BRANCH_NEAR, gather_near(d_hidden.astype(BF)))
    chain.add(result_sums=chip_sums(*chain.result_terms, n_seq // 2))
    d_branch_blocks = gather_cores(gather_far(near))
    d_branch_blocks, feed_gain_term = chain.stage(BRANCH_BLOCKS, (d_branch_blocks, grad_feed_gain_term.reshape(1, -1))
    )
    chain.add(result_left=scatter_relay(chain.begin(result_left=chain.result_sums)))
    chain.add(result_hops=early_hops(chain.result_left))
    d_branch, d_query_low, back_even, back_odd = attend_back(
        me_array,
        starts_all,
        cosine_all,
        sine_all,
        queries,
        mixed_low,
        lse,
        keys,
        values,
        full_query_up,
        full_output,
        d_branch_blocks,
        block,
    )
    back_even, back_odd = chain.stage(BACK_TERMS, (back_even, back_odd))
    back_sums = chain.stage(BACK_SUMS, chip_sums(back_even, back_odd, n_seq // 2))
    d_branch, latent_all = chain.begin(grad_attention_term=(d_branch, latent_all))
    chain.add(grad_attention_term=attention_grads(mixed_low, latent_all, d_query_low, d_branch, n_dp, query_rows),
    )
    back_left = chain.stage(BACK_LEFT, scatter_relay(back_sums))
    back_local = chain.stage(BACK_LOCAL, scatter_last(back_left))
    chain.add(grad_attention=scatter_dp(chain.grad_attention_term.reshape(-1, width)))
    chain.add(result_late=late_hops(chain.begin(result_last=chain.result_left)))
    load, d_tokens = last_products(
        me_array,
        back_local,
        latent,
        query_gain_row,
        input_low,
        attention_gain_row,
        cosine,
        sine_part,
        feed_gain_term,
        first_blocks,
    )
    load = chain.stage(FIRST_TERMS, load)
    result_left = chain.result_left
    hops = chain.result_hops + chain.result_late
    result = hidden + hops_sum(result_left, hops)
    layer_output = result.astype(BF)[None]
    chain.add(layer_output=layer_output)
    input_grad = (d_hidden + d_tokens)[None]
    chain.add(input_grad=input_grad)
    near = chain.stage(LAST_NEAR, gather_near(load))
    loads = chain.stage(LAST_BLOCKS, gather_cores(gather_far(near)))
    first_sum = chain.stage(FIRST_SUM, first_grads(me_array, chain.normed_columns, loads, latent_width)
    )
    gate_up_rows = chain.begin(gate_up_rows=chain.grad_gate_up)
    gate_up_rows = exchange(gate_up_rows.reshape(n_seq, 2, own_rows, -1))
    grad_first = scatter_dp(first_sum).astype(F32)

    grad_down = chain.grad_down
    grad_attention = chain.grad_attention
    grad_output_weight = grad_attention[:out_rows].astype(F32)
    grad_query_up = grad_attention[out_rows:].reshape(fold, -1, heads * HEAD_DIM)
    grad_query_up = grad_query_up.transpose(1, 0, 2).reshape(n_seq, query_rows, -1)
    grad_query_up = exchange(after(grad_query_up, gate_up_rows))
    grad_query_up = grad_query_up.transpose(1, 0, 2).reshape(query_rows, -1).astype(F32)

    grad_gate, grad_up = columns_back(gate_up_rows)
    return (
        layer_output,
        input_grad,
        grad_first[:, first_width],
        grad_first[:, :latent_width],
        grad_first[:query_rows, first_width + 2],
        grad_query_up,
        grad_first[:, latent_width:first_width],
        grad_output_weight,
        grad_first[:, first_width + 1],
        grad_gate,
        grad_up,
        grad_down.astype(F32),
    )


def solution(mesh):
    shards = P(("seq", "dp"))
    tokens = P("dp", "seq", None)
    weight = P(("seq", "dp"), None)
    return jax.shard_map(
        local,
        mesh=mesh,
        in_specs=(
            tokens,
            P("dp", None),
            shards,
            weight,
            shards,
            weight,
            weight,
            weight,
            shards,
            weight,
            weight,
            weight,
            tokens,
        ),
        out_specs=(
            tokens,
            tokens,
            shards,
            weight,
            shards,
            weight,
            weight,
            weight,
            shards,
            weight,
            weight,
            weight,
        ),
        check_vma=False,
    )
```

```python
import functools

import jax
import jax.numpy as jnp
from jax import lax
from jax.experimental import pallas as pl
from jax.experimental.pallas import tpu as pltpu
from jax.sharding import PartitionSpec as P

HEADS = 16
HEAD_DIM = 256


EPS = 1e-05
ROPE_BASE = 10000.0
NEGATIVE = -1e30
BF = jnp.bfloat16
F32 = jnp.float32
KERNEL_VMEM = 50 * 2**20


KERNEL_COST = dict(
    stack_blocks=0.01,
    first_projections=0.01,
    attend=0.01,
    feed_forward=0.01,
    feed_back=0.01,
    gate_up_grad=0.01,
    pair_product=3,
    attend_back=0.01,
    last_products=0.01,
    first_grads=0.01,
    columns_back=0.01,
    attention_grads=0.01,
)
(
    FIRST_PART,
    FIRST_NEAR,
    FIRST_FAR,
    FIRST_BLOCKS,
    PACK,
    PACK_NEAR,
    PACKS,
    ATTENDED,
    OUT_LEFT,
    HIDDEN,
    FEED_NEAR,
    FEED_BLOCKS,
    ACTIVE,
    TERMS_HIGH,
    TERMS_LOW,
    FEED_SUMS,
    FEED_LEFT,
    D_NORMED,
    BRANCH_NEAR,
    BRANCH_BLOCKS,
    BRANCH_ALL,
    BACK_TERMS,
    BACK_SUMS,
    BACK_LEFT,
    BACK_LOCAL,
    FIRST_TERMS,
    LAST_NEAR,
    LAST_BLOCKS,
    FIRST_SUM,
) = range(29)
DUE = dict(
    tables=FIRST_BLOCKS,
    feed_step=FIRST_PART,
    query_part=FIRST_PART,
    gate_up_parts=FIRST_NEAR,
    gate_up=PACK,
    gate_up_all=FEED_NEAR,
    feed_far=ATTENDED,
    feed_stack=FEED_NEAR,
    grad_down_term=ACTIVE,
    down_all=TERMS_HIGH,
    high_swap=TERMS_LOW,
    grad_down=D_NORMED,
    grad_gate_up_term=D_NORMED,
    result_terms=BRANCH_NEAR,
    result_sums=BRANCH_BLOCKS,
    result_left=BACK_TERMS,
    grad_gate_up=BACK_LEFT,
    grad_attention_term=BACK_LEFT,
    grad_attention=FIRST_SUM,
    attention=PACK,
    attention_weights=PACK_NEAR,
    normed_columns=ACTIVE,
    result_hops=BACK_TERMS,
    result_late=FIRST_TERMS,
    layer_output=LAST_NEAR,
    input_grad=LAST_NEAR,
)
BEGIN = dict(
    output=FIRST_PART,
    gate_up=FIRST_FAR,
    feed_far=PACKS,
    grad_gate_up_term=FEED_LEFT,
    result_terms=D_NORMED,
    result_left=BRANCH_NEAR,
    result_last=BACK_LOCAL,
    grad_attention_term=BACK_SUMS,
    normed_columns=FEED_BLOCKS,
    feed_stack=HIDDEN,
    gate_up_rows=LAST_BLOCKS,
)


def takes(kernel):
    microseconds = KERNEL_COST[kernel]
    return pl.CostEstimate(
        flops=int(microseconds * 1e9), bytes_accessed=int(microseconds * 2e6), transcendentals=0
    )


class Chain:
    def __init__(self):
        self.stages = {}
        self.side = {}

    def add(self, **made):
        self.side.update(made)

    def begin(self, **waiting):
        ((name, value),) = waiting.items()
        return after(value, self.stages[BEGIN[name]]) if name in BEGIN else value

    def stage(self, at, value):
        due = [name for name in self.side if DUE.get(name) == at]
        if due:
            value, there = together(value, [self.side[name] for name in due])
            self.side.update(zip(due, there, strict=True))
        self.stages[at] = value
        return value

    def __getattr__(self, name):
        return self.side[name]


def rms_norm(values, norm_gain):
    return values * lax.rsqrt(jnp.mean(values * values, axis=-1, keepdims=True) + EPS) * norm_gain


def rope_tables(position, feature_width):
    half_width = feature_width // 2
    freqs = ROPE_BASE ** (-jnp.arange(half_width, dtype=F32) * 2.0 / feature_width)
    angles = position.astype(F32)[:, None] * freqs[None, :]
    return (jnp.cos(angles), jnp.sin(angles))


def rotate(values, cosine, sine_part):
    half_width = values.shape[-1] // 2
    first_half = values[..., :half_width]
    second_half = values[..., half_width:]
    return jnp.concatenate(
        [
            first_half * cosine - second_half * sine_part,
            second_half * cosine + first_half * sine_part,
        ],
        axis=-1,
    )


def document_starts(lengths_row, group_len):
    doc_ends = jnp.cumsum(lengths_row)
    places = jnp.arange(group_len, dtype=jnp.int32)
    past_ends = (places[:, None] >= doc_ends[None, :]).astype(jnp.int32)
    starts = jnp.sum(past_ends * lengths_row[None, :], axis=1)
    return (starts, places - starts)


def gated(gate_proj, upward):
    return jax.nn.silu(gate_proj) * upward


def matmul(left_side, right_side):
    return jnp.dot(left_side, right_side, preferred_element_type=F32)


def dot_rows(left_side, right_side):
    return lax.dot_general(
        left_side, right_side, (((1,), (1,)), ((), ())), preferred_element_type=F32
    )


def dot_cols(left_side, right_side):
    return lax.dot_general(
        left_side, right_side, (((0,), (0,)), ((), ())), preferred_element_type=F32
    )


def flip(block, bits):
    n_seq = lax.axis_size("seq")
    return lax.ppermute(block, "seq", [(i, i ^ bits) for i in range(n_seq)])


def gather_near(rows):
    n_seq = lax.axis_size("seq")
    hops = (2, 4) if n_seq == 8 else range(2, n_seq, 2)
    return {0: rows} | {bits: flip(rows, bits) for bits in hops}


def gather_far(blocks):
    if lax.axis_size("seq") != 8:
        return blocks
    half = blocks[0].shape[0] // 2
    return blocks | {6: [flip(blocks[4][:half], 2), flip(blocks[2][half:], 4)]}


def gather_cores(blocks):
    whole = []
    for bits in range(0, lax.axis_size("seq"), 2):
        own = blocks[bits] if isinstance(blocks[bits], list) else [blocks[bits]]
        whole += own + [flip(piece, 1) for piece in own]
    return whole


def piece_slices(pieces):
    slices, first = [], 0
    for piece in pieces:
        slices.append(slice(first, first + piece.shape[0]))
        first += piece.shape[0]
    return slices


def gather_blocks(rows):
    return gather_cores(gather_far(gather_near(rows)))


def together(*values):
    flat, tree = jax.tree.flatten(values)
    return jax.tree.unflatten(tree, lax.optimization_barrier(flat))


def after(values, *first):
    return together(values, *first)[0]


def stack_kernel(count, *refs):
    sources, target, held, arrived, left = refs[:count], *refs[count:]
    moves = []
    for k, (source, rows) in enumerate(zip(sources, piece_slices(sources), strict=True)):
        here = pl.ds(rows.start, rows.stop - rows.start)
        moves.append(
            (
                pltpu.make_async_copy(source, held.at[here], arrived.at[k]),
                pltpu.make_async_copy(held.at[here], target.at[here], left.at[k]),
            )
        )
    for come, _ in moves:
        come.start()
    for come, go in moves:
        come.wait()
        go.start()
    for _, go in moves:
        go.wait()


def stack_blocks(pieces):
    width, dtype = pieces[0].shape[1], pieces[0].dtype
    shape = (sum(piece.shape[0] for piece in pieces), width)
    return pl.pallas_call(
        functools.partial(stack_kernel, len(pieces)),
        in_specs=[pl.BlockSpec(memory_space=pl.ANY)] * len(pieces),
        out_specs=pl.BlockSpec(memory_space=pl.ANY),
        out_shape=jax.ShapeDtypeStruct(shape, dtype),
        scratch_shapes=[pltpu.VMEM(shape, dtype)]
        + [pltpu.SemaphoreType.DMA((len(pieces),))] * 2,
        compiler_params=pltpu.CompilerParams(vmem_limit_bytes=KERNEL_VMEM),
        cost_estimate=takes("stack_blocks"),
        name="stack_blocks",
    )(*pieces)


def plus(first, second):
    return (first.astype(F32) + second.astype(F32)).astype(BF)


def split_chips(total, count):
    rows = total.shape[0] // count
    return [total[k * rows : (k + 1) * rows] for k in range(count)]


def chip_sums(even, odd, count):
    return split_chips(plus(even, flip(odd, 1)), count)


def scatter_relay(sums):
    n_seq = lax.axis_size("seq")
    if n_seq != 8:
        return {k: [part] for k, part in enumerate(sums)}
    half = sums[0].shape[0] // 2
    far_x = flip(sums[3][:half], 2)
    far_y = flip(sums[3][half:], 4)
    return {
        0: [sums[0]],
        1: [sums[1][:half], plus(sums[1][half:], far_y)],
        2: [sums[2][half:], plus(sums[2][:half], far_x)],
    }


def early_hops(left):
    if lax.axis_size("seq") != 8:
        return [flip(parts[0], 2 * k) for k, parts in left.items() if k]
    return [flip(left[1][0], 2), flip(left[2][0], 4)]


def late_hops(left):
    if lax.axis_size("seq") != 8:
        return []
    return [flip(left[1][1], 2), flip(left[2][1], 4)]


def hops_sum(left, hops):
    own = left[0][0].astype(F32)
    if lax.axis_size("seq") != 8:
        return sum((hop.astype(F32) for hop in hops), own)
    x_low, y_high, x_high, y_low = [hop.astype(F32) for hop in hops]
    return own + jnp.concatenate([x_low + y_low, x_high + y_high], axis=0)


def scatter_last(left):
    return hops_sum(left, early_hops(left) + late_hops(left))


def scatter_pairs(even, odd):
    count = lax.axis_size("seq") // 2
    return scatter_last(scatter_relay(chip_sums(even, odd, count)))


def relative(values, axis):
    n_seq, me = lax.axis_size("seq"), lax.axis_index("seq")
    size = values.shape[axis] // n_seq
    parts = [
        lax.dynamic_slice_in_dim(values, (me ^ k) * size, size, axis) for k in range(n_seq)
    ]
    return jnp.concatenate(parts, axis=axis)


def relative_vectors(values):
    n_seq, me = lax.axis_size("seq"), lax.axis_index("seq")
    count, length = values.shape
    values = values.reshape(count, n_seq, length // n_seq)
    bit = 1
    while bit < n_seq:
        pairs = values.reshape(count, n_seq // (2 * bit), 2, bit, length // n_seq)
        swapped = jnp.concatenate([pairs[:, :, 1:], pairs[:, :, :1]], axis=2)
        values = jnp.where((me & bit) != 0, swapped, pairs).reshape(values.shape)
        bit *= 2
    return values.reshape(count, length)


def gather_dp(rows):
    return lax.all_gather(rows, "dp", axis=0, tiled=True)


def gather_dp_steps(rows):
    n_dp, me = lax.axis_size("dp"), lax.axis_index("dp")
    size = rows.shape[0]
    whole = jnp.zeros((n_dp * size, rows.shape[1]), rows.dtype)
    for bits in range(n_dp):
        block = rows
        if bits:
            block = lax.ppermute(rows, "dp", [(i, i ^ bits) for i in range(n_dp)])
        whole = lax.dynamic_update_slice_in_dim(whole, block, (me ^ bits) * size, 0)
    return whole


def scatter_dp(terms):
    return lax.psum_scatter(terms, "dp", scatter_dimension=0, tiled=True)


def split_columns(shard):
    n_seq = lax.axis_size("seq")
    rows, width = shard.shape
    return shard.reshape(rows, n_seq, width // n_seq).transpose(1, 0, 2)


def exchange(parts):
    return lax.all_to_all(parts, "seq", 0, 0)


def rows_in_order(gathered, rows):
    n_seq, n_dp = lax.axis_size("seq"), lax.axis_size("dp")
    width = gathered.shape[-1]
    return gathered.reshape(n_dp, n_seq, rows, width).transpose(1, 0, 2, 3).reshape(-1, width)


def rows_by_dp(terms):
    n_seq, n_dp = lax.axis_size("seq"), lax.axis_size("dp")
    total, width = terms.shape
    rows = total // (n_seq * n_dp)
    return terms.reshape(n_seq, n_dp, rows, width).transpose(1, 0, 2, 3)


def spread(n_dp, own, rows):
    shape = (n_dp * own, n_dp * rows)
    at = lax.broadcasted_iota(jnp.int32, shape, 0)
    to = lax.broadcasted_iota(jnp.int32, shape, 1)
    hit = to == at // own * rows + at % own
    return jnp.where(hit, 1.0, 0.0).astype(BF)


def exchanged_rows(rows, me):
    count = len(rows)
    result = []
    for k in range(count):
        row = rows[0]
        for at in range(1, count):
            row = jnp.where((me ^ k) == at, rows[at], row)
        result.append(row)
    return result


def first_kernel(count, n_seq, n_dp, me_ref, x_ref, cos_ref, sin_ref, *refs):
    pieces = refs[:count]
    pack_ref, latent_ref, parts_ref, gain_ref, feed_gain_ref, query_gain_ref, out_ref = refs[count:]
    me = me_ref[0]
    latent_width = latent_ref.shape[1]
    low_width = pack_ref.shape[1]
    x = x_ref[...].astype(F32)
    scale = lax.rsqrt(jnp.mean(x * x, axis=1, keepdims=True) + EPS)
    size = x_ref.shape[1] // n_seq
    gains = []
    for k, here in enumerate(piece_slices(pieces)):
        gains.append(pieces[k][:, low_width:].astype(F32).T[:8])
        owner, first = me ^ (here.start // size), here.start % size
        rows = here.stop - here.start
        own = pl.ds(pl.multiple_of(owner * size + first, rows), rows)
        normed = (x_ref[:, own].astype(F32) * scale * gains[k][:1]).astype(BF)
        parts_ref[owner, :, first : first + rows] = normed
        gain_ref[:, own] = gains[k][:1]
        feed_gain_ref[:, own] = gains[k][1:2]
        part = matmul(normed, pieces[k][:, :low_width])
        if k == 0:
            out_ref[...] = part
        else:
            out_ref[...] += part
    gains = jnp.concatenate(gains, axis=1)
    own = latent_width // (n_seq * n_dp)
    query_rows = []
    for k in range(n_seq):
        query_rows.append(gains[2:3, k * size : (k + 1) * size])
    query_rows = exchanged_rows(query_rows, me)
    query_rows = dot_rows(
        jnp.concatenate(query_rows, axis=0).astype(BF), spread(n_dp, own, size // n_dp)
    )
    query_gain = jnp.concatenate([query_rows[k : k + 1] for k in range(n_seq)], axis=1)
    query_gain_ref[...] = query_gain
    latent = out_ref[:, :latent_width]
    latent_ref[...] = latent
    latent_scale = lax.rsqrt(jnp.mean(latent * latent, axis=1, keepdims=True) + EPS)
    pack_ref[:, :latent_width] = (latent * latent_scale * query_gain).astype(BF)
    keyvalue = out_ref[:, latent_width:]
    pack_ref[:, latent_width : latent_width + HEAD_DIM] = rotate_heads(
        keyvalue[:, :HEAD_DIM], cos_ref[...], sin_ref[...], 1.0
    ).astype(BF)
    pack_ref[:, latent_width + HEAD_DIM :] = keyvalue[:, HEAD_DIM:].astype(BF)


def first_projections(me, x, cosine, sine_part, pieces, latent_width):
    n_seq = lax.axis_size("seq")
    tok_count, width = x.shape
    low_width = pieces[0].shape[1] - 128
    vmem = pl.BlockSpec(memory_space=pltpu.VMEM)
    shape = jax.ShapeDtypeStruct
    return pl.pallas_call(
        functools.partial(
            first_kernel, len(pieces), lax.axis_size("seq"), lax.axis_size("dp")
        ),
        in_specs=[pl.BlockSpec(memory_space=pltpu.SMEM)] + [vmem] * (3 + len(pieces)),
        out_specs=[vmem] * 6,
        out_shape=[
            shape((tok_count, low_width), BF),
            shape((tok_count, latent_width), F32),
            shape((n_seq, tok_count, width // n_seq), BF),
            shape((1, width), F32),
            shape((1, width), F32),
            shape((1, latent_width), F32),
        ],
        scratch_shapes=[pltpu.VMEM((tok_count, low_width), F32)],
        compiler_params=pltpu.CompilerParams(vmem_limit_bytes=KERNEL_VMEM),
        cost_estimate=takes("first_projections"),
        name="first_projections",
    )(me, x, cosine, sine_part, *pieces)


def weights_in_order(raw_ref, gate_ref, up_ref):
    n_dp, n_seq, _, rows, _ = raw_ref.shape
    for s in range(n_seq):
        for z in range(n_dp):
            here = pl.ds((s * n_dp + z) * rows, rows)
            gate_ref[here, :] = raw_ref[z, s, 0]
            up_ref[here, :] = raw_ref[z, s, 1]


def feed_kernel(count, block, *refs):
    blocks, raw_ref = refs[:count], refs[count]
    x_ref, act_ref, silu_ref, slope_ref, gate_ref, up_ref = refs[count + 1 :]
    at = pl.program_id(0)

    @pl.when(at == 0)
    def _():
        for source, here in zip(blocks, piece_slices(blocks), strict=True):
            x_ref[here, :] = source[...]
        weights_in_order(raw_ref, gate_ref, up_ref)

    x = x_ref[pl.ds(pl.multiple_of(at * block, block), block), :]
    gate = matmul(x, gate_ref[...])
    upward = matmul(x, up_ref[...])
    sigmoid = 1.0 / (1.0 + jnp.exp(-gate))
    silu = gate * sigmoid
    act_ref[...] = (silu * upward).astype(BF)
    silu_ref[...] = silu.astype(BF)
    slope_ref[...] = (upward * (sigmoid + silu * (1.0 - sigmoid))).astype(BF)


def whole_spec(shape):
    return pl.BlockSpec(shape, lambda *_: (0,) * len(shape), pipeline_mode=pl.Buffered(1))


def feed_forward(blocks, raw, block):
    width = blocks[0].shape[1]
    group_len = sum(piece.shape[0] for piece in blocks)
    hidden = raw.shape[-1]
    units = pl.BlockSpec((block, hidden), lambda i: (i, 0))
    weight = jax.ShapeDtypeStruct((width, hidden), BF)
    return pl.pallas_call(
        functools.partial(feed_kernel, len(blocks), block),
        grid=(group_len // block,),
        in_specs=[whole_spec(piece.shape) for piece in blocks] + [whole_spec(raw.shape)],
        out_specs=[whole_spec((group_len, width))]
        + [units] * 3
        + [whole_spec((width, hidden))] * 2,
        out_shape=[jax.ShapeDtypeStruct((group_len, width), BF)]
        + [jax.ShapeDtypeStruct((group_len, hidden), BF)] * 3
        + [weight] * 2,
        compiler_params=pltpu.CompilerParams(vmem_limit_bytes=KERNEL_VMEM),
        cost_estimate=takes("feed_forward"),
        name="feed_forward",
    )(*blocks, raw)


def feed_back_kernel(
    d_ref, silu_ref, slope_ref, gate_ref, up_ref, down_ref, dg_ref, du_ref, even_ref, odd_ref
):
    d_active = dot_rows(d_ref[...], down_ref[...])
    d_gate = (d_active * slope_ref[...].astype(F32)).astype(BF)
    d_up = (d_active * silu_ref[...].astype(F32)).astype(BF)
    dg_ref[...] = d_gate
    du_ref[...] = d_up
    terms = (dot_rows(d_gate, gate_ref[...]) + dot_rows(d_up, up_ref[...])).astype(BF)
    half = terms.shape[0] // 2
    even_ref[...] = terms[:half]
    odd_ref[...] = terms[half:]


def feed_back(d, silu, slope, gate, up, down, block, first, count):
    width, hidden = gate.shape
    tokens = pl.BlockSpec((block, width), lambda i: (i + first, 0))
    units = pl.BlockSpec((block, hidden), lambda i: (i + first, 0))
    half = pl.BlockSpec((block // 2, width), lambda i: (i, 0))
    return pl.pallas_call(
        feed_back_kernel,
        grid=(count,),
        in_specs=[tokens, units, units]
        + [whole_spec(gate.shape), whole_spec(up.shape), whole_spec(down.shape)],
        out_specs=[pl.BlockSpec((block, hidden), lambda i: (i, 0))] * 2 + [half] * 2,
        out_shape=[jax.ShapeDtypeStruct((count * block, hidden), BF)] * 2
        + [jax.ShapeDtypeStruct((count * block // 2, width), BF)] * 2,
        compiler_params=pltpu.CompilerParams(vmem_limit_bytes=KERNEL_VMEM),
        cost_estimate=takes("feed_back"),
        name="feed_back",
    )(d, silu, slope, gate, up, down)


def gate_up_grad_kernel(x_ref, dg_low, du_low, dg_high, du_high, out_ref):
    n_dp, _, _, rows, _ = out_ref.shape
    middle = dg_low.shape[0]
    low, high = x_ref[:middle, :], x_ref[middle:, :]
    for which, (d_low, d_high) in enumerate(((dg_low, dg_high), (du_low, du_high))):
        terms = (dot_cols(low, d_low[...]) + dot_cols(high, d_high[...])).astype(BF)
        for z in range(n_dp):
            out_ref[z, 0, which] = terms[z * rows : (z + 1) * rows]


def gate_up_grad(x, low, high, n_dp, n_seq):
    group_len, width = x.shape
    hidden = low[0].shape[1]
    rows = width // (n_dp * n_seq)
    return pl.pallas_call(
        gate_up_grad_kernel,
        grid=(n_seq,),
        in_specs=[pl.BlockSpec((group_len, n_dp * rows), lambda i: (0, i))]
        + [whole_spec(part.shape) for part in (*low, *high)],
        out_specs=pl.BlockSpec((n_dp, 1, 2, rows, hidden), lambda i: (0, i, 0, 0, 0)),
        out_shape=jax.ShapeDtypeStruct((n_dp, n_seq, 2, rows, hidden), BF),
        compiler_params=pltpu.CompilerParams(vmem_limit_bytes=KERNEL_VMEM),
        cost_estimate=takes("gate_up_grad"),
        name="gate_up_grad",
    )(x, *low, *high)


def pair_product_kernel(left_ref, right_ref, even_ref, odd_ref):
    terms = matmul(left_ref[...], right_ref[...]).astype(BF)
    half = terms.shape[0] // 2
    even_ref[...] = terms[:half]
    odd_ref[...] = terms[half:]


def pair_product(left, right, block):
    rows, depth = left.shape
    width = right.shape[1]
    half = pl.BlockSpec((block // 2, width), lambda i: (i, 0))
    return pl.pallas_call(
        pair_product_kernel,
        grid=(rows // block,),
        in_specs=[pl.BlockSpec((block, depth), lambda i: (i, 0)), whole_spec(right.shape)],
        out_specs=[half] * 2,
        out_shape=[jax.ShapeDtypeStruct((rows // 2, width), BF)] * 2,
        compiler_params=pltpu.CompilerParams(vmem_limit_bytes=KERNEL_VMEM),
        cost_estimate=takes("pair_product"),
        name="pair_product",
    )(left, right)


GAIN_ROWS = 32


def last_kernel(
    count,
    n_seq,
    me_ref,
    back_ref,
    latent_ref,
    query_gain_ref,
    x_ref,
    gain_ref,
    cos_ref,
    sin_ref,
    feed_term_ref,
    *refs,
):
    blocks, (load_ref, dx_ref) = refs[:count], refs[count:]
    me = me_ref[0]
    latent_width = latent_ref.shape[1]
    tok_count, first_width = back_ref.shape
    width = x_ref.shape[1]
    size = width // n_seq

    def norm_back(v, e, gain):
        r = lax.rsqrt(jnp.mean(v * v, axis=1, keepdims=True) + EPS)
        u = v * r
        eg = e * gain
        grad = r * (eg - u * jnp.mean(eg * u, axis=1, keepdims=True))
        return grad, jnp.sum(e * u, axis=0, keepdims=True)

    d_latent, query_term = norm_back(
        latent_ref[...], back_ref[:, :latent_width], query_gain_ref[...]
    )
    half = HEAD_DIM // 2
    first_half = back_ref[:, latent_width : latent_width + half]
    second_half = back_ref[:, latent_width + half : latent_width + HEAD_DIM]
    cosine, sine_part = cos_ref[...], sin_ref[...]
    d_first = jnp.concatenate(
        [
            d_latent,
            first_half * cosine + second_half * sine_part,
            second_half * cosine - first_half * sine_part,
            back_ref[:, latent_width + HEAD_DIM :],
        ],
        axis=1,
    ).astype(BF)
    load_ref[:tok_count, :] = d_first
    for piece, here in zip(blocks, piece_slices(blocks), strict=True):
        rows = here.stop - here.start
        place = (me ^ (here.start // size)) * size + here.start % size
        own = pl.ds(pl.multiple_of(place, rows), rows)
        dx_ref[:, own] = dot_rows(d_first, piece[:, :first_width])
    dx_ref[...], gain_term = norm_back(x_ref[...].astype(F32), dx_ref[...], gain_ref[...])
    pad = jnp.zeros((1, 2 * first_width - width), F32)
    rows = [
        gain_term[:, :first_width],
        jnp.concatenate([gain_term[:, first_width:], pad], axis=1),
        feed_term_ref[:, :first_width],
        jnp.concatenate([feed_term_ref[:, first_width:], pad], axis=1),
        jnp.concatenate([query_term, jnp.zeros((1, first_width - latent_width), F32)], axis=1),
        jnp.zeros((GAIN_ROWS - 5, first_width), F32),
    ]
    load_ref[tok_count:, :] = jnp.concatenate(rows, axis=0).astype(BF)


def last_products(me, back, latent, query_gain, x, gain, cosine, sine_part, feed_term, blocks):
    tok_count, width = x.shape
    vmem = pl.BlockSpec(memory_space=pltpu.VMEM)
    return pl.pallas_call(
        functools.partial(last_kernel, len(blocks), lax.axis_size("seq")),
        in_specs=[pl.BlockSpec(memory_space=pltpu.SMEM)] + [vmem] * (8 + len(blocks)),
        out_specs=[vmem] * 2,
        out_shape=[
            jax.ShapeDtypeStruct((tok_count + GAIN_ROWS, back.shape[1]), BF),
            jax.ShapeDtypeStruct((tok_count, width), F32),
        ],
        compiler_params=pltpu.CompilerParams(vmem_limit_bytes=KERNEL_VMEM),
        cost_estimate=takes("last_products"),
        name="last_products",
    )(me, back, latent, query_gain, x, gain, cosine, sine_part, feed_term, *blocks)


def first_grads_kernel(count, n_seq, n_dp, latent_width, me_ref, normed_ref, *refs):
    pieces, (out_ref, d_ref, x_ref) = refs[:count], refs[count:]
    me = me_ref[0]
    tok_count, size = normed_ref.shape[1:]
    first_width = d_ref.shape[1]
    block = tok_count + GAIN_ROWS
    terms = jnp.zeros((8, first_width), F32)
    for piece, here in zip(pieces, piece_slices(pieces), strict=True):
        k, first = here.start // block, here.start % block
        tokens = min(tok_count - first, piece.shape[0])
        d_ref[k * tok_count + first : k * tok_count + first + tokens, :] = piece[:tokens, :]
        if tokens < piece.shape[0]:
            terms = terms + piece[tokens : tokens + 16, :].astype(F32)[:8]
    for k in range(n_seq):
        x_ref[k * tok_count : (k + 1) * tok_count, :] = normed_ref[me ^ k]
    out_ref[:, :first_width] = dot_cols(x_ref[...], d_ref[...]).astype(BF)
    width = size * n_seq
    rest = width - first_width

    def share(row, length):
        own = row[:, :length]
        for k in range(1, n_seq):
            own = jnp.where(me == k, row[:, k * length : (k + 1) * length], own)
        return own

    gain = jnp.concatenate([terms[0:1], terms[1:2, :rest]], axis=1)
    feed = jnp.concatenate([terms[2:3], terms[3:4, :rest]], axis=1)
    query = share(terms[4:5, :latent_width], latent_width // n_seq)
    query = matmul(
        jnp.concatenate([query] * 8, axis=0).astype(BF),
        spread(n_dp, query.shape[1] // n_dp, size // n_dp),
    )[:1]
    rows = [share(gain, size), share(feed, size), query, jnp.zeros((125, size), F32)]
    out_ref[:, first_width:] = jnp.concatenate(rows, axis=0).T.astype(BF)


def first_grads(me, normed, pieces, latent_width):
    n_seq, tok_count, size = normed.shape
    first_width = pieces[0].shape[1]
    vmem = pl.BlockSpec(memory_space=pltpu.VMEM)
    return pl.pallas_call(
        functools.partial(
            first_grads_kernel, len(pieces), n_seq, lax.axis_size("dp"), latent_width
        ),
        in_specs=[pl.BlockSpec(memory_space=pltpu.SMEM)] + [vmem] * (1 + len(pieces)),
        out_specs=vmem,
        out_shape=jax.ShapeDtypeStruct((size, first_width + 128), BF),
        scratch_shapes=[
            pltpu.VMEM((n_seq * tok_count, first_width), BF),
            pltpu.VMEM((n_seq * tok_count, size), BF),
        ],
        compiler_params=pltpu.CompilerParams(vmem_limit_bytes=KERNEL_VMEM),
        cost_estimate=takes("first_grads"),
        name="first_grads",
    )(me, normed, *pieces)


def block_places(shape, axis, core):
    rows = lax.broadcasted_iota(jnp.int32, shape, axis)
    half = shape[axis] // 2
    return rows + core * jnp.where(rows < half, half, -half)


def rotate_heads(values, cosine, sine_part, scale):
    half = HEAD_DIM // 2
    parts = []
    for at in range(0, values.shape[1], HEAD_DIM):
        first_half = values[:, at : at + half]
        second_half = values[:, at + half : at + HEAD_DIM]
        parts.append((first_half * cosine - second_half * sine_part) * scale)
        parts.append((second_half * cosine + first_half * sine_part) * scale)
    return jnp.concatenate(parts, axis=1)


def attend_kernel(
    count,
    heads,
    block,
    me_ref,
    starts_ref,
    cos_ref,
    sin_ref,
    wq_ref,
    wo_ref,
    *refs,
):
    packs = refs[:count]
    lat_ref, k_ref, v_ref, q_ref, mixed_ref, lse_ref, even_ref, odd_ref, vt_ref = refs[count:]
    me = me_ref[0]
    chip, core = me >> 1, me & 1
    index = pl.program_id(0)
    at = index ^ chip
    latent_width = lat_ref.shape[1]

    @pl.when(index == 0)
    def _():
        for pack, here in zip(packs, piece_slices(packs), strict=True):
            lat_ref[here, :] = pack[:, :latent_width]
            k_ref[here, :] = pack[:, latent_width : latent_width + HEAD_DIM]
            v_ref[here, :] = pack[:, latent_width + HEAD_DIM :]
        for j in range(k_ref.shape[0] // block):
            here = slice(j * block, (j + 1) * block)
            vt_ref[:, here] = v_ref[here, :].T

    own = pl.ds(pl.multiple_of(index * block, block), block)
    query_raw = matmul(lat_ref[own, :], wq_ref[...])
    q_ref[...] = rotate_heads(
        query_raw, cos_ref[...], sin_ref[...], HEAD_DIM ** (-0.5)
    ).astype(BF)
    starts_row = starts_ref[...]
    key_place = block_places((block, 1), 0, core)
    query_place = at * block + block_places((1, block), 1, core)
    columns = [slice(h * HEAD_DIM, (h + 1) * HEAD_DIM) for h in range(heads)]

    def step(b, running):
        here = pl.ds(pl.multiple_of((b ^ chip) * block, block), block)
        keys_here = b * block + key_place
        visible = (keys_here <= query_place) & (keys_here >= starts_row)
        result = []
        for head in range(heads):
            running_max, running_sum, total = running[head]
            scores = dot_rows(k_ref[here, :], q_ref[:, columns[head]])
            scores = jnp.where(visible, scores, NEGATIVE)
            new_max = jnp.maximum(running_max, jnp.max(scores, axis=0, keepdims=True))
            factor = jnp.exp(running_max - new_max)
            terms = jnp.where(visible, jnp.exp(scores - new_max), 0.0)
            running_sum = running_sum * factor + jnp.sum(terms, axis=0, keepdims=True)
            total = total * factor + matmul(vt_ref[:, here], terms.astype(BF))
            result.append((new_max, running_sum, total))
        return tuple(result)

    start = (
        jnp.full((1, block), NEGATIVE, F32),
        jnp.zeros((1, block), F32),
        jnp.zeros((HEAD_DIM, block), F32),
    )
    running = lax.fori_loop(0, at + 1, step, (start,) * heads)
    for head in range(heads):
        running_max, running_sum, total = running[head]
        mixed_ref[:, columns[head]] = (total / running_sum).T.astype(BF)
        lse_ref[head : head + 1, :] = running_max + jnp.log(running_sum)
    terms = matmul(mixed_ref[...], wo_ref[...]).astype(BF)
    even_ref[...] = terms[: block // 2]
    odd_ref[...] = terms[block // 2 :]


def attend(me, starts, cosine, sine_part, query_up, output, packs, latent_width, block):
    pack_width = packs[0].shape[1]
    group_len = sum(piece.shape[0] for piece in packs)
    width = query_up.shape[1]
    heads = width // HEAD_DIM
    out_width = output.shape[1]
    tokens = pl.BlockSpec((block, width), lambda i, me: (i, 0))
    half = pl.BlockSpec((block // 2, out_width), lambda i, me: (i, 0))
    angle = pl.BlockSpec((block, HEAD_DIM // 2), lambda i, me: (i, 0))
    lanes = pl.BlockSpec((heads, block), lambda i, me: (0, i))
    shape = jax.ShapeDtypeStruct
    return pl.pallas_call(
        functools.partial(attend_kernel, len(packs), heads, block),
        grid_spec=pltpu.PrefetchScalarGridSpec(
            num_scalar_prefetch=1,
            grid=(group_len // block,),
            in_specs=[
                pl.BlockSpec((1, block), lambda i, me: (0, i)),
                angle,
                angle,
                whole_spec(query_up.shape),
                whole_spec(output.shape),
            ]
            + [whole_spec(piece.shape) for piece in packs],
            out_specs=[
                whole_spec((group_len, latent_width)),
                whole_spec((group_len, HEAD_DIM)),
                whole_spec((group_len, HEAD_DIM)),
                tokens,
                tokens,
                lanes,
                half,
                half,
            ],
            scratch_shapes=[pltpu.VMEM((HEAD_DIM, group_len), BF)],
        ),
        out_shape=[
            shape((group_len, latent_width), BF),
            shape((group_len, HEAD_DIM), BF),
            shape((group_len, HEAD_DIM), BF),
            shape((group_len, width), BF),
            shape((group_len, width), BF),
            shape((heads, group_len), F32),
            shape((group_len // 2, out_width), BF),
            shape((group_len // 2, out_width), BF),
        ],
        compiler_params=pltpu.CompilerParams(vmem_limit_bytes=KERNEL_VMEM),
        cost_estimate=takes("attend"),
        name="attend",
    )(me, starts, cosine, sine_part, query_up, output, *packs)


def attend_back_kernel(
    count,
    heads,
    block,
    me_ref,
    starts_ref,
    cos_ref,
    sin_ref,
    q_ref,
    mixed_ref,
    lse_ref,
    k_ref,
    v_ref,
    wq_ref,
    wo_ref,
    *refs,
):
    blocks = refs[:count]
    d_ref, dq_ref, even_ref, odd_ref, dk_ref, dv_ref = refs[count:]
    me = me_ref[0]
    chip, core = me >> 1, me & 1
    index = pl.program_id(0)
    at = index ^ chip
    half = block // 2
    latent_width = wq_ref.shape[0]

    @pl.when(index == 0)
    def _():
        for source, here in zip(blocks, piece_slices(blocks), strict=True):
            d_ref[here, :] = source[...]
        dk_ref[...] = jnp.zeros_like(dk_ref)
        dv_ref[...] = jnp.zeros_like(dv_ref)

    own = pl.ds(pl.multiple_of(index * block, block), block)
    d_mixed = dot_rows(d_ref[own, :], wo_ref[...]).astype(BF)
    starts_row = starts_ref[...]
    key_place = block_places((block, 1), 0, core)
    query_place = at * block + block_places((1, block), 1, core)
    columns = [slice(h * HEAD_DIM, (h + 1) * HEAD_DIM) for h in range(heads)]
    offsets = [
        jnp.sum(
            (d_mixed[:, cols].astype(F32) * mixed_ref[:, cols].astype(F32)).T,
            axis=0,
            keepdims=True,
        )
        for cols in columns
    ]

    def step(b, running):
        here = pl.ds(pl.multiple_of((b ^ chip) * block, block), block)
        keys_here = b * block + key_place
        visible = (keys_here <= query_place) & (keys_here >= starts_row)
        keys, values = k_ref[here, :], v_ref[here, :]
        result = []
        for head in range(heads):
            q, dm = q_ref[:, columns[head]], d_mixed[:, columns[head]]
            scores = dot_rows(keys, q)
            scores = jnp.where(visible, scores, NEGATIVE)
            probs = jnp.where(visible, jnp.exp(scores - lse_ref[head : head + 1, :]), 0.0)
            d_probs = dot_rows(values, dm)
            d_scores = (probs * (d_probs - offsets[head])).astype(BF)
            dv_ref[here, :] += matmul(probs.astype(BF), dm)
            dk_ref[here, :] += matmul(d_scores, q)
            result.append(running[head] + dot_cols(d_scores, keys))
        return tuple(result)

    start = (jnp.zeros((block, HEAD_DIM), F32),) * heads
    d_queries = jnp.concatenate(lax.fori_loop(0, at + 1, step, start), axis=1)
    dq_ref[...] = rotate_heads(
        d_queries, cos_ref[...], -sin_ref[...], HEAD_DIM ** (-0.5)
    ).astype(BF)
    terms = dot_rows(dq_ref[...], wq_ref[...]).astype(BF)
    rows_here = pl.ds(pl.multiple_of(index * half, half), half)
    even_ref[rows_here, :latent_width] = terms[:half]
    odd_ref[rows_here, :latent_width] = terms[half:]

    @pl.when(index == pl.num_programs(0) - 1)
    def _():
        for j in range(k_ref.shape[0] // block):
            to = slice(j * half, (j + 1) * half)
            for target, first in ((even_ref, j * block), (odd_ref, j * block + half)):
                rows = slice(first, first + half)
                target[to, latent_width : latent_width + HEAD_DIM] = dk_ref[rows, :].astype(BF)
                target[to, latent_width + HEAD_DIM :] = dv_ref[rows, :].astype(BF)


def attend_back(
    me, starts, cosine, sine_part, queries, mixed, lse, keys, values, query_up, output, blocks, block
):
    group_len, width = queries.shape
    heads = width // HEAD_DIM
    out_width = blocks[0].shape[1]
    latent_width = query_up.shape[0]
    pack_width = latent_width + 2 * HEAD_DIM
    tokens = pl.BlockSpec((block, width), lambda i, me: (i, 0))
    angle = pl.BlockSpec((block, HEAD_DIM // 2), lambda i, me: (i, 0))
    lanes = pl.BlockSpec((heads, block), lambda i, me: (0, i))
    half = (group_len // 2, pack_width)
    shape = jax.ShapeDtypeStruct
    return pl.pallas_call(
        functools.partial(attend_back_kernel, len(blocks), heads, block),
        grid_spec=pltpu.PrefetchScalarGridSpec(
            num_scalar_prefetch=1,
            grid=(group_len // block,),
            in_specs=[
                pl.BlockSpec((1, block), lambda i, me: (0, i)),
                angle,
                angle,
                tokens,
                tokens,
                lanes,
                whole_spec(keys.shape),
                whole_spec(values.shape),
                whole_spec(query_up.shape),
                whole_spec(output.shape),
            ]
            + [whole_spec(piece.shape) for piece in blocks],
            out_specs=[
                whole_spec((group_len, out_width)),
                tokens,
                whole_spec(half),
                whole_spec(half),
            ],
            scratch_shapes=[pltpu.VMEM((group_len, HEAD_DIM), F32)] * 2,
        ),
        out_shape=[
            shape((group_len, out_width), BF),
            shape((group_len, width), BF),
            shape(half, BF),
            shape(half, BF),
        ],
        compiler_params=pltpu.CompilerParams(vmem_limit_bytes=KERNEL_VMEM),
        cost_estimate=takes("attend_back"),
        name="attend_back",
    )(
        me,
        starts,
        cosine,
        sine_part,
        queries,
        mixed,
        lse,
        keys,
        values,
        query_up,
        output,
        *blocks,
    )


def attention_grads_kernel(n_dp, query_rows, mixed_ref, latent_ref, dq_ref, d_ref, out_ref):
    out_rows = mixed_ref.shape[1] // n_dp
    output_terms = dot_cols(mixed_ref[...], d_ref[...]).astype(BF)
    query_terms = dot_cols(latent_ref[...], dq_ref[...])
    for z in range(n_dp):
        out_ref[z, :out_rows, :] = output_terms[z * out_rows : (z + 1) * out_rows]
        parts = [
            query_terms[first : first + query_rows]
            for first in range(z * query_rows, query_terms.shape[0], n_dp * query_rows)
        ]
        out_ref[z, out_rows:, :] = jnp.concatenate(parts, axis=0).astype(BF)


def attention_grads(mixed, latent, d_query, d_branch, n_dp, query_rows):
    group_len, width = d_branch.shape
    heads_width = mixed.shape[1]
    sets = width // heads_width
    part = latent.shape[1] // sets
    rows = heads_width // n_dp + part // n_dp
    return pl.pallas_call(
        functools.partial(attention_grads_kernel, n_dp, query_rows),
        grid=(sets,),
        in_specs=[
            whole_spec(mixed.shape),
            pl.BlockSpec((group_len, part), lambda j: (0, j)),
            whole_spec(d_query.shape),
            pl.BlockSpec((group_len, heads_width), lambda j: (0, j)),
        ],
        out_specs=pl.BlockSpec((n_dp, rows, heads_width), lambda j: (0, 0, j)),
        out_shape=jax.ShapeDtypeStruct((n_dp, rows, width), BF),
        compiler_params=pltpu.CompilerParams(vmem_limit_bytes=KERNEL_VMEM),
        cost_estimate=takes("attention_grads"),
        name="attention_grads",
    )(mixed, latent, d_query, d_branch)


def columns_back_kernel(parts_ref, *targets):
    for which, target in enumerate(targets):
        parts = [parts_ref[k, which].astype(F32) for k in range(parts_ref.shape[0])]
        target[...] = jnp.concatenate(parts, axis=1)


def columns_back(parts):
    n_seq, kinds, rows, columns = parts.shape
    vmem = pl.BlockSpec(memory_space=pltpu.VMEM)
    return pl.pallas_call(
        columns_back_kernel,
        in_specs=[vmem],
        out_specs=[vmem] * kinds,
        out_shape=[jax.ShapeDtypeStruct((rows, n_seq * columns), F32)] * kinds,
        compiler_params=pltpu.CompilerParams(vmem_limit_bytes=KERNEL_VMEM),
        cost_estimate=takes("columns_back"),
        name="columns_back",
    )(parts)


def local(
    layer_input,
    doc_lengths,
    attention_gain,
    query_down,
    query_gain,
    query_up,
    keyvalue_weight,
    output_weight,
    feedforward_gain,
    gate_weight,
    up_weight,
    down_weight,
    cotangent,
):
    n_seq, n_dp = lax.axis_size("seq"), lax.axis_size("dp")
    me = lax.axis_index("seq")
    input_low = layer_input[0]
    tokens = input_low.astype(F32)
    tok_count, width = tokens.shape
    latent_width = query_down.shape[1]
    group_len = tok_count * n_seq
    heads = HEADS // n_seq
    hidden_units = gate_weight.shape[1] // n_seq

    starts_all, position_all = document_starts(doc_lengths[0], group_len)
    starts_all = relative(starts_all, 0)
    position_all = relative(position_all, 0)
    cosine_all, sine_all = rope_tables(position_all, HEAD_DIM)
    me_array = me.astype(jnp.int32).reshape(1)

    own_rows = query_down.shape[0]
    query_rows = query_gain.shape[0]
    gains = jnp.stack(
        [attention_gain, feedforward_gain, jnp.pad(query_gain, (0, own_rows - query_rows))], axis=1
    )
    first_set = jnp.concatenate(
        [query_down, keyvalue_weight, jnp.pad(gains, ((0, 0), (0, 125)))], axis=1
    )
    chain = Chain()
    block = 2 * tok_count
    half_chips = n_seq // 4
    first_width = latent_width + 2 * HEAD_DIM
    out_rows = output_weight.shape[0]

    chain.add(tables=(cosine_all, sine_all, starts_all.reshape(1, group_len)))
    first_set, query_up = together(first_set, query_up)
    chain.add(query_part=exchange(split_columns(query_up)))
    chain.add(feed_step=gather_near(cotangent[0]))
    first_part = chain.stage(FIRST_PART, gather_dp_steps(first_set))
    query_part = chain.query_part.reshape(-1, query_up.shape[1] // n_seq)
    fold = query_part.shape[0] * query_part.shape[1] // width
    attention_set = jnp.concatenate([output_weight, query_part.reshape(fold, width)], axis=0)
    chain.add(attention=gather_dp(chain.begin(attention=attention_set)))
    chain.add(gate_up_parts=jnp.stack([split_columns(gate_weight), split_columns(up_weight)], axis=1),
    )
    near = chain.stage(FIRST_NEAR, gather_near(first_part))
    far = chain.stage(FIRST_FAR, gather_far(near))
    chain.add(gate_up=exchange(chain.begin(gate_up=chain.gate_up_parts)))
    first_blocks = chain.stage(FIRST_BLOCKS, gather_cores(far))
    cosine_all, sine_all, starts_all = chain.tables
    cosine, sine_part = cosine_all[:tok_count], sine_all[:tok_count]
    pack, latent, normed_parts, attention_gain_row, feed_gain_row, query_gain_row = first_projections(
        me_array, input_low, cosine, sine_part, first_blocks, latent_width
    )
    feed_gain_f = feed_gain_row[0]
    pack = chain.stage(PACK, pack)
    attention_part = chain.attention.reshape(n_dp, -1, width)
    full_output = attention_part[:, :out_rows].reshape(-1, width)
    full_query_up = rows_in_order(
        attention_part[:, out_rows:].reshape(-1, query_part.shape[1]), query_up.shape[0]
    )
    chain.add(attention_weights=(full_output, full_query_up))
    near = chain.stage(PACK_NEAR, gather_near(pack))
    gate_up = chain.gate_up
    chain.add(gate_up_all=gather_dp(gate_up.reshape(-1, hidden_units)).reshape(n_dp, *gate_up.shape),
    )
    chain.add(down_all=gather_dp(down_weight))
    packs = chain.stage(PACKS, gather_cores(gather_far(near)))
    full_output, full_query_up = chain.attention_weights
    chain.add(feed_far=gather_far(chain.begin(feed_far=chain.feed_step)))
    latent_all, keys, values, queries, mixed_low, lse, out_even, out_odd = attend(
        me_array,
        starts_all,
        cosine_all,
        sine_all,
        full_query_up,
        full_output,
        packs,
        latent_width,
        block,
    )
    out_even, out_odd = chain.stage(ATTENDED, (out_even, out_odd))
    feed_pieces = gather_cores(chain.feed_far)
    out_left = chain.stage(OUT_LEFT, scatter_relay(chip_sums(out_even, out_odd, n_seq // 2))
    )
    hidden = chain.stage(HIDDEN, tokens + scatter_last(out_left))

    chain.add(feed_stack=stack_blocks(chain.begin(feed_stack=feed_pieces)))
    feed_low = rms_norm(hidden, feed_gain_f).astype(BF)
    near = chain.stage(FEED_NEAR, gather_near(feed_low))
    feed_blocks = chain.stage(FEED_BLOCKS, gather_cores(gather_far(near)))
    chain.add(normed_columns=exchange(chain.begin(normed_columns=normed_parts)))
    feed, active_low, silu_low, slope_low, gate_ordered, up_ordered = feed_forward(
        feed_blocks, chain.gate_up_all, block
    )
    chain.add(grad_down_term=dot_cols(active_low, chain.feed_stack).astype(BF))
    silu_low = chain.stage(ACTIVE, silu_low)
    d_feed = chain.feed_stack
    chain.add(grad_down=scatter_dp(chain.grad_down_term))
    weights = (gate_ordered, up_ordered, chain.down_all)
    dg_high, du_high, even_high, odd_high = feed_back(
        d_feed, silu_low, slope_low, *weights, block, half_chips, half_chips
    )
    even_high, odd_high = chain.stage(TERMS_HIGH, (even_high, odd_high))
    chain.add(high_swap=flip(odd_high, 1))
    dg_low, du_low, *terms_low = feed_back(
        d_feed, after(silu_low, odd_high), slope_low, *weights, block, 0, half_chips
    )
    terms_low = chain.stage(TERMS_LOW, terms_low)
    feed_sums = chip_sums(*terms_low, half_chips) + split_chips(
        plus(even_high, chain.high_swap), half_chips
    )
    feed_sums = chain.stage(FEED_SUMS, feed_sums)
    feed_left = chain.stage(FEED_LEFT, scatter_relay(feed_sums))
    grad_gate_up_term = gate_up_grad(
        chain.begin(grad_gate_up_term=feed), (dg_low, du_low), (dg_high, du_high), n_dp, n_seq
    )
    chain.add(grad_gate_up_term=grad_gate_up_term)
    chain.add(grad_gate_up=scatter_dp(grad_gate_up_term.reshape(-1, hidden_units)))
    d_feed_normed = chain.stage(D_NORMED, scatter_last(feed_left))

    d_result = cotangent[0].astype(F32)
    d_hidden_norm, grad_feed_gain_term = jax.vjp(rms_norm, hidden, feed_gain_f)[1](d_feed_normed)
    d_hidden = d_result + d_hidden_norm
    chain.add(result_terms=pair_product(chain.begin(result_terms=active_low), chain.down_all, block),
    )
    near = chain.stage(BRANCH_NEAR, gather_near(d_hidden.astype(BF)))
    chain.add(result_sums=chip_sums(*chain.result_terms, n_seq // 2))
    d_branch_blocks = gather_cores(gather_far(near))
    d_branch_blocks, feed_gain_term = chain.stage(BRANCH_BLOCKS, (d_branch_blocks, grad_feed_gain_term.reshape(1, -1))
    )
    chain.add(result_left=scatter_relay(chain.begin(result_left=chain.result_sums)))
    chain.add(result_hops=early_hops(chain.result_left))
    d_branch, d_query_low, back_even, back_odd = attend_back(
        me_array,
        starts_all,
        cosine_all,
        sine_all,
        queries,
        mixed_low,
        lse,
        keys,
        values,
        full_query_up,
        full_output,
        d_branch_blocks,
        block,
    )
    back_even, back_odd = chain.stage(BACK_TERMS, (back_even, back_odd))
    back_sums = chain.stage(BACK_SUMS, chip_sums(back_even, back_odd, n_seq // 2))
    d_branch, latent_all = chain.begin(grad_attention_term=(d_branch, latent_all))
    chain.add(grad_attention_term=attention_grads(mixed_low, latent_all, d_query_low, d_branch, n_dp, query_rows),
    )
    back_left = chain.stage(BACK_LEFT, scatter_relay(back_sums))
    back_local = chain.stage(BACK_LOCAL, scatter_last(back_left))
    chain.add(grad_attention=scatter_dp(chain.grad_attention_term.reshape(-1, width)))
    chain.add(result_late=late_hops(chain.begin(result_last=chain.result_left)))
    load, d_tokens = last_products(
        me_array,
        back_local,
        latent,
        query_gain_row,
        input_low,
        attention_gain_row,
        cosine,
        sine_part,
        feed_gain_term,
        first_blocks,
    )
    load = chain.stage(FIRST_TERMS, load)
    result_left = chain.result_left
    hops = chain.result_hops + chain.result_late
    result = hidden + hops_sum(result_left, hops)
    layer_output = result.astype(BF)[None]
    chain.add(layer_output=layer_output)
    input_grad = (d_hidden + d_tokens)[None]
    chain.add(input_grad=input_grad)
    near = chain.stage(LAST_NEAR, gather_near(load))
    loads = chain.stage(LAST_BLOCKS, gather_cores(gather_far(near)))
    first_sum = chain.stage(FIRST_SUM, first_grads(me_array, chain.normed_columns, loads, latent_width)
    )
    gate_up_rows = chain.begin(gate_up_rows=chain.grad_gate_up)
    gate_up_rows = exchange(gate_up_rows.reshape(n_seq, 2, own_rows, -1))
    grad_first = scatter_dp(first_sum).astype(F32)

    grad_down = chain.grad_down
    grad_attention = chain.grad_attention
    grad_output_weight = grad_attention[:out_rows].astype(F32)
    grad_query_up = grad_attention[out_rows:].reshape(fold, -1, heads * HEAD_DIM)
    grad_query_up = grad_query_up.transpose(1, 0, 2).reshape(n_seq, query_rows, -1)
    grad_query_up = exchange(after(grad_query_up, gate_up_rows))
    grad_query_up = grad_query_up.transpose(1, 0, 2).reshape(query_rows, -1).astype(F32)

    grad_gate, grad_up = columns_back(gate_up_rows)
    return (
        layer_output,
        input_grad,
        grad_first[:, first_width],
        grad_first[:, :latent_width],
        grad_first[:query_rows, first_width + 2],
        grad_query_up,
        grad_first[:, latent_width:first_width],
        grad_output_weight,
        grad_first[:, first_width + 1],
        grad_gate,
        grad_up,
        grad_down.astype(F32),
    )


def solution(mesh):
    shards = P(("seq", "dp"))
    tokens = P("dp", "seq", None)
    weight = P(("seq", "dp"), None)
    return jax.shard_map(
        local,
        mesh=mesh,
        in_specs=(
            tokens,
            P("dp", None),
            shards,
            weight,
            shards,
            weight,
            weight,
            weight,
            shards,
            weight,
            weight,
            weight,
            tokens,
        ),
        out_specs=(
            tokens,
            tokens,
            shards,
            weight,
            shards,
            weight,
            weight,
            weight,
            shards,
            weight,
            weight,
            weight,
        ),
        check_vma=False,
    )
```

```python
import functools

import jax
import jax.numpy as jnp
from jax import lax
from jax.experimental import pallas as pl
from jax.experimental.pallas import tpu as pltpu
from jax.sharding import PartitionSpec as P

HEADS = 16
HEAD_DIM = 256


EPS = 1e-05
ROPE_BASE = 10000.0
NEGATIVE = -1e30
BF = jnp.bfloat16
F32 = jnp.float32
KERNEL_VMEM = 50 * 2**20


KERNEL_COST = dict(
    stack_blocks=0.01,
    first_projections=0.01,
    attend=0.01,
    feed_forward=0.01,
    feed_back=0.01,
    gate_up_grad=0.01,
    pair_product=3,
    attend_back=0.01,
    last_products=0.01,
    first_grads=0.01,
    columns_back=0.01,
    attention_grads=0.01,
)
(
    FIRST_PART,
    FIRST_NEAR,
    FIRST_FAR,
    FIRST_BLOCKS,
    PACK,
    PACK_NEAR,
    PACKS,
    ATTENDED,
    OUT_LEFT,
    HIDDEN,
    FEED_NEAR,
    FEED_BLOCKS,
    ACTIVE,
    TERMS_HIGH,
    TERMS_LOW,
    FEED_SUMS,
    FEED_LEFT,
    D_NORMED,
    BRANCH_NEAR,
    BRANCH_BLOCKS,
    BRANCH_ALL,
    BACK_TERMS,
    BACK_SUMS,
    BACK_LEFT,
    BACK_LOCAL,
    FIRST_TERMS,
    LAST_NEAR,
    LAST_BLOCKS,
    FIRST_SUM,
) = range(29)
DUE = dict(
    tables=FIRST_BLOCKS,
    feed_step=FIRST_PART,
    query_part=FIRST_PART,
    gate_up_parts=FIRST_NEAR,
    gate_up=PACK,
    gate_up_all=FEED_NEAR,
    feed_far=ATTENDED,
    feed_stack=FEED_NEAR,
    grad_down_term=ACTIVE,
    down_all=TERMS_HIGH,
    high_swap=TERMS_LOW,
    grad_down=D_NORMED,
    grad_gate_up_term=D_NORMED,
    result_terms=BRANCH_NEAR,
    result_sums=BRANCH_BLOCKS,
    result_left=BACK_TERMS,
    grad_gate_up=BACK_LEFT,
    grad_attention_term=BACK_LEFT,
    grad_attention=FIRST_SUM,
    attention=PACK,
    attention_weights=PACK_NEAR,
    normed_columns=ACTIVE,
    result_hops=BACK_TERMS,
    result_late=FIRST_TERMS,
    layer_output=LAST_NEAR,
    input_grad=LAST_NEAR,
)
BEGIN = dict(
    output=FIRST_PART,
    gate_up=FIRST_FAR,
    feed_far=PACKS,
    grad_gate_up_term=FEED_LEFT,
    result_terms=D_NORMED,
    result_left=BRANCH_NEAR,
    result_last=BACK_LOCAL,
    grad_attention_term=BACK_SUMS,
    normed_columns=FEED_BLOCKS,
    feed_stack=HIDDEN,
    gate_up_rows=LAST_BLOCKS,
)


def takes(kernel):
    microseconds = KERNEL_COST[kernel]
    return pl.CostEstimate(
        flops=int(microseconds * 1e9), bytes_accessed=int(microseconds * 2e6), transcendentals=0
    )


class Chain:
    def __init__(self):
        self.stages = {}
        self.side = {}

    def add(self, **made):
        self.side.update(made)

    def begin(self, **waiting):
        ((name, value),) = waiting.items()
        return after(value, self.stages[BEGIN[name]]) if name in BEGIN else value

    def stage(self, at, value):
        due = [name for name in self.side if DUE.get(name) == at]
        if due:
            value, there = together(value, [self.side[name] for name in due])
            self.side.update(zip(due, there, strict=True))
        self.stages[at] = value
        return value

    def __getattr__(self, name):
        return self.side[name]


def rms_norm(values, norm_gain):
    return values * lax.rsqrt(jnp.mean(values * values, axis=-1, keepdims=True) + EPS) * norm_gain


def rope_tables(position, feature_width):
    half_width = feature_width // 2
    freqs = ROPE_BASE ** (-jnp.arange(half_width, dtype=F32) * 2.0 / feature_width)
    angles = position.astype(F32)[:, None] * freqs[None, :]
    return (jnp.cos(angles), jnp.sin(angles))


def rotate(values, cosine, sine_part):
    half_width = values.shape[-1] // 2
    first_half = values[..., :half_width]
    second_half = values[..., half_width:]
    return jnp.concatenate(
        [
            first_half * cosine - second_half * sine_part,
            second_half * cosine + first_half * sine_part,
        ],
        axis=-1,
    )


def document_starts(lengths_row, group_len):
    doc_ends = jnp.cumsum(lengths_row)
    places = jnp.arange(group_len, dtype=jnp.int32)
    past_ends = (places[:, None] >= doc_ends[None, :]).astype(jnp.int32)
    starts = jnp.sum(past_ends * lengths_row[None, :], axis=1)
    return (starts, places - starts)


def gated(gate_proj, upward):
    return jax.nn.silu(gate_proj) * upward


def matmul(left_side, right_side):
    return jnp.dot(left_side, right_side, preferred_element_type=F32)


def dot_rows(left_side, right_side):
    return lax.dot_general(
        left_side, right_side, (((1,), (1,)), ((), ())), preferred_element_type=F32
    )


def dot_cols(left_side, right_side):
    return lax.dot_general(
        left_side, right_side, (((0,), (0,)), ((), ())), preferred_element_type=F32
    )


def flip(block, bits):
    n_seq = lax.axis_size("seq")
    return lax.ppermute(block, "seq", [(i, i ^ bits) for i in range(n_seq)])


def gather_near(rows):
    n_seq = lax.axis_size("seq")
    hops = (2, 4) if n_seq == 8 else range(2, n_seq, 2)
    return {0: rows} | {bits: flip(rows, bits) for bits in hops}


def gather_far(blocks):
    if lax.axis_size("seq") != 8:
        return blocks
    half = blocks[0].shape[0] // 2
    return blocks | {6: [flip(blocks[4][:half], 2), flip(blocks[2][half:], 4)]}


def gather_cores(blocks):
    whole = []
    for bits in range(0, lax.axis_size("seq"), 2):
        own = blocks[bits] if isinstance(blocks[bits], list) else [blocks[bits]]
        whole += own + [flip(piece, 1) for piece in own]
    return whole


def piece_slices(pieces):
    slices, first = [], 0
    for piece in pieces:
        slices.append(slice(first, first + piece.shape[0]))
        first += piece.shape[0]
    return slices


def gather_blocks(rows):
    return gather_cores(gather_far(gather_near(rows)))


def together(*values):
    flat, tree = jax.tree.flatten(values)
    return jax.tree.unflatten(tree, lax.optimization_barrier(flat))


def after(values, *first):
    return together(values, *first)[0]


def stack_kernel(count, *refs):
    sources, target, held, arrived, left = refs[:count], *refs[count:]
    moves = []
    for k, (source, rows) in enumerate(zip(sources, piece_slices(sources), strict=True)):
        here = pl.ds(rows.start, rows.stop - rows.start)
        moves.append(
            (
                pltpu.make_async_copy(source, held.at[here], arrived.at[k]),
                pltpu.make_async_copy(held.at[here], target.at[here], left.at[k]),
            )
        )
    for come, _ in moves:
        come.start()
    for come, go in moves:
        come.wait()
        go.start()
    for _, go in moves:
        go.wait()


def stack_blocks(pieces):
    width, dtype = pieces[0].shape[1], pieces[0].dtype
    shape = (sum(piece.shape[0] for piece in pieces), width)
    return pl.pallas_call(
        functools.partial(stack_kernel, len(pieces)),
        in_specs=[pl.BlockSpec(memory_space=pl.ANY)] * len(pieces),
        out_specs=pl.BlockSpec(memory_space=pl.ANY),
        out_shape=jax.ShapeDtypeStruct(shape, dtype),
        scratch_shapes=[pltpu.VMEM(shape, dtype)]
        + [pltpu.SemaphoreType.DMA((len(pieces),))] * 2,
        compiler_params=pltpu.CompilerParams(vmem_limit_bytes=KERNEL_VMEM),
        cost_estimate=takes("stack_blocks"),
        name="stack_blocks",
    )(*pieces)


def plus(first, second):
    return (first.astype(F32) + second.astype(F32)).astype(BF)


def split_chips(total, count):
    rows = total.shape[0] // count
    return [total[k * rows : (k + 1) * rows] for k in range(count)]


def chip_sums(even, odd, count):
    return split_chips(plus(even, flip(odd, 1)), count)


def scatter_relay(sums):
    n_seq = lax.axis_size("seq")
    if n_seq != 8:
        return {k: [part] for k, part in enumerate(sums)}
    half = sums[0].shape[0] // 2
    far_x = flip(sums[3][:half], 2)
    far_y = flip(sums[3][half:], 4)
    return {
        0: [sums[0]],
        1: [sums[1][:half], plus(sums[1][half:], far_y)],
        2: [sums[2][half:], plus(sums[2][:half], far_x)],
    }


def early_hops(left):
    if lax.axis_size("seq") != 8:
        return [flip(parts[0], 2 * k) for k, parts in left.items() if k]
    return [flip(left[1][0], 2), flip(left[2][0], 4)]


def late_hops(left):
    if lax.axis_size("seq") != 8:
        return []
    return [flip(left[1][1], 2), flip(left[2][1], 4)]


def hops_sum(left, hops):
    own = left[0][0].astype(F32)
    if lax.axis_size("seq") != 8:
        return sum((hop.astype(F32) for hop in hops), own)
    x_low, y_high, x_high, y_low = [hop.astype(F32) for hop in hops]
    return own + jnp.concatenate([x_low + y_low, x_high + y_high], axis=0)


def scatter_last(left):
    return hops_sum(left, early_hops(left) + late_hops(left))


def scatter_pairs(even, odd):
    count = lax.axis_size("seq") // 2
    return scatter_last(scatter_relay(chip_sums(even, odd, count)))


def relative(values, axis):
    n_seq, me = lax.axis_size("seq"), lax.axis_index("seq")
    size = values.shape[axis] // n_seq
    parts = [
        lax.dynamic_slice_in_dim(values, (me ^ k) * size, size, axis) for k in range(n_seq)
    ]
    return jnp.concatenate(parts, axis=axis)


def relative_vectors(values):
    n_seq, me = lax.axis_size("seq"), lax.axis_index("seq")
    count, length = values.shape
    values = values.reshape(count, n_seq, length // n_seq)
    bit = 1
    while bit < n_seq:
        pairs = values.reshape(count, n_seq // (2 * bit), 2, bit, length // n_seq)
        swapped = jnp.concatenate([pairs[:, :, 1:], pairs[:, :, :1]], axis=2)
        values = jnp.where((me & bit) != 0, swapped, pairs).reshape(values.shape)
        bit *= 2
    return values.reshape(count, length)


def gather_dp(rows):
    return lax.all_gather(rows, "dp", axis=0, tiled=True)


def gather_dp_steps(rows):
    n_dp, me = lax.axis_size("dp"), lax.axis_index("dp")
    size = rows.shape[0]
    whole = jnp.zeros((n_dp * size, rows.shape[1]), rows.dtype)
    for bits in range(n_dp):
        block = rows
        if bits:
            block = lax.ppermute(rows, "dp", [(i, i ^ bits) for i in range(n_dp)])
        whole = lax.dynamic_update_slice_in_dim(whole, block, (me ^ bits) * size, 0)
    return whole


def scatter_dp(terms):
    return lax.psum_scatter(terms, "dp", scatter_dimension=0, tiled=True)


def split_columns(shard):
    n_seq = lax.axis_size("seq")
    rows, width = shard.shape
    return shard.reshape(rows, n_seq, width // n_seq).transpose(1, 0, 2)


def exchange(parts):
    return lax.all_to_all(parts, "seq", 0, 0)


def rows_in_order(gathered, rows):
    n_seq, n_dp = lax.axis_size("seq"), lax.axis_size("dp")
    width = gathered.shape[-1]
    return gathered.reshape(n_dp, n_seq, rows, width).transpose(1, 0, 2, 3).reshape(-1, width)


def rows_by_dp(terms):
    n_seq, n_dp = lax.axis_size("seq"), lax.axis_size("dp")
    total, width = terms.shape
    rows = total // (n_seq * n_dp)
    return terms.reshape(n_seq, n_dp, rows, width).transpose(1, 0, 2, 3)


def spread(n_dp, own, rows):
    shape = (n_dp * own, n_dp * rows)
    at = lax.broadcasted_iota(jnp.int32, shape, 0)
    to = lax.broadcasted_iota(jnp.int32, shape, 1)
    hit = to == at // own * rows + at % own
    return jnp.where(hit, 1.0, 0.0).astype(BF)


def exchanged_rows(rows, me):
    count = len(rows)
    result = []
    for k in range(count):
        row = rows[0]
        for at in range(1, count):
            row = jnp.where((me ^ k) == at, rows[at], row)
        result.append(row)
    return result


def first_kernel(count, n_seq, n_dp, me_ref, x_ref, cos_ref, sin_ref, *refs):
    pieces = refs[:count]
    pack_ref, latent_ref, parts_ref, gain_ref, feed_gain_ref, query_gain_ref, out_ref = refs[count:]
    me = me_ref[0]
    latent_width = latent_ref.shape[1]
    low_width = pack_ref.shape[1]
    x = x_ref[...].astype(F32)
    scale = lax.rsqrt(jnp.mean(x * x, axis=1, keepdims=True) + EPS)
    size = x_ref.shape[1] // n_seq
    gains = []
    for k, here in enumerate(piece_slices(pieces)):
        gains.append(pieces[k][:, low_width:].astype(F32).T[:8])
        owner, first = me ^ (here.start // size), here.start % size
        rows = here.stop - here.start
        own = pl.ds(pl.multiple_of(owner * size + first, rows), rows)
        normed = (x_ref[:, own].astype(F32) * scale * gains[k][:1]).astype(BF)
        parts_ref[owner, :, first : first + rows] = normed
        gain_ref[:, own] = gains[k][:1]
        feed_gain_ref[:, own] = gains[k][1:2]
        part = matmul(normed, pieces[k][:, :low_width])
        if k == 0:
            out_ref[...] = part
        else:
            out_ref[...] += part
    gains = jnp.concatenate(gains, axis=1)
    own = latent_width // (n_seq * n_dp)
    query_rows = []
    for k in range(n_seq):
        query_rows.append(gains[2:3, k * size : (k + 1) * size])
    query_rows = exchanged_rows(query_rows, me)
    query_rows = dot_rows(
        jnp.concatenate(query_rows, axis=0).astype(BF), spread(n_dp, own, size // n_dp)
    )
    query_gain = jnp.concatenate([query_rows[k : k + 1] for k in range(n_seq)], axis=1)
    query_gain_ref[...] = query_gain
    latent = out_ref[:, :latent_width]
    latent_ref[...] = latent
    latent_scale = lax.rsqrt(jnp.mean(latent * latent, axis=1, keepdims=True) + EPS)
    pack_ref[:, :latent_width] = (latent * latent_scale * query_gain).astype(BF)
    keyvalue = out_ref[:, latent_width:]
    pack_ref[:, latent_width : latent_width + HEAD_DIM] = rotate_heads(
        keyvalue[:, :HEAD_DIM], cos_ref[...], sin_ref[...], 1.0
    ).astype(BF)
    pack_ref[:, latent_width + HEAD_DIM :] = keyvalue[:, HEAD_DIM:].astype(BF)


def first_projections(me, x, cosine, sine_part, pieces, latent_width):
    n_seq = lax.axis_size("seq")
    tok_count, width = x.shape
    low_width = pieces[0].shape[1] - 128
    vmem = pl.BlockSpec(memory_space=pltpu.VMEM)
    shape = jax.ShapeDtypeStruct
    return pl.pallas_call(
        functools.partial(
            first_kernel, len(pieces), lax.axis_size("seq"), lax.axis_size("dp")
        ),
        in_specs=[pl.BlockSpec(memory_space=pltpu.SMEM)] + [vmem] * (3 + len(pieces)),
        out_specs=[vmem] * 6,
        out_shape=[
            shape((tok_count, low_width), BF),
            shape((tok_count, latent_width), F32),
            shape((n_seq, tok_count, width // n_seq), BF),
            shape((1, width), F32),
            shape((1, width), F32),
            shape((1, latent_width), F32),
        ],
        scratch_shapes=[pltpu.VMEM((tok_count, low_width), F32)],
        compiler_params=pltpu.CompilerParams(vmem_limit_bytes=KERNEL_VMEM),
        cost_estimate=takes("first_projections"),
        name="first_projections",
    )(me, x, cosine, sine_part, *pieces)


def weights_in_order(raw_ref, gate_ref, up_ref):
    n_dp, n_seq, _, rows, _ = raw_ref.shape
    for s in range(n_seq):
        for z in range(n_dp):
            here = pl.ds((s * n_dp + z) * rows, rows)
            gate_ref[here, :] = raw_ref[z, s, 0]
            up_ref[here, :] = raw_ref[z, s, 1]


def feed_kernel(count, block, *refs):
    blocks, raw_ref = refs[:count], refs[count]
    x_ref, act_ref, silu_ref, slope_ref, gate_ref, up_ref = refs[count + 1 :]
    at = pl.program_id(0)

    @pl.when(at == 0)
    def _():
        for source, here in zip(blocks, piece_slices(blocks), strict=True):
            x_ref[here, :] = source[...]
        weights_in_order(raw_ref, gate_ref, up_ref)

    x = x_ref[pl.ds(pl.multiple_of(at * block, block), block), :]
    gate = matmul(x, gate_ref[...])
    upward = matmul(x, up_ref[...])
    sigmoid = 1.0 / (1.0 + jnp.exp(-gate))
    silu = gate * sigmoid
    act_ref[...] = (silu * upward).astype(BF)
    silu_ref[...] = silu.astype(BF)
    slope_ref[...] = (upward * (sigmoid + silu * (1.0 - sigmoid))).astype(BF)


def whole_spec(shape):
    return pl.BlockSpec(shape, lambda *_: (0,) * len(shape), pipeline_mode=pl.Buffered(1))


def feed_forward(blocks, raw, block):
    width = blocks[0].shape[1]
    group_len = sum(piece.shape[0] for piece in blocks)
    hidden = raw.shape[-1]
    units = pl.BlockSpec((block, hidden), lambda i: (i, 0))
    weight = jax.ShapeDtypeStruct((width, hidden), BF)
    return pl.pallas_call(
        functools.partial(feed_kernel, len(blocks), block),
        grid=(group_len // block,),
        in_specs=[whole_spec(piece.shape) for piece in blocks] + [whole_spec(raw.shape)],
        out_specs=[whole_spec((group_len, width))]
        + [units] * 3
        + [whole_spec((width, hidden))] * 2,
        out_shape=[jax.ShapeDtypeStruct((group_len, width), BF)]
        + [jax.ShapeDtypeStruct((group_len, hidden), BF)] * 3
        + [weight] * 2,
        compiler_params=pltpu.CompilerParams(vmem_limit_bytes=KERNEL_VMEM),
        cost_estimate=takes("feed_forward"),
        name="feed_forward",
    )(*blocks, raw)


def feed_back_kernel(
    d_ref, silu_ref, slope_ref, gate_ref, up_ref, down_ref, dg_ref, du_ref, even_ref, odd_ref
):
    d_active = dot_rows(d_ref[...], down_ref[...])
    d_gate = (d_active * slope_ref[...].astype(F32)).astype(BF)
    d_up = (d_active * silu_ref[...].astype(F32)).astype(BF)
    dg_ref[...] = d_gate
    du_ref[...] = d_up
    terms = (dot_rows(d_gate, gate_ref[...]) + dot_rows(d_up, up_ref[...])).astype(BF)
    half = terms.shape[0] // 2
    even_ref[...] = terms[:half]
    odd_ref[...] = terms[half:]


def feed_back(d, silu, slope, gate, up, down, block, first, count):
    width, hidden = gate.shape
    tokens = pl.BlockSpec((block, width), lambda i: (i + first, 0))
    units = pl.BlockSpec((block, hidden), lambda i: (i + first, 0))
    half = pl.BlockSpec((block // 2, width), lambda i: (i, 0))
    return pl.pallas_call(
        feed_back_kernel,
        grid=(count,),
        in_specs=[tokens, units, units]
        + [whole_spec(gate.shape), whole_spec(up.shape), whole_spec(down.shape)],
        out_specs=[pl.BlockSpec((block, hidden), lambda i: (i, 0))] * 2 + [half] * 2,
        out_shape=[jax.ShapeDtypeStruct((count * block, hidden), BF)] * 2
        + [jax.ShapeDtypeStruct((count * block // 2, width), BF)] * 2,
        compiler_params=pltpu.CompilerParams(vmem_limit_bytes=KERNEL_VMEM),
        cost_estimate=takes("feed_back"),
        name="feed_back",
    )(d, silu, slope, gate, up, down)


def gate_up_grad_kernel(x_ref, dg_low, du_low, dg_high, du_high, out_ref):
    n_dp, _, _, rows, _ = out_ref.shape
    middle = dg_low.shape[0]
    low, high = x_ref[:middle, :], x_ref[middle:, :]
    for which, (d_low, d_high) in enumerate(((dg_low, dg_high), (du_low, du_high))):
        terms = (dot_cols(low, d_low[...]) + dot_cols(high, d_high[...])).astype(BF)
        for z in range(n_dp):
            out_ref[z, 0, which] = terms[z * rows : (z + 1) * rows]


def gate_up_grad(x, low, high, n_dp, n_seq):
    group_len, width = x.shape
    hidden = low[0].shape[1]
    rows = width // (n_dp * n_seq)
    return pl.pallas_call(
        gate_up_grad_kernel,
        grid=(n_seq,),
        in_specs=[pl.BlockSpec((group_len, n_dp * rows), lambda i: (0, i))]
        + [whole_spec(part.shape) for part in (*low, *high)],
        out_specs=pl.BlockSpec((n_dp, 1, 2, rows, hidden), lambda i: (0, i, 0, 0, 0)),
        out_shape=jax.ShapeDtypeStruct((n_dp, n_seq, 2, rows, hidden), BF),
        compiler_params=pltpu.CompilerParams(vmem_limit_bytes=KERNEL_VMEM),
        cost_estimate=takes("gate_up_grad"),
        name="gate_up_grad",
    )(x, *low, *high)


def pair_product_kernel(left_ref, right_ref, even_ref, odd_ref):
    terms = matmul(left_ref[...], right_ref[...]).astype(BF)
    half = terms.shape[0] // 2
    even_ref[...] = terms[:half]
    odd_ref[...] = terms[half:]


def pair_product(left, right, block):
    rows, depth = left.shape
    width = right.shape[1]
    half = pl.BlockSpec((block // 2, width), lambda i: (i, 0))
    return pl.pallas_call(
        pair_product_kernel,
        grid=(rows // block,),
        in_specs=[pl.BlockSpec((block, depth), lambda i: (i, 0)), whole_spec(right.shape)],
        out_specs=[half] * 2,
        out_shape=[jax.ShapeDtypeStruct((rows // 2, width), BF)] * 2,
        compiler_params=pltpu.CompilerParams(vmem_limit_bytes=KERNEL_VMEM),
        cost_estimate=takes("pair_product"),
        name="pair_product",
    )(left, right)


GAIN_ROWS = 32


def last_kernel(
    count,
    n_seq,
    me_ref,
    back_ref,
    latent_ref,
    query_gain_ref,
    x_ref,
    gain_ref,
    cos_ref,
    sin_ref,
    feed_term_ref,
    *refs,
):
    blocks, (load_ref, dx_ref) = refs[:count], refs[count:]
    me = me_ref[0]
    latent_width = latent_ref.shape[1]
    tok_count, first_width = back_ref.shape
    width = x_ref.shape[1]
    size = width // n_seq

    def norm_back(v, e, gain):
        r = lax.rsqrt(jnp.mean(v * v, axis=1, keepdims=True) + EPS)
        u = v * r
        eg = e * gain
        grad = r * (eg - u * jnp.mean(eg * u, axis=1, keepdims=True))
        return grad, jnp.sum(e * u, axis=0, keepdims=True)

    d_latent, query_term = norm_back(
        latent_ref[...], back_ref[:, :latent_width], query_gain_ref[...]
    )
    half = HEAD_DIM // 2
    first_half = back_ref[:, latent_width : latent_width + half]
    second_half = back_ref[:, latent_width + half : latent_width + HEAD_DIM]
    cosine, sine_part = cos_ref[...], sin_ref[...]
    d_first = jnp.concatenate(
        [
            d_latent,
            first_half * cosine + second_half * sine_part,
            second_half * cosine - first_half * sine_part,
            back_ref[:, latent_width + HEAD_DIM :],
        ],
        axis=1,
    ).astype(BF)
    load_ref[:tok_count, :] = d_first
    for piece, here in zip(blocks, piece_slices(blocks), strict=True):
        rows = here.stop - here.start
        place = (me ^ (here.start // size)) * size + here.start % size
        own = pl.ds(pl.multiple_of(place, rows), rows)
        dx_ref[:, own] = dot_rows(d_first, piece[:, :first_width])
    dx_ref[...], gain_term = norm_back(x_ref[...].astype(F32), dx_ref[...], gain_ref[...])
    pad = jnp.zeros((1, 2 * first_width - width), F32)
    rows = [
        gain_term[:, :first_width],
        jnp.concatenate([gain_term[:, first_width:], pad], axis=1),
        feed_term_ref[:, :first_width],
        jnp.concatenate([feed_term_ref[:, first_width:], pad], axis=1),
        jnp.concatenate([query_term, jnp.zeros((1, first_width - latent_width), F32)], axis=1),
        jnp.zeros((GAIN_ROWS - 5, first_width), F32),
    ]
    load_ref[tok_count:, :] = jnp.concatenate(rows, axis=0).astype(BF)


def last_products(me, back, latent, query_gain, x, gain, cosine, sine_part, feed_term, blocks):
    tok_count, width = x.shape
    vmem = pl.BlockSpec(memory_space=pltpu.VMEM)
    return pl.pallas_call(
        functools.partial(last_kernel, len(blocks), lax.axis_size("seq")),
        in_specs=[pl.BlockSpec(memory_space=pltpu.SMEM)] + [vmem] * (8 + len(blocks)),
        out_specs=[vmem] * 2,
        out_shape=[
            jax.ShapeDtypeStruct((tok_count + GAIN_ROWS, back.shape[1]), BF),
            jax.ShapeDtypeStruct((tok_count, width), F32),
        ],
        compiler_params=pltpu.CompilerParams(vmem_limit_bytes=KERNEL_VMEM),
        cost_estimate=takes("last_products"),
        name="last_products",
    )(me, back, latent, query_gain, x, gain, cosine, sine_part, feed_term, *blocks)


def first_grads_kernel(count, n_seq, n_dp, latent_width, me_ref, normed_ref, *refs):
    pieces, (out_ref, d_ref, x_ref) = refs[:count], refs[count:]
    me = me_ref[0]
    tok_count, size = normed_ref.shape[1:]
    first_width = d_ref.shape[1]
    block = tok_count + GAIN_ROWS
    terms = jnp.zeros((8, first_width), F32)
    for piece, here in zip(pieces, piece_slices(pieces), strict=True):
        k, first = here.start // block, here.start % block
        tokens = min(tok_count - first, piece.shape[0])
        d_ref[k * tok_count + first : k * tok_count + first + tokens, :] = piece[:tokens, :]
        if tokens < piece.shape[0]:
            terms = terms + piece[tokens : tokens + 16, :].astype(F32)[:8]
    for k in range(n_seq):
        x_ref[k * tok_count : (k + 1) * tok_count, :] = normed_ref[me ^ k]
    out_ref[:, :first_width] = dot_cols(x_ref[...], d_ref[...]).astype(BF)
    width = size * n_seq
    rest = width - first_width

    def share(row, length):
        own = row[:, :length]
        for k in range(1, n_seq):
            own = jnp.where(me == k, row[:, k * length : (k + 1) * length], own)
        return own

    gain = jnp.concatenate([terms[0:1], terms[1:2, :rest]], axis=1)
    feed = jnp.concatenate([terms[2:3], terms[3:4, :rest]], axis=1)
    query = share(terms[4:5, :latent_width], latent_width // n_seq)
    query = matmul(
        jnp.concatenate([query] * 8, axis=0).astype(BF),
        spread(n_dp, query.shape[1] // n_dp, size // n_dp),
    )[:1]
    rows = [share(gain, size), share(feed, size), query, jnp.zeros((125, size), F32)]
    out_ref[:, first_width:] = jnp.concatenate(rows, axis=0).T.astype(BF)


def first_grads(me, normed, pieces, latent_width):
    n_seq, tok_count, size = normed.shape
    first_width = pieces[0].shape[1]
    vmem = pl.BlockSpec(memory_space=pltpu.VMEM)
    return pl.pallas_call(
        functools.partial(
            first_grads_kernel, len(pieces), n_seq, lax.axis_size("dp"), latent_width
        ),
        in_specs=[pl.BlockSpec(memory_space=pltpu.SMEM)] + [vmem] * (1 + len(pieces)),
        out_specs=vmem,
        out_shape=jax.ShapeDtypeStruct((size, first_width + 128), BF),
        scratch_shapes=[
            pltpu.VMEM((n_seq * tok_count, first_width), BF),
            pltpu.VMEM((n_seq * tok_count, size), BF),
        ],
        compiler_params=pltpu.CompilerParams(vmem_limit_bytes=KERNEL_VMEM),
        cost_estimate=takes("first_grads"),
        name="first_grads",
    )(me, normed, *pieces)


def block_places(shape, axis, core):
    rows = lax.broadcasted_iota(jnp.int32, shape, axis)
    half = shape[axis] // 2
    return rows + core * jnp.where(rows < half, half, -half)


def rotate_heads(values, cosine, sine_part, scale):
    half = HEAD_DIM // 2
    parts = []
    for at in range(0, values.shape[1], HEAD_DIM):
        first_half = values[:, at : at + half]
        second_half = values[:, at + half : at + HEAD_DIM]
        parts.append((first_half * cosine - second_half * sine_part) * scale)
        parts.append((second_half * cosine + first_half * sine_part) * scale)
    return jnp.concatenate(parts, axis=1)


def attend_kernel(
    count,
    heads,
    block,
    me_ref,
    starts_ref,
    cos_ref,
    sin_ref,
    wq_ref,
    wo_ref,
    *refs,
):
    packs = refs[:count]
    lat_ref, k_ref, v_ref, q_ref, mixed_ref, lse_ref, even_ref, odd_ref, vt_ref = refs[count:]
    me = me_ref[0]
    chip, core = me >> 1, me & 1
    index = pl.program_id(0)
    at = index ^ chip
    latent_width = lat_ref.shape[1]

    @pl.when(index == 0)
    def _():
        for pack, here in zip(packs, piece_slices(packs), strict=True):
            lat_ref[here, :] = pack[:, :latent_width]
            k_ref[here, :] = pack[:, latent_width : latent_width + HEAD_DIM]
            v_ref[here, :] = pack[:, latent_width + HEAD_DIM :]
        for j in range(k_ref.shape[0] // block):
            here = slice(j * block, (j + 1) * block)
            vt_ref[:, here] = v_ref[here, :].T

    own = pl.ds(pl.multiple_of(index * block, block), block)
    query_raw = matmul(lat_ref[own, :], wq_ref[...])
    q_ref[...] = rotate_heads(
        query_raw, cos_ref[...], sin_ref[...], HEAD_DIM ** (-0.5)
    ).astype(BF)
    starts_row = starts_ref[...]
    key_place = block_places((block, 1), 0, core)
    query_place = at * block + block_places((1, block), 1, core)
    columns = [slice(h * HEAD_DIM, (h + 1) * HEAD_DIM) for h in range(heads)]

    def step(b, running):
        here = pl.ds(pl.multiple_of((b ^ chip) * block, block), block)
        keys_here = b * block + key_place
        visible = (keys_here <= query_place) & (keys_here >= starts_row)
        result = []
        for head in range(heads):
            running_max, running_sum, total = running[head]
            scores = dot_rows(k_ref[here, :], q_ref[:, columns[head]])
            scores = jnp.where(visible, scores, NEGATIVE)
            new_max = jnp.maximum(running_max, jnp.max(scores, axis=0, keepdims=True))
            factor = jnp.exp(running_max - new_max)
            terms = jnp.where(visible, jnp.exp(scores - new_max), 0.0)
            running_sum = running_sum * factor + jnp.sum(terms, axis=0, keepdims=True)
            total = total * factor + matmul(vt_ref[:, here], terms.astype(BF))
            result.append((new_max, running_sum, total))
        return tuple(result)

    start = (
        jnp.full((1, block), NEGATIVE, F32),
        jnp.zeros((1, block), F32),
        jnp.zeros((HEAD_DIM, block), F32),
    )
    running = lax.fori_loop(0, at + 1, step, (start,) * heads)
    for head in range(heads):
        running_max, running_sum, total = running[head]
        mixed_ref[:, columns[head]] = (total / running_sum).T.astype(BF)
        lse_ref[head : head + 1, :] = running_max + jnp.log(running_sum)
    terms = matmul(mixed_ref[...], wo_ref[...]).astype(BF)
    even_ref[...] = terms[: block // 2]
    odd_ref[...] = terms[block // 2 :]


def attend(me, starts, cosine, sine_part, query_up, output, packs, latent_width, block):
    pack_width = packs[0].shape[1]
    group_len = sum(piece.shape[0] for piece in packs)
    width = query_up.shape[1]
    heads = width // HEAD_DIM
    out_width = output.shape[1]
    tokens = pl.BlockSpec((block, width), lambda i, me: (i, 0))
    half = pl.BlockSpec((block // 2, out_width), lambda i, me: (i, 0))
    angle = pl.BlockSpec((block, HEAD_DIM // 2), lambda i, me: (i, 0))
    lanes = pl.BlockSpec((heads, block), lambda i, me: (0, i))
    shape = jax.ShapeDtypeStruct
    return pl.pallas_call(
        functools.partial(attend_kernel, len(packs), heads, block),
        grid_spec=pltpu.PrefetchScalarGridSpec(
            num_scalar_prefetch=1,
            grid=(group_len // block,),
            in_specs=[
                pl.BlockSpec((1, block), lambda i, me: (0, i)),
                angle,
                angle,
                whole_spec(query_up.shape),
                whole_spec(output.shape),
            ]
            + [whole_spec(piece.shape) for piece in packs],
            out_specs=[
                whole_spec((group_len, latent_width)),
                whole_spec((group_len, HEAD_DIM)),
                whole_spec((group_len, HEAD_DIM)),
                tokens,
                tokens,
                lanes,
                half,
                half,
            ],
            scratch_shapes=[pltpu.VMEM((HEAD_DIM, group_len), BF)],
        ),
        out_shape=[
            shape((group_len, latent_width), BF),
            shape((group_len, HEAD_DIM), BF),
            shape((group_len, HEAD_DIM), BF),
            shape((group_len, width), BF),
            shape((group_len, width), BF),
            shape((heads, group_len), F32),
            shape((group_len // 2, out_width), BF),
            shape((group_len // 2, out_width), BF),
        ],
        compiler_params=pltpu.CompilerParams(vmem_limit_bytes=KERNEL_VMEM),
        cost_estimate=takes("attend"),
        name="attend",
    )(me, starts, cosine, sine_part, query_up, output, *packs)


def attend_back_kernel(
    count,
    heads,
    block,
    me_ref,
    starts_ref,
    cos_ref,
    sin_ref,
    q_ref,
    mixed_ref,
    lse_ref,
    k_ref,
    v_ref,
    wq_ref,
    wo_ref,
    *refs,
):
    blocks = refs[:count]
    d_ref, dq_ref, even_ref, odd_ref, dk_ref, dv_ref = refs[count:]
    me = me_ref[0]
    chip, core = me >> 1, me & 1
    index = pl.program_id(0)
    at = index ^ chip
    half = block // 2
    latent_width = wq_ref.shape[0]

    @pl.when(index == 0)
    def _():
        for source, here in zip(blocks, piece_slices(blocks), strict=True):
            d_ref[here, :] = source[...]
        dk_ref[...] = jnp.zeros_like(dk_ref)
        dv_ref[...] = jnp.zeros_like(dv_ref)

    own = pl.ds(pl.multiple_of(index * block, block), block)
    d_mixed = dot_rows(d_ref[own, :], wo_ref[...]).astype(BF)
    starts_row = starts_ref[...]
    key_place = block_places((block, 1), 0, core)
    query_place = at * block + block_places((1, block), 1, core)
    columns = [slice(h * HEAD_DIM, (h + 1) * HEAD_DIM) for h in range(heads)]
    offsets = [
        jnp.sum(
            (d_mixed[:, cols].astype(F32) * mixed_ref[:, cols].astype(F32)).T,
            axis=0,
            keepdims=True,
        )
        for cols in columns
    ]

    def step(b, running):
        here = pl.ds(pl.multiple_of((b ^ chip) * block, block), block)
        keys_here = b * block + key_place
        visible = (keys_here <= query_place) & (keys_here >= starts_row)
        keys, values = k_ref[here, :], v_ref[here, :]
        result = []
        for head in range(heads):
            q, dm = q_ref[:, columns[head]], d_mixed[:, columns[head]]
            scores = dot_rows(keys, q)
            scores = jnp.where(visible, scores, NEGATIVE)
            probs = jnp.where(visible, jnp.exp(scores - lse_ref[head : head + 1, :]), 0.0)
            d_probs = dot_rows(values, dm)
            d_scores = (probs * (d_probs - offsets[head])).astype(BF)
            dv_ref[here, :] += matmul(probs.astype(BF), dm)
            dk_ref[here, :] += matmul(d_scores, q)
            result.append(running[head] + dot_cols(d_scores, keys))
        return tuple(result)

    start = (jnp.zeros((block, HEAD_DIM), F32),) * heads
    d_queries = jnp.concatenate(lax.fori_loop(0, at + 1, step, start), axis=1)
    dq_ref[...] = rotate_heads(
        d_queries, cos_ref[...], -sin_ref[...], HEAD_DIM ** (-0.5)
    ).astype(BF)
    terms = dot_rows(dq_ref[...], wq_ref[...]).astype(BF)
    rows_here = pl.ds(pl.multiple_of(index * half, half), half)
    even_ref[rows_here, :latent_width] = terms[:half]
    odd_ref[rows_here, :latent_width] = terms[half:]

    @pl.when(index == pl.num_programs(0) - 1)
    def _():
        for j in range(k_ref.shape[0] // block):
            to = slice(j * half, (j + 1) * half)
            for target, first in ((even_ref, j * block), (odd_ref, j * block + half)):
                rows = slice(first, first + half)
                target[to, latent_width : latent_width + HEAD_DIM] = dk_ref[rows, :].astype(BF)
                target[to, latent_width + HEAD_DIM :] = dv_ref[rows, :].astype(BF)


def attend_back(
    me, starts, cosine, sine_part, queries, mixed, lse, keys, values, query_up, output, blocks, block
):
    group_len, width = queries.shape
    heads = width // HEAD_DIM
    out_width = blocks[0].shape[1]
    latent_width = query_up.shape[0]
    pack_width = latent_width + 2 * HEAD_DIM
    tokens = pl.BlockSpec((block, width), lambda i, me: (i, 0))
    angle = pl.BlockSpec((block, HEAD_DIM // 2), lambda i, me: (i, 0))
    lanes = pl.BlockSpec((heads, block), lambda i, me: (0, i))
    half = (group_len // 2, pack_width)
    shape = jax.ShapeDtypeStruct
    return pl.pallas_call(
        functools.partial(attend_back_kernel, len(blocks), heads, block),
        grid_spec=pltpu.PrefetchScalarGridSpec(
            num_scalar_prefetch=1,
            grid=(group_len // block,),
            in_specs=[
                pl.BlockSpec((1, block), lambda i, me: (0, i)),
                angle,
                angle,
                tokens,
                tokens,
                lanes,
                whole_spec(keys.shape),
                whole_spec(values.shape),
                whole_spec(query_up.shape),
                whole_spec(output.shape),
            ]
            + [whole_spec(piece.shape) for piece in blocks],
            out_specs=[
                whole_spec((group_len, out_width)),
                tokens,
                whole_spec(half),
                whole_spec(half),
            ],
            scratch_shapes=[pltpu.VMEM((group_len, HEAD_DIM), F32)] * 2,
        ),
        out_shape=[
            shape((group_len, out_width), BF),
            shape((group_len, width), BF),
            shape(half, BF),
            shape(half, BF),
        ],
        compiler_params=pltpu.CompilerParams(vmem_limit_bytes=KERNEL_VMEM),
        cost_estimate=takes("attend_back"),
        name="attend_back",
    )(
        me,
        starts,
        cosine,
        sine_part,
        queries,
        mixed,
        lse,
        keys,
        values,
        query_up,
        output,
        *blocks,
    )


def attention_grads_kernel(n_dp, query_rows, mixed_ref, latent_ref, dq_ref, d_ref, out_ref):
    out_rows = mixed_ref.shape[1] // n_dp
    output_terms = dot_cols(mixed_ref[...], d_ref[...]).astype(BF)
    query_terms = dot_cols(latent_ref[...], dq_ref[...])
    for z in range(n_dp):
        out_ref[z, :out_rows, :] = output_terms[z * out_rows : (z + 1) * out_rows]
        parts = [
            query_terms[first : first + query_rows]
            for first in range(z * query_rows, query_terms.shape[0], n_dp * query_rows)
        ]
        out_ref[z, out_rows:, :] = jnp.concatenate(parts, axis=0).astype(BF)


def attention_grads(mixed, latent, d_query, d_branch, n_dp, query_rows):
    group_len, width = d_branch.shape
    heads_width = mixed.shape[1]
    sets = width // heads_width
    part = latent.shape[1] // sets
    rows = heads_width // n_dp + part // n_dp
    return pl.pallas_call(
        functools.partial(attention_grads_kernel, n_dp, query_rows),
        grid=(sets,),
        in_specs=[
            whole_spec(mixed.shape),
            pl.BlockSpec((group_len, part), lambda j: (0, j)),
            whole_spec(d_query.shape),
            pl.BlockSpec((group_len, heads_width), lambda j: (0, j)),
        ],
        out_specs=pl.BlockSpec((n_dp, rows, heads_width), lambda j: (0, 0, j)),
        out_shape=jax.ShapeDtypeStruct((n_dp, rows, width), BF),
        compiler_params=pltpu.CompilerParams(vmem_limit_bytes=KERNEL_VMEM),
        cost_estimate=takes("attention_grads"),
        name="attention_grads",
    )(mixed, latent, d_query, d_branch)


def columns_back_kernel(parts_ref, *targets):
    for which, target in enumerate(targets):
        parts = [parts_ref[k, which].astype(F32) for k in range(parts_ref.shape[0])]
        target[...] = jnp.concatenate(parts, axis=1)


def columns_back(parts):
    n_seq, kinds, rows, columns = parts.shape
    vmem = pl.BlockSpec(memory_space=pltpu.VMEM)
    return pl.pallas_call(
        columns_back_kernel,
        in_specs=[vmem],
        out_specs=[vmem] * kinds,
        out_shape=[jax.ShapeDtypeStruct((rows, n_seq * columns), F32)] * kinds,
        compiler_params=pltpu.CompilerParams(vmem_limit_bytes=KERNEL_VMEM),
        cost_estimate=takes("columns_back"),
        name="columns_back",
    )(parts)


def local(
    layer_input,
    doc_lengths,
    attention_gain,
    query_down,
    query_gain,
    query_up,
    keyvalue_weight,
    output_weight,
    feedforward_gain,
    gate_weight,
    up_weight,
    down_weight,
    cotangent,
):
    n_seq, n_dp = lax.axis_size("seq"), lax.axis_size("dp")
    me = lax.axis_index("seq")
    input_low = layer_input[0]
    tokens = input_low.astype(F32)
    tok_count, width = tokens.shape
    latent_width = query_down.shape[1]
    group_len = tok_count * n_seq
    heads = HEADS // n_seq
    hidden_units = gate_weight.shape[1] // n_seq

    starts_all, position_all = document_starts(doc_lengths[0], group_len)
    starts_all = relative(starts_all, 0)
    position_all = relative(position_all, 0)
    cosine_all, sine_all = rope_tables(position_all, HEAD_DIM)
    me_array = me.astype(jnp.int32).reshape(1)

    own_rows = query_down.shape[0]
    query_rows = query_gain.shape[0]
    gains = jnp.stack(
        [attention_gain, feedforward_gain, jnp.pad(query_gain, (0, own_rows - query_rows))], axis=1
    )
    first_set = jnp.concatenate(
        [query_down, keyvalue_weight, jnp.pad(gains, ((0, 0), (0, 125)))], axis=1
    )
    chain = Chain()
    block = 2 * tok_count
    half_chips = n_seq // 4
    first_width = latent_width + 2 * HEAD_DIM
    out_rows = output_weight.shape[0]

    chain.add(tables=(cosine_all, sine_all, starts_all.reshape(1, group_len)))
    first_set, query_up = together(first_set, query_up)
    chain.add(query_part=exchange(split_columns(query_up)))
    chain.add(feed_step=gather_near(cotangent[0]))
    first_part = chain.stage(FIRST_PART, gather_dp_steps(first_set))
    query_part = chain.query_part.reshape(-1, query_up.shape[1] // n_seq)
    fold = query_part.shape[0] * query_part.shape[1] // width
    attention_set = jnp.concatenate([output_weight, query_part.reshape(fold, width)], axis=0)
    chain.add(attention=gather_dp(chain.begin(attention=attention_set)))
    chain.add(gate_up_parts=jnp.stack([split_columns(gate_weight), split_columns(up_weight)], axis=1),
    )
    near = chain.stage(FIRST_NEAR, gather_near(first_part))
    far = chain.stage(FIRST_FAR, gather_far(near))
    chain.add(gate_up=exchange(chain.begin(gate_up=chain.gate_up_parts)))
    first_blocks = chain.stage(FIRST_BLOCKS, gather_cores(far))
    cosine_all, sine_all, starts_all = chain.tables
    cosine, sine_part = cosine_all[:tok_count], sine_all[:tok_count]
    pack, latent, normed_parts, attention_gain_row, feed_gain_row, query_gain_row = first_projections(
        me_array, input_low, cosine, sine_part, first_blocks, latent_width
    )
    feed_gain_f = feed_gain_row[0]
    pack = chain.stage(PACK, pack)
    attention_part = chain.attention.reshape(n_dp, -1, width)
    full_output = attention_part[:, :out_rows].reshape(-1, width)
    full_query_up = rows_in_order(
        attention_part[:, out_rows:].reshape(-1, query_part.shape[1]), query_up.shape[0]
    )
    chain.add(attention_weights=(full_output, full_query_up))
    near = chain.stage(PACK_NEAR, gather_near(pack))
    gate_up = chain.gate_up
    chain.add(gate_up_all=gather_dp(gate_up.reshape(-1, hidden_units)).reshape(n_dp, *gate_up.shape),
    )
    chain.add(down_all=gather_dp(down_weight))
    packs = chain.stage(PACKS, gather_cores(gather_far(near)))
    full_output, full_query_up = chain.attention_weights
    chain.add(feed_far=gather_far(chain.begin(feed_far=chain.feed_step)))
    latent_all, keys, values, queries, mixed_low, lse, out_even, out_odd = attend(
        me_array,
        starts_all,
        cosine_all,
        sine_all,
        full_query_up,
        full_output,
        packs,
        latent_width,
        block,
    )
    out_even, out_odd = chain.stage(ATTENDED, (out_even, out_odd))
    feed_pieces = gather_cores(chain.feed_far)
    out_left = chain.stage(OUT_LEFT, scatter_relay(chip_sums(out_even, out_odd, n_seq // 2))
    )
    hidden = chain.stage(HIDDEN, tokens + scatter_last(out_left))

    chain.add(feed_stack=stack_blocks(chain.begin(feed_stack=feed_pieces)))
    feed_low = rms_norm(hidden, feed_gain_f).astype(BF)
    near = chain.stage(FEED_NEAR, gather_near(feed_low))
    feed_blocks = chain.stage(FEED_BLOCKS, gather_cores(gather_far(near)))
    chain.add(normed_columns=exchange(chain.begin(normed_columns=normed_parts)))
    feed, active_low, silu_low, slope_low, gate_ordered, up_ordered = feed_forward(
        feed_blocks, chain.gate_up_all, block
    )
    chain.add(grad_down_term=dot_cols(active_low, chain.feed_stack).astype(BF))
    silu_low = chain.stage(ACTIVE, silu_low)
    d_feed = chain.feed_stack
    chain.add(grad_down=scatter_dp(chain.grad_down_term))
    weights = (gate_ordered, up_ordered, chain.down_all)
    dg_high, du_high, even_high, odd_high = feed_back(
        d_feed, silu_low, slope_low, *weights, block, half_chips, half_chips
    )
    even_high, odd_high = chain.stage(TERMS_HIGH, (even_high, odd_high))
    chain.add(high_swap=flip(odd_high, 1))
    dg_low, du_low, *terms_low = feed_back(
        d_feed, after(silu_low, odd_high), slope_low, *weights, block, 0, half_chips
    )
    terms_low = chain.stage(TERMS_LOW, terms_low)
    feed_sums = chip_sums(*terms_low, half_chips) + split_chips(
        plus(even_high, chain.high_swap), half_chips
    )
    feed_sums = chain.stage(FEED_SUMS, feed_sums)
    feed_left = chain.stage(FEED_LEFT, scatter_relay(feed_sums))
    grad_gate_up_term = gate_up_grad(
        chain.begin(grad_gate_up_term=feed), (dg_low, du_low), (dg_high, du_high), n_dp, n_seq
    )
    chain.add(grad_gate_up_term=grad_gate_up_term)
    chain.add(grad_gate_up=scatter_dp(grad_gate_up_term.reshape(-1, hidden_units)))
    d_feed_normed = chain.stage(D_NORMED, scatter_last(feed_left))

    d_result = cotangent[0].astype(F32)
    d_hidden_norm, grad_feed_gain_term = jax.vjp(rms_norm, hidden, feed_gain_f)[1](d_feed_normed)
    d_hidden = d_result + d_hidden_norm
    chain.add(result_terms=pair_product(chain.begin(result_terms=active_low), chain.down_all, block),
    )
    near = chain.stage(BRANCH_NEAR, gather_near(d_hidden.astype(BF)))
    chain.add(result_sums=chip_sums(*chain.result_terms, n_seq // 2))
    d_branch_blocks = gather_cores(gather_far(near))
    d_branch_blocks, feed_gain_term = chain.stage(BRANCH_BLOCKS, (d_branch_blocks, grad_feed_gain_term.reshape(1, -1))
    )
    chain.add(result_left=scatter_relay(chain.begin(result_left=chain.result_sums)))
    chain.add(result_hops=early_hops(chain.result_left))
    d_branch, d_query_low, back_even, back_odd = attend_back(
        me_array,
        starts_all,
        cosine_all,
        sine_all,
        queries,
        mixed_low,
        lse,
        keys,
        values,
        full_query_up,
        full_output,
        d_branch_blocks,
        block,
    )
    back_even, back_odd = chain.stage(BACK_TERMS, (back_even, back_odd))
    back_sums = chain.stage(BACK_SUMS, chip_sums(back_even, back_odd, n_seq // 2))
    d_branch, latent_all = chain.begin(grad_attention_term=(d_branch, latent_all))
    chain.add(grad_attention_term=attention_grads(mixed_low, latent_all, d_query_low, d_branch, n_dp, query_rows),
    )
    back_left = chain.stage(BACK_LEFT, scatter_relay(back_sums))
    back_local = chain.stage(BACK_LOCAL, scatter_last(back_left))
    chain.add(grad_attention=scatter_dp(chain.grad_attention_term.reshape(-1, width)))
    chain.add(result_late=late_hops(chain.begin(result_last=chain.result_left)))
    load, d_tokens = last_products(
        me_array,
        back_local,
        latent,
        query_gain_row,
        input_low,
        attention_gain_row,
        cosine,
        sine_part,
        feed_gain_term,
        first_blocks,
    )
    load = chain.stage(FIRST_TERMS, load)
    result_left = chain.result_left
    hops = chain.result_hops + chain.result_late
    result = hidden + hops_sum(result_left, hops)
    layer_output = result.astype(BF)[None]
    chain.add(layer_output=layer_output)
    input_grad = (d_hidden + d_tokens)[None]
    chain.add(input_grad=input_grad)
    near = chain.stage(LAST_NEAR, gather_near(load))
    loads = chain.stage(LAST_BLOCKS, gather_cores(gather_far(near)))
    first_sum = chain.stage(FIRST_SUM, first_grads(me_array, chain.normed_columns, loads, latent_width)
    )
    gate_up_rows = chain.begin(gate_up_rows=chain.grad_gate_up)
    gate_up_rows = exchange(gate_up_rows.reshape(n_seq, 2, own_rows, -1))
    grad_first = scatter_dp(first_sum).astype(F32)

    grad_down = chain.grad_down
    grad_attention = chain.grad_attention
    grad_output_weight = grad_attention[:out_rows].astype(F32)
    grad_query_up = grad_attention[out_rows:].reshape(fold, -1, heads * HEAD_DIM)
    grad_query_up = grad_query_up.transpose(1, 0, 2).reshape(n_seq, query_rows, -1)
    grad_query_up = exchange(grad_query_up)
    grad_query_up = grad_query_up.transpose(1, 0, 2).reshape(query_rows, -1).astype(F32)

    grad_gate, grad_up = columns_back(gate_up_rows)
    return (
        layer_output,
        input_grad,
        grad_first[:, first_width],
        grad_first[:, :latent_width],
        grad_first[:query_rows, first_width + 2],
        grad_query_up,
        grad_first[:, latent_width:first_width],
        grad_output_weight,
        grad_first[:, first_width + 1],
        grad_gate,
        grad_up,
        grad_down.astype(F32),
    )


def solution(mesh):
    shards = P(("seq", "dp"))
    tokens = P("dp", "seq", None)
    weight = P(("seq", "dp"), None)
    return jax.shard_map(
        local,
        mesh=mesh,
        in_specs=(
            tokens,
            P("dp", None),
            shards,
            weight,
            shards,
            weight,
            weight,
            weight,
            shards,
            weight,
            weight,
            weight,
            tokens,
        ),
        out_specs=(
            tokens,
            tokens,
            shards,
            weight,
            shards,
            weight,
            weight,
            weight,
            shards,
            weight,
            weight,
            weight,
        ),
        check_vma=False,
    )
```
